128 devices in a mesh: clip: 8 (over z, x_hi), seq: 16 (over y, x_lo, core).
Axes of the slice: x: 4 (x_hi: 2, x_lo: 2; x = x_hi * 2 + x_lo), y: 4, z: 4, core: 2. Of those that a mesh axis runs over, the one named last changes fastest.
Arguments:
- x_saved: float32 [8, 16, 256, 1152], P('clip', 'seq'), may hold values from -20 to 20, as said below
- grad_out: float32 [8, 16, 256, 1152], P('clip', 'seq'), may hold values from -6 to 6
- keep_mask: int32 [8, 16, 256], P('clip', 'seq'), may hold values 0 or 1
- w_qkv: float32 [1152, 3456], replicated, may hold values from -0.1620453 to 0.1620453, as said below
- w_out: float32 [1152, 1152], replicated, may hold values from -0.1875 to 0.1875
Outputs:
- grad_input: float32 [8, 16, 256, 1152], P('clip', 'seq')
- grad_w_qkv: float32 [1152, 3456], P('clip', 'seq')
- grad_w_out: float32 [1152, 1152], P('clip', 'seq')
The draws below stay inside these ranges and needn't reach their ends.
Inputs may be any that keep to these rules, and one draw needn't show every extreme that they name: `x_saved`: saved activations. `w_qkv`: projection entries of order 1152 ** -0.5.
All inputs are finite; a program needn't handle non-finite values. No bound on the sum of `keep_mask` on one device may be relied on, other than what follows from the above.
Results may differ from the reference program's by a relative error of at most 0.0003.
Values sent between devices are 32-bit elements; how exact they have to be, the bound alone decides.
A program may use at most 192 MiB of HBM per device.

```python
import jax
import jax.numpy as jnp
from jax import lax

HEADS = 16
HEAD_DIM = 72
D = 1152
PATCHES = 256
FRAMES = 16
CLIPS = 8


def draw_x_saved(key, part):
    key = jax.random.fold_in(key, 1)
    full_shape = (CLIPS, FRAMES, PATCHES, D)
    return jnp.clip(jax.random.normal(key, full_shape, jnp.float32), -6.0, 6.0)


def draw_w_qkv(key, part):
    key = jax.random.fold_in(key, 2)
    background = jnp.clip(jax.random.normal(key, (D, 3, D), jnp.float32), -4.0, 4.0) * D ** (-0.5)
    queries = background[:, 0]
    key_mix = 0.5 * background[:, 0] + 0.87 * background[:, 1]
    values = background[:, 2]
    return jnp.concatenate([queries, key_mix, values], axis=1)


def set_ends(array, key, low, high):
    spot = [jax.random.randint(jax.random.fold_in(key, axis), (), 0, length) for axis, length in enumerate(array.shape)]
    longest = array.shape.index(max(array.shape))
    next_to = spot[:longest] + [(spot[longest] + 1) % array.shape[longest]] + spot[longest + 1:]
    return array.at[tuple(spot)].set(low).at[tuple(next_to)].set(high)


def strengthened(values, own_key, source, target, parts, factor):
    owner, partner = [(jnp.arange(values.shape[dim]) // (values.shape[dim] // parts)).reshape([-1 if axis == dim else 1 for axis in range(values.ndim)]) for dim in (source, target)]
    chosen = jax.random.permutation(own_key, parts)[partner]
    strong = (owner == chosen) | (owner == (partner + parts // 2) % parts)
    return jnp.where(strong, factor * values, values)


def shard_levels(key, shape, cuts, smallest, top_value):
    gain = 1.0
    for dim, parts in cuts:
        steps = jax.random.uniform(jax.random.fold_in(jax.random.fold_in(key, 6), dim), (parts,), jnp.float32, smallest / len(cuts), top_value / len(cuts))
        gain = gain * jnp.repeat(jnp.exp(steps), shape[dim] // parts).reshape((-1,) + (1,) * (len(shape) - 1 - dim))
    return gain


def bell_draw(stream_key, shape, deviation, reach, shards=(), held_as=jnp.bfloat16):
    array = deviation * jax.random.normal(stream_key, shape, jnp.float32)
    if shards:
        array = array * shard_levels(stream_key, shape, shards, -0.22, 0.18)
    return jnp.clip(array, -reach, reach).astype(held_as)


def heavy_noise(own_key, extent, scale, reach, cuts, heavy, kind=jnp.bfloat16):
    values = scale * jax.random.normal(own_key, extent, jnp.float32)
    if cuts:
        values = values * shard_levels(own_key, extent, cuts, -0.22, 0.18)
    return jnp.clip(strengthened(values, jax.random.fold_in(own_key, 3), *heavy), -reach, reach).astype(kind)


def setup_inputs(seed: int = 0) -> dict:
    streams_of = jax.random.split(jax.random.key(seed), 6)
    return {
        "x_saved": draw_x_saved(jax.random.fold_in(streams_of[5], 71), 0),
        "grad_out": heavy_noise(streams_of[1], (CLIPS, FRAMES, PATCHES, D), 1.0, 6.0, ((0, 8), (1, 16)), (1, 3, 16, 2.0), jnp.float32),
        "keep_mask": set_ends((jax.random.randint(streams_of[2], (CLIPS, FRAMES, PATCHES), 0, 10) < 9).astype(jnp.int32), jax.random.fold_in(streams_of[2], 1), 0, 1),
        "w_qkv": draw_w_qkv(jax.random.fold_in(streams_of[5], 71), 0),
        "w_out": bell_draw(streams_of[4], (D, D), D ** -0.5, 0.1875, (), jnp.float32),
    }


KEEP_RATE = 0.9


def clip_grads(x_clip, grad_clip, mask_clip, w_qkv, w_out):
    high = lax.Precision.HIGHEST
    frames = x_clip.shape[0]
    patches = x_clip.shape[1]
    width = HEADS * HEAD_DIM
    scaling = HEAD_DIM ** -0.5
    tokens = x_clip.reshape(frames * patches, width)
    qkv = jnp.dot(tokens, w_qkv, precision=high, preferred_element_type=jnp.float32)
    split = qkv.reshape(frames, patches, 3, HEADS, HEAD_DIM)
    queries = split[:, :, 0]
    key_rows = split[:, :, 1]
    value_rows = split[:, :, 2]
    scores = jnp.einsum("fphd,gphd->phfg", queries, key_rows, precision=high) * scaling
    shifted = scores - jnp.max(scores, axis=-1, keepdims=True)
    expo = jnp.exp(shifted)
    attn = expo / jnp.sum(expo, axis=-1, keepdims=True)
    mixed = jnp.einsum("phfg,gphd->fphd", attn, value_rows, precision=high).reshape(frames * patches, width)
    grad_proj = grad_clip.reshape(frames * patches, width) * (mask_clip.reshape(frames * patches, 1).astype(jnp.float32) / KEEP_RATE)
    term_out = jnp.dot(mixed.T, grad_proj, precision=high, preferred_element_type=jnp.float32)
    grad_mixed = jnp.dot(grad_proj, w_out.T, precision=high, preferred_element_type=jnp.float32)
    grad_mixed = grad_mixed.reshape(frames, patches, HEADS, HEAD_DIM)
    grad_values = jnp.einsum("phfg,fphd->gphd", attn, grad_mixed, precision=high)
    grad_attn = jnp.einsum("fphd,gphd->phfg", grad_mixed, value_rows, precision=high)
    grad_scores = attn * (grad_attn - jnp.sum(grad_attn * attn, axis=-1, keepdims=True))
    grad_queries = jnp.einsum("phfg,gphd->fphd", grad_scores, key_rows, precision=high) * scaling
    grad_keys = jnp.einsum("phfg,fphd->gphd", grad_scores, queries, precision=high) * scaling
    grad_qkv = jnp.stack([grad_queries, grad_keys, grad_values], axis=2).reshape(frames * patches, 3 * width)
    term_qkv = jnp.dot(tokens.T, grad_qkv, precision=high, preferred_element_type=jnp.float32)
    grad_input = jnp.dot(grad_qkv, w_qkv.T, precision=high, preferred_element_type=jnp.float32)
    return grad_input.reshape(frames, patches, width), term_qkv, term_out


def reference(x_saved, grad_out, keep_mask, w_qkv, w_out):
    width = HEADS * HEAD_DIM

    def step(carry, item):
        x_clip, grad_clip, mask_clip = item
        grad_input, term_qkv, term_out = clip_grads(x_clip, grad_clip, mask_clip, w_qkv, w_out)
        return (carry[0] + term_qkv, carry[1] + term_out), grad_input

    start = (jnp.zeros((width, 3 * width), jnp.float32), jnp.zeros((width, width), jnp.float32))
    totals, grad_input = lax.scan(step, start, (x_saved, grad_out, keep_mask))
    return grad_input, totals[0], totals[1]
```

```python
import jax
import jax.numpy as jnp
from jax import lax
from jax.sharding import PartitionSpec as P

HEADS = 16
HEAD_DIM = 72
KEEP_RATE = 0.9
HIGH = lax.Precision.HIGH


def project(left, right):
    return jnp.dot(left, right, precision=HIGH, preferred_element_type=jnp.float32)


def project_back(left, right):
    return lax.dot_general(
        left, right, (((1,), (1,)), ((), ())), precision=HIGH, preferred_element_type=jnp.float32
    )


def outer_sum(left, right):
    return lax.dot_general(
        left, right, (((0,), (0,)), ((), ())), precision=HIGH, preferred_element_type=jnp.float32
    )


def on_device(x_saved, grad_out, keep_mask, w_qkv, w_out):
    frames = lax.axis_size("seq")
    width = x_saved.shape[-1]
    patches = x_saved.shape[2] // frames
    scaling = HEAD_DIM ** (-0.5)
    grad_proj = grad_out * (keep_mask.astype(jnp.float32)[..., None] / KEEP_RATE)
    x_p = lax.all_to_all(x_saved, "seq", split_axis=2, concat_axis=1, tiled=True)
    g_p = lax.all_to_all(grad_proj, "seq", split_axis=2, concat_axis=1, tiled=True)
    x_t = x_p.reshape(-1, width)
    g_t = g_p.reshape(-1, width)
    qkv = project(x_t, w_qkv)
    split = qkv.reshape(frames, patches, 3, HEADS, HEAD_DIM)
    q, k, v = split[:, :, 0], split[:, :, 1], split[:, :, 2]
    scores = jnp.einsum("fphd,gphd->phfg", q, k, precision=HIGH) * scaling
    shifted = scores - jnp.max(scores, axis=-1, keepdims=True)
    expo = jnp.exp(shifted)
    attn = expo / jnp.sum(expo, axis=-1, keepdims=True)
    mixed = jnp.einsum("phfg,gphd->fphd", attn, v, precision=HIGH).reshape(-1, width)
    term_out = outer_sum(mixed, g_t)
    gm = project_back(g_t, w_out).reshape(frames, patches, HEADS, HEAD_DIM)
    gv = jnp.einsum("phfg,fphd->gphd", attn, gm, precision=HIGH)
    ga = jnp.einsum("fphd,gphd->phfg", gm, v, precision=HIGH)
    gs = attn * (ga - jnp.sum(ga * attn, axis=-1, keepdims=True))
    gq = jnp.einsum("phfg,gphd->fphd", gs, k, precision=HIGH) * scaling
    gk = jnp.einsum("phfg,fphd->gphd", gs, q, precision=HIGH) * scaling
    gqkv = jnp.stack([gq, gk, gv], axis=2).reshape(-1, 3 * width)
    term_qkv = outer_sum(x_t, gqkv)
    gi = project_back(gqkv, w_qkv).reshape(1, frames, patches, width)
    grad_input = lax.all_to_all(gi, "seq", split_axis=1, concat_axis=2, tiled=True)
    total_out = lax.psum_scatter(
        lax.psum_scatter(term_out, "seq", scatter_dimension=1, tiled=True), "clip", scatter_dimension=0, tiled=True
    )
    total_qkv = lax.psum_scatter(
        lax.psum_scatter(term_qkv, "seq", scatter_dimension=1, tiled=True), "clip", scatter_dimension=0, tiled=True
    )
    return (grad_input, total_qkv, total_out)


def solution(mesh):
    return jax.shard_map(
        on_device,
        mesh=mesh,
        in_specs=(
            P("clip", "seq", None, None),
            P("clip", "seq", None, None),
            P("clip", "seq", None),
            P(),
            P(),
        ),
        out_specs=(P("clip", "seq", None, None), P("clip", "seq"), P("clip", "seq")),
        check_vma=False,
    )
```

```python
import jax
import jax.numpy as jnp
from jax import lax
from jax.experimental import pallas as pl
from jax.experimental.pallas import tpu as pltpu
from jax.sharding import PartitionSpec as P

HEADS = 16
HEAD_DIM = 72
KEEP_RATE = 0.9
D = 1152
LOCAL = 8
PART = 640
ROWS = 120
MESH = pl.DeviceIdType.MESH
F32 = jnp.float32
BF16 = jnp.bfloat16

NN = (((1,), (0,)), ((), ()))
NT = (((1,), (1,)), ((), ()))


def split(value):
    high = value.astype(BF16)
    return high, (value - high.astype(F32)).astype(BF16)


def dot(left, right, dims):
    return lax.dot_general(left, right, dims, preferred_element_type=F32)


def dot3(left_high, left_low, right_high, right_low, dims):
    return (
        dot(left_high, right_high, dims)
        + dot(left_low, right_high, dims)
        + dot(left_high, right_low, dims)
    )


def iota(shape, dim):
    return lax.broadcasted_iota(jnp.int32, shape, dim)


def wait_copy(ref, sem):
    pltpu.make_async_copy(ref, ref, sem).wait()


def compute_kernel(
    x_hbm, g_hbm, mask_ref, wqkv_hbm, wout_hbm, gw_hbm, gi_hbm,
    xl, gl, gsrc, wst, sel, wph, wpl, woh, wol, xth, xtl, qkv, gqkv, gm, mixed, mth, mtl,
    gph, gpl, big_h, big_l, gqh, gql, outw, gwbuf, gibuf,
    xs_sem, xr_sem, xfs_sem, xfr_sem, gs_sem, gr_sem, gfs_sem, gfr_sem, loc_sem, w_sem, gw_sem,
):
    clip = lax.axis_index("clip")
    seq = lax.axis_index("seq")
    chip = seq // 2
    core = seq % 2
    sibling = (clip, 2 * chip + 1 - core)

    def peer(d):
        return (clip, 2 * ((chip + d) % 8) + core)

    def frame_from(d, c):
        return 2 * ((chip + 8 - d) % 8) + c

    barrier = pltpu.get_barrier_semaphore()
    for d in range(1, 8):
        pl.semaphore_signal(barrier, inc=1, device_id=peer(d), device_id_type=MESH)
    pl.semaphore_signal(barrier, inc=1, device_id=sibling, device_id_type=MESH)

    own_frame = 2 * chip + core
    load_x = pltpu.make_async_copy(x_hbm.at[chip], xl.at[:, own_frame], loc_sem.at[0])
    load_x.start()
    load_g = pltpu.make_async_copy(g_hbm, gsrc, loc_sem.at[1])
    load_g.start()

    def weight_copy(step, slot):
        return pltpu.make_async_copy(
            wqkv_hbm.at[pl.ds(step * 144, 144)], wst.at[slot], w_sem.at[slot]
        )

    weight_copy(0, 0).start()
    pl.semaphore_wait(barrier, 8)

    def send(src, dst, send_sems, recv_sems, d):
        p = (chip + d) % 8
        return pltpu.make_async_remote_copy(
            src_ref=src.at[p],
            dst_ref=dst.at[:, own_frame],
            send_sem=send_sems.at[d],
            recv_sem=recv_sems.at[d],
            device_id=peer(d),
            device_id_type=MESH,
        )

    def arrival(dst, send_sems, recv_sems, d):
        view = dst.at[:, frame_from(d, core)]
        return pltpu.make_async_remote_copy(
            src_ref=view, dst_ref=view, send_sem=send_sems.at[d], recv_sem=recv_sems.at[d],
            device_id=peer(d), device_id_type=MESH,
        )

    def forward(dst, send_sems, recv_sems, d):
        view = dst.at[:, frame_from(d, core)]
        return pltpu.make_async_remote_copy(
            src_ref=view, dst_ref=view, send_sem=send_sems.at[d], recv_sem=recv_sems.at[d],
            device_id=sibling, device_id_type=MESH,
        )

    def forwarded(dst, send_sems, recv_sems, d):
        view = dst.at[:, frame_from(d, 1 - core)]
        return pltpu.make_async_remote_copy(
            src_ref=view, dst_ref=view, send_sem=send_sems.at[d], recv_sem=recv_sems.at[d],
            device_id=sibling, device_id_type=MESH,
        )

    for d in range(1, 8):
        send(x_hbm, xl, xs_sem, xr_sem, d).start()

    load_g.wait()
    same = iota((256, 256), 0) == iota((256, 256), 1)
    keep = mask_ref[...].astype(F32)
    column = jnp.sum(jnp.where(same, keep, 0.0), axis=1, keepdims=True) / KEEP_RATE
    column = column.reshape(8, 4, 8, 1)
    for p in range(8):
        gsrc[p] = gsrc[p] * column[p]

    bases = (0, 128, 384, 640, 640)
    for n in range(5):
        lane = iota((512, 128), 1) + 128 * n
        head = lane // HEAD_DIM
        source = lane + HEAD_DIM * (head + core) - bases[n]
        hit = (iota((512, 128), 0) == source) & (lane < LOCAL * HEAD_DIM)
        sel[n] = jnp.where(hit, 1.0, 0.0).astype(BF16)

    load_x.wait()
    forward(xl, xfs_sem, xfr_sem, 0).start()

    def prepare(step, carry):
        slot = step % 2

        @pl.when(step < 7)
        def _():
            weight_copy(step + 1, 1 - slot).start()

        weight_copy(step, slot).wait()
        rows = pl.ds(pl.multiple_of(step * 144, 16), 144)
        for part in range(3):
            for n in range(5):
                first = D * part + bases[n]
                high, low = split(wst[slot, :, first : first + 512])
                to = pl.ds(PART * part + 128 * n, 128)
                wph[rows, to] = dot(high, sel[n], NN).astype(BF16)
                wpl[rows, to] = dot(low, sel[n], NN).astype(BF16)
        return carry

    lax.fori_loop(0, 8, prepare, 0)

    def head_copy(a):
        return pltpu.make_async_copy(
            wout_hbm.at[pl.ds(HEAD_DIM * (2 * a + core), HEAD_DIM)],
            outw.at[pl.ds(HEAD_DIM * a, HEAD_DIM)],
            w_sem.at[2 + a],
        )

    for a in range(LOCAL):
        head_copy(a).start()

    for d in range(1, 8):
        arrival(xl, xs_sem, xr_sem, d).wait_recv()
        forward(xl, xfs_sem, xfr_sem, d).start()
    for d in range(1, 8):
        send(x_hbm, xl, xs_sem, xr_sem, d).wait_send()
    for d in range(1, 8):
        send(gsrc, gl, gs_sem, gr_sem, d).start()
    own_g = pltpu.make_async_copy(gsrc.at[chip], gl.at[:, own_frame], loc_sem.at[2])
    own_g.start()

    for a in range(LOCAL):
        head_copy(a).wait()
    for n in range(4):
        high, low = split(outw[144 * n : 144 * n + 144, :])
        woh[144 * n : 144 * n + 144, :] = high
        wol[144 * n : 144 * n + 144, :] = low
    woh[576:640, :] = jnp.zeros((64, D), BF16)
    wol[576:640, :] = jnp.zeros((64, D), BF16)

    for d in range(8):
        forwarded(xl, xfs_sem, xfr_sem, d).wait_recv()
    own_g.wait()
    forward(gl, gfs_sem, gfr_sem, 0).start()

    def split_rows(src, high_ref, low_ref, turn):
        def body(g, carry):
            rows = pl.ds(pl.multiple_of(g * 128, 128), 128)
            value = src[g].reshape(128, D)
            high, low = split(value)
            high_ref[rows, 0:D] = high
            low_ref[rows, 0:D] = low
            if turn:
                high, low = split(value.T)
                xth[:, rows] = high
                xtl[:, rows] = low
            return carry

        lax.fori_loop(0, 4, body, 0)

    split_rows(xl, big_h, big_l, True)

    def project(first, width):
        to = pl.ds(first, width)
        qkv[:, to] = dot3(
            big_h[:, 0:D], big_l[:, 0:D], wph[:, to], wpl[:, to], NN
        )

    def project_tile(n, carry):
        project(pl.multiple_of(n * 256, 256), 256)
        return carry

    lax.fori_loop(0, 7, project_tile, 0)
    project(1792, 128)

    for d in range(1, 8):
        arrival(gl, gs_sem, gr_sem, d).wait_recv()
        forward(gl, gfs_sem, gfr_sem, d).start()
    for part in range(3):
        gqkv[:, PART * part + 512 : PART * part + 640] = jnp.zeros((512, 128), F32)
    mixed[:, 512:640] = jnp.zeros((512, 128), F32)
    for d in range(8):
        forwarded(gl, gfs_sem, gfr_sem, d).wait_recv()
    split_rows(gl, gqh, gql, False)

    for first, width in ((0, 256), (256, 256), (512, 128)):
        gm[:, first : first + width] = dot3(
            gqh[:, 0:D], gql[:, 0:D], woh[first : first + width, :], wol[first : first + width, :], NT
        )

    def regroup(g, carry):
        rows = pl.ds(pl.multiple_of(g * 128, 128), 128)
        value = gl[g].reshape(128, D)
        lane = iota((128, 128), 1)
        rest = value[:, 128:256]
        for j in range(8):
            tile = 144 * j // 128
            offset = 144 * j % 128
            if offset:
                window = value[:, 128 * tile : 128 * tile + 256]
                piece = pltpu.roll(window, 256 - offset, 1)[:, 0:128]
            else:
                piece = value[:, 128 * tile : 128 * tile + 128]
            high, low = split(piece)
            gph[rows, 128 * j : 128 * j + 128] = high
            gpl[rows, 128 * j : 128 * j + 128] = low
            if j:
                rest = jnp.where(lane // 16 == j, value[:, 128 * (j + 1) : 128 * (j + 2)], rest)
        high, low = split(rest)
        gph[rows, 1024:1152] = high
        gpl[rows, 1024:1152] = low
        return carry

    lax.fori_loop(0, 4, regroup, 0)

    scaling = HEAD_DIM ** (-0.5)

    def attend(g, carry):
        rows = pl.ds(pl.multiple_of(g * 128, 128), 128)
        same_patch = (iota((128, 128), 0) % 8) == (iota((128, 128), 1) % 8)
        lane = iota((128, 256), 1)
        for a in range(LOCAL):
            first = min(HEAD_DIM * a // 128 * 128, 384)
            low_lane = HEAD_DIM * a - first
            mine = (lane >= low_lane) & (lane < low_lane + HEAD_DIM)
            q = jnp.where(mine, qkv[rows, first : first + 256], 0.0) * scaling
            qh, ql = split(q)
            kh, kl = split(qkv[rows, PART + first : PART + first + 256])
            vh, vl = split(qkv[rows, 2 * PART + first : 2 * PART + first + 256])
            mh, ml = split(jnp.where(mine, gm[rows, first : first + 256], 0.0))
            scores = jnp.where(same_patch, dot3(qh, ql, kh, kl, NT), -1e30)
            expo = jnp.exp(scores - jnp.max(scores, axis=1, keepdims=True))
            attn = expo / jnp.sum(expo, axis=1, keepdims=True)
            ah, al = split(attn)
            grad_attn = dot3(mh, ml, vh, vl, NT)
            grad_scores = attn * (grad_attn - jnp.sum(grad_attn * attn, axis=1, keepdims=True))
            sh, sl = split(grad_scores)
            th, tl = split(attn.T)
            uh, ul = split(grad_scores.T)

            def put(ref, start, value):
                pltpu.store(ref.at[rows, start + first : start + first + 256], value, mask=mine)

            put(mixed, 0, dot3(ah, al, vh, vl, NN))
            put(gqkv, 0, dot3(sh, sl, kh, kl, NN) * scaling)
            put(gqkv, PART, dot3(uh, ul, qh, ql, NN))
            put(gqkv, 2 * PART, dot3(th, tl, mh, ml, NN))
        return carry

    lax.fori_loop(0, 4, attend, 0)

    def arrange(g, carry):
        rows = pl.ds(pl.multiple_of(g * 128, 128), 128)
        high, low = split(gqkv[rows, :])
        gqh[rows, :] = high
        gql[rows, :] = low
        lane = iota((128, 256), 1)
        for j in range(8):
            starts = [PART * ((3 * j + k) // 8) + HEAD_DIM * ((3 * j + k) % 8) for k in range(3)]
            base = starts[0] // 128 * 128
            end = -(-(starts[2] + HEAD_DIM) // 128) * 128
            window = gqkv[rows, base:end]
            value = jnp.zeros((128, 256), F32)
            done = {}
            for k in range(3):
                shift = (starts[k] - base - HEAD_DIM * k) % (end - base)
                if shift not in done:
                    moved = window if shift == 0 else pltpu.roll(window, end - base - shift, 1)
                    done[shift] = moved[:, 0:256]
                value = jnp.where((lane >= HEAD_DIM * k) & (lane < HEAD_DIM * k + HEAD_DIM), done[shift], value)
            high, low = split(value)
            big_h[rows, 256 * j : 256 * j + 256] = high
            big_l[rows, 256 * j : 256 * j + 256] = low
        high, low = split(mixed[rows, :].T)
        mth[:, rows] = high
        mtl[:, rows] = low
        return carry

    lax.fori_loop(0, 4, arrange, 0)

    def out_tile(first, width):
        to = pl.ds(first, width)
        outw[:, to] = dot3(mth[...], mtl[...], gph[:, to], gpl[:, to], NN)[0:576]

    def out_step(n, carry):
        out_tile(pl.multiple_of(n * 256, 256), 256)
        return carry

    lax.fori_loop(0, 4, out_step, 0)
    out_tile(1024, 128)

    def gw_copies(j, slot):
        dy = j // 2
        dx_low = j % 2
        copies = []
        for dx_high in range(2):
            dx = 2 * dx_high + dx_low
            for t, target in enumerate(
                (gw_hbm.at[0, dx, dy], gw_hbm.at[1, dy, :, dx], gw_hbm.at[2, :, dx, dy])
            ):
                copies.append(
                    pltpu.make_async_copy(
                        gwbuf.at[slot, t, dx_high], target, gw_sem.at[slot, 3 * dx_high + t]
                    )
                )
        return copies

    def gw_step(j, carry):
        slot = j % 2

        @pl.when(j >= 2)
        def _():
            for copy in gw_copies(j - 2, slot):
                copy.wait()

        to = pl.ds(pl.multiple_of(j * 256, 256), 256)
        rest = pltpu.roll(outw[:, 1024:1152], (88 + 128 - 16 * j) % 128, 1)
        lane = iota((24, 128), 1)
        inside = (lane >= 88) & (lane < 104)
        main = pl.ds(pl.multiple_of(j * 128, 128), 128)
        term = dot3(xth[...], xtl[...], big_h[:, to], big_l[:, to], NN)
        for i in range(8):
            dz, dx_high = i // 2, i % 2
            for t in range(3):
                row = 144 * i + 48 * t
                gwbuf[slot, t, dx_high, dz, 0:48, :] = term[row : row + 48, 0:128]
                second = term[row : row + 48, 128:256]
                out_row = HEAD_DIM * i + 24 * t
                gwbuf[slot, t, dx_high, dz, 48:72, :] = jnp.where(
                    inside, rest[out_row : out_row + 24], second[0:24]
                )
                gwbuf[slot, t, dx_high, dz, 72:96, :] = second[24:48]
                gwbuf[slot, t, dx_high, dz, 96:120, :] = outw[out_row : out_row + 24, main]
        for copy in gw_copies(j, slot):
            copy.start()
        return carry

    lax.fori_loop(0, 8, gw_step, 0)

    def input_tile(first, width):
        to = pl.ds(first, width)
        term = dot3(gqh[...], gql[...], wph[to, :], wpl[to, :], NT)
        gibuf[:, :, :, to] = term.reshape(4, 16, 8, width)

    def input_step(n, carry):
        input_tile(pl.multiple_of(n * 256, 256), 256)
        return carry

    lax.fori_loop(0, 4, input_step, 0)
    input_tile(1024, 128)
    store = pltpu.make_async_copy(gibuf, gi_hbm, loc_sem.at[3])
    store.start()
    for d in range(1, 8):
        send(gsrc, gl, gs_sem, gr_sem, d).wait_send()
    for d in range(8):
        forward(xl, xfs_sem, xfr_sem, d).wait_send()
        forward(gl, gfs_sem, gfr_sem, d).wait_send()
    for j in (6, 7):
        for copy in gw_copies(j, j % 2):
            copy.wait()
    store.wait()


def exchange_kernel(
    gw_hbm, gi_hbm, input_out, qkv_out, out_out,
    one1, two1, load1, own1, one2, two2, own2, one3, two3, own3, last, other, gi_own, gi_recv,
    rs_send, rs_recv, ld_sem, gi_ld, gx_send, gx_recv, ga_send, ga_recv, fin_sem,
):
    clip = lax.axis_index("clip")
    seq = lax.axis_index("seq")
    chip = seq // 2
    core = seq % 2
    sibling = (clip, 2 * chip + 1 - core)
    here = (2 * (clip % 2) + chip % 2, chip // 2, clip // 2)

    def at(x, y, z):
        return (2 * z + x // 2, 4 * y + 2 * (x % 2) + core)

    def along(axis, step):
        place = list(here)
        place[axis] = (place[axis] + step + 4) % 4
        return at(*place)

    def peer(d):
        return (clip, 2 * ((chip + d) % 8) + core)

    barrier = pltpu.get_barrier_semaphore()
    for axis in range(3):
        for step in (1, -1):
            pl.semaphore_signal(barrier, inc=1, device_id=along(axis, step), device_id_type=MESH)
    for d in range(1, 8):
        pl.semaphore_signal(barrier, inc=1, device_id=peer(d), device_id_type=MESH)
    pl.semaphore_signal(barrier, inc=1, device_id=sibling, device_id_type=MESH)

    orders = ((0, 1, 2), (1, 2, 0), (2, 0, 1))
    ones = (one1, one2, one3)
    twos = (two1, two2, two3)
    halves = (((0, 2), (2, 2)), ((0, 2), (2, 2)), ((0, 64), (64, 56)))

    def spots(t, stage):
        me = here[orders[t][stage]]
        return me, (me + 1) % 4, (me + 3) % 4, (me + 2) % 4

    def source(t, stage, spot, half):
        start, size = halves[stage][half]
        ref = (gw_hbm, own1, own2)[stage]
        return ref.at[t, spot, pl.ds(start, size)]

    def first_hop(t, stage, half):
        me, up, down, far = spots(t, stage)
        start, size = halves[stage][half]
        return pltpu.make_async_remote_copy(
            src_ref=source(t, stage, far, half),
            dst_ref=ones[stage].at[t, half, pl.ds(0, size)],
            send_sem=rs_send.at[t, stage, half],
            recv_sem=rs_recv.at[t, stage, half],
            device_id=along(orders[t][stage], 1 if half == 0 else -1),
            device_id_type=MESH,
        )

    def second_hop(t, stage, way, half):
        me, up, down, far = spots(t, stage)
        start, size = halves[stage][half]
        if half == way:
            src = ones[stage].at[t, half, pl.ds(0, size)]
        else:
            src = source(t, stage, up if way == 0 else down, half)
        slot = 2 + 2 * way + half
        return pltpu.make_async_remote_copy(
            src_ref=src,
            dst_ref=twos[stage].at[t, way, pl.ds(start, size)],
            send_sem=rs_send.at[t, stage, slot],
            recv_sem=rs_recv.at[t, stage, slot],
            device_id=along(orders[t][stage], 1 if way == 0 else -1),
            device_id_type=MESH,
        )

    def local_loads(t):
        me, up, down, far = spots(t, 0)
        return (
            pltpu.make_async_copy(source(t, 0, up, 0), load1.at[t, 0], ld_sem.at[t, 0]),
            pltpu.make_async_copy(source(t, 0, down, 1), load1.at[t, 1], ld_sem.at[t, 1]),
            pltpu.make_async_copy(gw_hbm.at[t, me], own1.at[t], ld_sem.at[t, 2]),
        )

    def gi_load(p):
        return pltpu.make_async_copy(gi_hbm.at[:, 2 * p + core], gi_own.at[p], gi_ld.at[p])

    def gi_cross(p):
        return pltpu.make_async_remote_copy(
            src_ref=gi_hbm.at[:, 2 * p + 1 - core],
            dst_ref=gi_recv.at[p],
            send_sem=gx_send.at[p],
            recv_sem=gx_recv.at[p],
            device_id=sibling,
            device_id_type=MESH,
        )

    def gi_back(d):
        return pltpu.make_async_remote_copy(
            src_ref=gi_own.at[(chip + d) % 8],
            dst_ref=input_out.at[chip],
            send_sem=ga_send.at[d],
            recv_sem=ga_recv.at[d],
            device_id=peer(d),
            device_id_type=MESH,
        )

    def gi_arrival(d):
        view = input_out.at[(chip + 8 - d) % 8]
        return pltpu.make_async_remote_copy(
            src_ref=view, dst_ref=view, send_sem=ga_send.at[d], recv_sem=ga_recv.at[d],
            device_id=peer(d), device_id_type=MESH,
        )

    for t in range(3):
        for copy in local_loads(t):
            copy.start()
    for p in range(8):
        gi_load(p).start()
    pl.semaphore_wait(barrier, 14)

    def open_stage(stage):
        for half in range(2):
            for t in range(3):
                first_hop(t, stage, half).start()
        for way in range(2):
            for t in range(3):
                second_hop(t, stage, way, 1 - way).start()

    def middle(stage):
        for t in range(3):
            for way in range(2):
                first_hop(t, stage, way).wait_recv()
                start, size = halves[stage][way]
                me, up, down, far = spots(t, stage)
                to = ones[stage].at[t, way, pl.ds(0, size)]
                if stage == 0:
                    to[...] = to[...] + load1[t, way]
                else:
                    to[...] = to[...] + source(t, stage, up if way == 0 else down, way)[...]
                second_hop(t, stage, way, way).start()

    def close_stage(stage):
        for t in range(3):
            me, up, down, far = spots(t, stage)
            for way in range(2):
                for half in range(2):
                    second_hop(t, stage, way, half).wait_recv()
            if stage == 0:
                own1[t] = own1[t] + two1[t, 0] + two1[t, 1]
            elif stage == 1:
                own2[t] = own1[t, me] + two2[t, 0] + two2[t, 1]
            else:
                last[t] = own2[t, me] + two3[t, 0] + two3[t, 1]

    open_stage(0)
    for p in range(8):
        gi_cross(p).start()
    for t in range(3):
        for copy in local_loads(t):
            copy.wait()
    for d in range(8):
        p = (chip + d) % 8
        gi_load(p).wait()
        gi_cross(p).wait_recv()
        gi_own[p] = gi_own[p] + gi_recv[p]
        if d:
            gi_back(d).start()
    keep = pltpu.make_async_copy(gi_own.at[chip], input_out.at[chip], fin_sem.at[0])
    keep.start()
    middle(0)
    close_stage(0)
    open_stage(1)
    middle(1)
    close_stage(1)
    open_stage(2)
    middle(2)
    close_stage(2)

    swap = pltpu.make_async_remote_copy(
        src_ref=last, dst_ref=other, send_sem=fin_sem.at[1], recv_sem=fin_sem.at[2],
        device_id=sibling, device_id_type=MESH,
    )
    swap.start()
    swap.wait_recv()

    lane = iota((48, 256), 1)
    even = core == 0
    lane_out = iota((24, 128), 1)
    for t in range(3):
        mine = jnp.concatenate([last[t, 0:48, :], last[t, 48:96, :]], axis=1)
        yours = jnp.concatenate([other[t, 0:48, :], other[t, 48:96, :]], axis=1)
        turned = jnp.where(even, pltpu.roll(mine, HEAD_DIM, 1), pltpu.roll(mine, 256 - HEAD_DIM, 1))
        middle_part = jnp.where(even, pltpu.roll(yours, HEAD_DIM, 1), pltpu.roll(yours, 256 - HEAD_DIM, 1))
        left = jnp.where(even, mine, turned)
        right = jnp.where(even, turned, mine)
        whole = jnp.where(lane < HEAD_DIM, left, jnp.where(lane < 2 * HEAD_DIM, middle_part, right))
        qkv_out[48 * t : 48 * t + 48, :] = whole[:, 0:216]

        def out_rows(ref):
            main = ref[t, 96:120, :]
            rest = pltpu.roll(ref[t, 48:72, :], 128 - 32, 1)
            moved = jnp.where(lane_out < 56, pltpu.roll(main, 128 - HEAD_DIM, 1), rest)
            return jnp.where(even, main, moved)

        a = out_rows(last)
        b = out_rows(other)
        out_out[24 * t : 24 * t + 24, :] = jnp.where(even, a, b)[:, 0:HEAD_DIM]
        out_out[72 + 24 * t : 96 + 24 * t, :] = jnp.where(even, b, a)[:, 0:HEAD_DIM]

    for d in range(1, 8):
        gi_arrival(d).wait_recv()
        gi_back(d).wait_send()
    for p in range(8):
        gi_cross(p).wait_send()
    for stage in range(3):
        for t in range(3):
            for half in range(2):
                first_hop(t, stage, half).wait_send()
                for way in range(2):
                    second_hop(t, stage, way, half).wait_send()
    swap.wait_send()
    keep.wait()


def on_device(x_saved, grad_out, keep_mask, w_qkv, w_out):
    any_space = pl.BlockSpec(memory_space=pl.ANY)
    in_vmem = pl.BlockSpec(memory_space=pltpu.VMEM)
    dma = pltpu.SemaphoreType.DMA
    shape = jax.ShapeDtypeStruct
    vmem = pltpu.VMEM
    gw, gi = pl.pallas_call(
        compute_kernel,
        out_shape=(shape((3, 4, 4, 4, ROWS, 128), F32), shape((4, 16, 8, D), F32)),
        in_specs=[any_space, any_space, in_vmem, any_space, any_space],
        out_specs=(any_space, any_space),
        scratch_shapes=[
            vmem((4, 16, 8, D), F32),
            vmem((4, 16, 8, D), F32),
            vmem((8, 4, 8, D), F32),
            vmem((2, 144, 3 * D), F32),
            vmem((5, 512, 128), BF16),
            vmem((D, 3 * PART), BF16),
            vmem((D, 3 * PART), BF16),
            vmem((PART, D), BF16),
            vmem((PART, D), BF16),
            vmem((D, 512), BF16),
            vmem((D, 512), BF16),
            vmem((512, 3 * PART), F32),
            vmem((512, 3 * PART), F32),
            vmem((512, PART), F32),
            vmem((512, PART), F32),
            vmem((PART, 512), BF16),
            vmem((PART, 512), BF16),
            vmem((512, D), BF16),
            vmem((512, D), BF16),
            vmem((512, 2048), BF16),
            vmem((512, 2048), BF16),
            vmem((512, 3 * PART), BF16),
            vmem((512, 3 * PART), BF16),
            vmem((576, D), F32),
            vmem((2, 3, 2, 4, ROWS, 128), F32),
            vmem((4, 16, 8, D), F32),
            dma((8,)), dma((8,)), dma((8,)), dma((8,)),
            dma((8,)), dma((8,)), dma((8,)), dma((8,)),
            dma((4,)), dma((10,)), dma((2, 6)),
        ],
        compiler_params=pltpu.CompilerParams(
            collective_id=0, has_side_effects=True, vmem_limit_bytes=62 * 2**20
        ),
        cost_estimate=pl.CostEstimate(flops=23 * 10**9, bytes_accessed=40 * 10**6, transcendentals=10**6),
    )(
        x_saved.reshape(8, 4, 8, D),
        grad_out.reshape(8, 4, 8, D),
        keep_mask.reshape(1, 256),
        w_qkv,
        w_out,
    )
    grad_input, total_qkv, total_out = pl.pallas_call(
        exchange_kernel,
        out_shape=(shape((8, 4, 8, D), F32), shape((144, 216), F32), shape((144, 72), F32)),
        in_specs=[any_space, any_space],
        out_specs=(any_space, in_vmem, in_vmem),
        scratch_shapes=[
            vmem((3, 2, 2, 4, ROWS, 128), F32),
            vmem((3, 2, 4, 4, ROWS, 128), F32),
            vmem((3, 2, 2, 4, ROWS, 128), F32),
            vmem((3, 4, 4, ROWS, 128), F32),
            vmem((3, 2, 2, ROWS, 128), F32),
            vmem((3, 2, 4, ROWS, 128), F32),
            vmem((3, 4, ROWS, 128), F32),
            vmem((3, 2, 64, 128), F32),
            vmem((3, 2, ROWS, 128), F32),
            vmem((3, ROWS, 128), F32),
            vmem((3, ROWS, 128), F32),
            vmem((3, ROWS, 128), F32),
            vmem((8, 4, 8, D), F32),
            vmem((8, 4, 8, D), F32),
            dma((3, 3, 6)), dma((3, 3, 6)), dma((3, 3)), dma((8,)),
            dma((8,)), dma((8,)), dma((8,)), dma((8,)), dma((3,)),
        ],
        compiler_params=pltpu.CompilerParams(
            collective_id=1, has_side_effects=True, vmem_limit_bytes=48 * 2**20
        ),
        cost_estimate=pl.CostEstimate(flops=10**7, bytes_accessed=40 * 10**6, transcendentals=0),
    )(gw, gi)
    return (grad_input.reshape(1, 1, 256, D), total_qkv, total_out)


def solution(mesh):
    return jax.shard_map(
        on_device,
        mesh=mesh,
        in_specs=(
            P("clip", "seq", None, None),
            P("clip", "seq", None, None),
            P("clip", "seq", None),
            P(),
            P(),
        ),
        out_specs=(P("clip", "seq", None, None), P("clip", "seq"), P("clip", "seq")),
        check_vma=False,
    )
```

```python
import jax
import jax.numpy as jnp
from jax import lax
from jax.experimental import pallas as pl
from jax.experimental.pallas import tpu as pltpu
from jax.sharding import PartitionSpec as P

HEADS = 16
HEAD_DIM = 72
KEEP_RATE = 0.9
D = 1152
LOCAL = 8
PART = 640
PARTS = ((24, 24, 24), (40, 40, 48), (48, 48, 64))
TOPS = (0, 72, 200)
SHARE = 360
CUTS = ((0, 64), (64, 80))
ORDERS = ((0, 1, 2), (1, 2, 0), (2, 0, 1))
MESH = pl.DeviceIdType.MESH
F32 = jnp.float32
BF16 = jnp.bfloat16

NN = (((1,), (0,)), ((), ()))
NT = (((1,), (1,)), ((), ()))


def split(value):
    high = value.astype(BF16)
    return high, (value - high.astype(F32)).astype(BF16)


def dot(left, right, dims):
    return lax.dot_general(left, right, dims, preferred_element_type=F32)


def dot3(left_high, left_low, right_high, right_low, dims):
    return (
        dot(left_high, right_high, dims)
        + dot(left_low, right_high, dims)
        + dot(left_high, right_low, dims)
    )


def iota(shape, dim):
    return lax.broadcasted_iota(jnp.int32, shape, dim)


def wait_copy(ref, sem):
    pltpu.make_async_copy(ref, ref, sem).wait()


class Share:
    def __init__(self, index, part, t, rows, here, at, gw, load, scratch, sems, last):
        self.index, self.t, self.rows = index, t, rows
        self.here, self.at = here, at
        self.gw, self.load = gw, load
        one1, two1, own1, one2, two2, own2, one3, two3 = scratch
        self.ones, self.twos = (one1, one2, one3), (two1, two2, two3)
        self.sources = (gw, own1, own2)
        self.send_sem, self.recv_sem, self.load_sem = sems
        top = TOPS[part] + sum(PARTS[part][:t])
        self.last = last.at[pl.ds(top, rows)]
        low = (rows // 16) * 8
        self.halves = (((0, 2), (2, 2)), ((0, 2), (2, 2)), ((0, rows - low), (rows - low, low)))

    def along(self, stage, step):
        axis = ORDERS[self.t][stage]
        place = list(self.here)
        place[axis] = (place[axis] + step + 4) % 4
        return self.at(*place)

    def spots(self, stage):
        me = self.here[ORDERS[self.t][stage]]
        return me, (me + 1) % 4, (me + 3) % 4, (me + 2) % 4

    def source(self, stage, spot, half):
        start, size = self.halves[stage][half]
        return self.sources[stage].at[spot, pl.ds(start, size)]

    def first_hop(self, stage, half):
        far = self.spots(stage)[3]
        size = self.halves[stage][half][1]
        return pltpu.make_async_remote_copy(
            src_ref=self.source(stage, far, half),
            dst_ref=self.ones[stage].at[half, pl.ds(0, size)],
            send_sem=self.send_sem.at[self.index, stage, half],
            recv_sem=self.recv_sem.at[self.index, stage, half],
            device_id=self.along(stage, 1 if half == 0 else -1),
            device_id_type=MESH,
        )

    def second_hop(self, stage, way, half):
        me, up, down, far = self.spots(stage)
        start, size = self.halves[stage][half]
        if half == way:
            src = self.ones[stage].at[half, pl.ds(0, size)]
        else:
            src = self.source(stage, up if way == 0 else down, half)
        slot = 2 + 2 * way + half
        return pltpu.make_async_remote_copy(
            src_ref=src,
            dst_ref=self.twos[stage].at[way, pl.ds(start, size)],
            send_sem=self.send_sem.at[self.index, stage, slot],
            recv_sem=self.recv_sem.at[self.index, stage, slot],
            device_id=self.along(stage, 1 if way == 0 else -1),
            device_id_type=MESH,
        )

    def loads(self):
        me, up, down, far = self.spots(0)
        copy = pltpu.make_async_copy
        return (
            copy(self.source(0, up, 0), self.load.at[0], self.load_sem.at[self.index, 0]),
            copy(self.source(0, down, 1), self.load.at[1], self.load_sem.at[self.index, 1]),
            copy(self.gw.at[me], self.sources[1], self.load_sem.at[self.index, 2]),
        )

    def middle(self, stage):
        me, up, down, far = self.spots(stage)
        for way in range(2):
            self.first_hop(stage, way).wait_recv()
            size = self.halves[stage][way][1]
            to = self.ones[stage].at[way, pl.ds(0, size)]
            if stage == 0:
                to[...] = to[...] + self.load[way]
            else:
                to[...] = to[...] + self.source(stage, up if way == 0 else down, way)[...]
            self.second_hop(stage, way, way).start()

    def close(self, stage):
        me = self.spots(stage)[0]
        for way in range(2):
            for half in range(2):
                self.second_hop(stage, way, half).wait_recv()
        two = self.twos[stage]
        if stage == 0:
            own = self.sources[1]
            own[...] = own[...] + two[0] + two[1]
        elif stage == 1:
            own = self.sources[2]
            own[...] = self.sources[1][me] + two[0] + two[1]
        else:
            self.last[...] = self.sources[2][me] + two[0] + two[1]

    def finish(self):
        for stage in range(3):
            for half in range(2):
                self.first_hop(stage, half).wait_send()
                for way in range(2):
                    self.second_hop(stage, way, half).wait_send()


def open_stage(shares, stage):
    for half in range(2):
        for share in shares:
            share.first_hop(stage, half).start()
    for way in range(2):
        for share in shares:
            share.second_hop(stage, way, 1 - way).start()


def middle(shares, stage):
    for share in shares:
        share.middle(stage)


def close(shares, stage):
    for share in shares:
        share.close(stage)


def scratch_of(rows):
    vmem = pltpu.VMEM
    return [
        vmem((2, 2, 4, rows, 128), F32),
        vmem((2, 4, 4, rows, 128), F32),
        vmem((4, 4, rows, 128), F32),
        vmem((2, 2, rows, 128), F32),
        vmem((2, 4, rows, 128), F32),
        vmem((4, rows, 128), F32),
        vmem((2, rows - (rows // 16) * 8, 128), F32),
        vmem((2, rows, 128), F32),
    ]


def stack(high, low):
    return jnp.concatenate([high, low], axis=0)


def all_nt(left, right):
    rows = left.shape[0] // 2
    columns = right.shape[0] // 2
    full = dot(left, right, NT)
    return (full[:rows, :columns] + full[:rows, columns:]) + (full[rows:, :columns] + full[rows:, columns:])


def all_nn(left, right):
    rows = left.shape[0] // 2
    full = dot(jnp.concatenate([left, left], axis=1), right, NN)
    return full[:rows] + full[rows:]


def kernel(*refs):
    x_hbm, g_hbm, mask_ref, wqkv_hbm, wout_hbm = refs[0:5]
    input_out, qkv_out, out_out = refs[5:8]
    gw = [refs[8 + 3 * part : 11 + 3 * part] for part in range(3)]
    (
        xl, gl, gsrc, sel, wph, wpl, woh, wol, xth1, xtl1, xth2, xtl2, qkv, gqkv, gm, mixed, probs, mth, mtl,
        gph, gpl, big_h, big_l, gqh, gql, outw, last, other,
        xs_sem, xr_sem, xfs_sem, xfr_sem, gs_sem, gr_sem, gfs_sem, gfr_sem, loc_sem, w_sem, gw_sem, out_sem,
        rs_send, rs_recv, ld_sem, gx_send, gx_recv, ga_send, ga_recv, fin_sem,
    ) = refs[17:65]
    rest = refs[65:]
    stage_refs = [rest[0:3], rest[3:6]]
    load_refs = rest[6:9]
    rest = rest[9:]

    clip = lax.axis_index("clip")
    seq = lax.axis_index("seq")
    chip = seq // 2
    core = seq % 2
    sibling = (clip, 2 * chip + 1 - core)
    here = (2 * (clip % 2) + chip % 2, chip // 2, clip // 2)

    def at(x, y, z):
        return (2 * z + x // 2, 4 * y + 2 * (x % 2) + core)

    shares = []
    for part in range(3):
        for t in range(3):
            index = 3 * part + t
            rows = PARTS[part][t]
            load = load_refs[t].at[:, :, :, pl.ds(0, rows)]
            shares.append(
                Share(index, part, t, rows, here, at, gw[part][t], load,
                      rest[8 * index : 8 * index + 8], (rs_send, rs_recv, ld_sem), last)
            )
    out_shares, first_shares, second_shares = shares[0:3], shares[3:6], shares[6:9]

    def peer(d):
        return (clip, 2 * ((chip + d) % 8) + core)

    def frame_from(d, c):
        return 2 * ((chip + 8 - d) % 8) + c

    barrier = pltpu.get_barrier_semaphore()
    for d in range(1, 8):
        pl.semaphore_signal(barrier, inc=1, device_id=peer(d), device_id_type=MESH)
    pl.semaphore_signal(barrier, inc=1, device_id=sibling, device_id_type=MESH)
    for t in range(3):
        for step in (1, -1):
            pl.semaphore_signal(
                barrier, inc=1, device_id=out_shares[t].along(0, step), device_id_type=MESH
            )

    own_frame = 2 * chip + core
    load_x = pltpu.make_async_copy(x_hbm.at[chip], xl.at[:, own_frame], loc_sem.at[0])
    load_x.start()
    load_g = pltpu.make_async_copy(g_hbm, gsrc, loc_sem.at[1])
    load_g.start()

    def weight_copy(step, slot):
        rows = pl.ds(pl.multiple_of((step % 6) * 192, 8), 192)
        columns = pl.ds(pl.multiple_of((step // 6) * D, 128), D)
        to = pl.ds(pl.multiple_of(slot * 192, 8), 192)
        return pltpu.make_async_copy(wqkv_hbm.at[rows, columns], qkv.at[to, pl.ds(0, D)], w_sem.at[slot])

    weight_copy(0, 0).start()
    pl.semaphore_wait(barrier, 14)

    def send(src, dst, send_sems, recv_sems, d):
        p = (chip + d) % 8
        return pltpu.make_async_remote_copy(
            src_ref=src.at[p],
            dst_ref=dst.at[:, own_frame],
            send_sem=send_sems.at[d],
            recv_sem=recv_sems.at[d],
            device_id=peer(d),
            device_id_type=MESH,
        )

    def same_place(view, send_sems, recv_sems, d, device):
        return pltpu.make_async_remote_copy(
            src_ref=view, dst_ref=view, send_sem=send_sems.at[d], recv_sem=recv_sems.at[d],
            device_id=device, device_id_type=MESH,
        )

    def arrival(dst, send_sems, recv_sems, d):
        return same_place(dst.at[:, frame_from(d, core)], send_sems, recv_sems, d, peer(d))

    def forward(dst, send_sems, recv_sems, d):
        return same_place(dst.at[:, frame_from(d, core)], send_sems, recv_sems, d, sibling)

    def forwarded(dst, send_sems, recv_sems, d):
        return same_place(dst.at[:, frame_from(d, 1 - core)], send_sems, recv_sems, d, sibling)

    for d in range(1, 8):
        send(x_hbm, xl, xs_sem, xr_sem, d).start()

    load_g.wait()
    same = iota((256, 256), 0) == iota((256, 256), 1)
    keep = mask_ref[...].astype(F32)
    column = jnp.sum(jnp.where(same, keep, 0.0), axis=1, keepdims=True) / KEEP_RATE
    column = column.reshape(8, 4, 8, 1)
    for p in range(8):
        gsrc[p] = gsrc[p] * column[p]

    bases = (0, 128, 384, 640, 640)
    for n in range(5):
        lane = iota((512, 128), 1) + 128 * n
        head = lane // HEAD_DIM
        source = lane + HEAD_DIM * (head + core) - bases[n]
        hit = (iota((512, 128), 0) == source) & (lane < LOCAL * HEAD_DIM)
        sel[n] = jnp.where(hit, 1.0, 0.0).astype(BF16)

    load_x.wait()
    forward(xl, xfs_sem, xfr_sem, 0).start()

    def head_copy(a):
        return pltpu.make_async_copy(
            wout_hbm.at[pl.ds(HEAD_DIM * (2 * a + core), HEAD_DIM)],
            outw.at[a // 2, a % 2],
            w_sem.at[2 + a],
        )

    for a in range(LOCAL):
        head_copy(a).start()

    def prepare(step, carry):
        slot = step % 2

        @pl.when(step < 17)
        def _():
            weight_copy(step + 1, 1 - slot).start()

        weight_copy(step, slot).wait()
        rows = pl.ds(pl.multiple_of((step % 6) * 192, 16), 192)
        staged = pl.ds(pl.multiple_of(slot * 192, 8), 192)
        part = step // 6
        for n in range(5):
            high, low = split(qkv[staged, bases[n] : bases[n] + 512])
            to = pl.ds(pl.multiple_of(PART * part + 128 * n, 128), 128)
            wph[rows, to] = dot(high, sel[n], NN).astype(BF16)
            wpl[rows, to] = dot(low, sel[n], NN).astype(BF16)
        return carry

    lax.fori_loop(0, 18, prepare, 0)

    own_g = pltpu.make_async_copy(gsrc.at[chip], gl.at[:, own_frame], loc_sem.at[2])
    own_g.start()
    for d in range(1, 8):
        send(x_hbm, xl, xs_sem, xr_sem, d).wait_send()
        send(gsrc, gl, gs_sem, gr_sem, d).start()
    for d in range(1, 8):
        arrival(xl, xs_sem, xr_sem, d).wait_recv()
        forward(xl, xfs_sem, xfr_sem, d).start()

    for a in range(LOCAL):
        head_copy(a).wait()
    for n in range(4):
        high, low = split(outw[n].reshape(144, D))
        woh[144 * n : 144 * n + 144, :] = high
        wol[144 * n : 144 * n + 144, :] = low
    woh[576:640, :] = jnp.zeros((64, D), BF16)
    wol[576:640, :] = jnp.zeros((64, D), BF16)
    for part in range(3):
        gqkv[:, PART * part + 512 : PART * part + 640] = jnp.zeros((128, 128), F32)
    mixed[:, 512:640] = jnp.zeros((128, 128), F32)

    for d in range(8):
        forwarded(xl, xfs_sem, xfr_sem, d).wait_recv()
    own_g.wait()
    forward(gl, gfs_sem, gfr_sem, 0).start()

    def split_x(g, carry):
        rows = pl.ds(pl.multiple_of(g * 128, 128), 128)
        value = xl[g].reshape(128, D)
        high, low = split(value)
        big_h[rows, 0:D] = high
        big_l[rows, 0:D] = low
        high, low = split(value.T)
        for i in range(8):
            xth1[64 * i : 64 * i + 64, rows] = high[144 * i : 144 * i + 64]
            xtl1[64 * i : 64 * i + 64, rows] = low[144 * i : 144 * i + 64]
            xth2[80 * i : 80 * i + 80, rows] = high[144 * i + 64 : 144 * i + 144]
            xtl2[80 * i : 80 * i + 80, rows] = low[144 * i + 64 : 144 * i + 144]
        return carry

    lax.fori_loop(0, 4, split_x, 0)

    def project(first, width):
        to = pl.ds(first, width)
        qkv[:, to] = dot3(
            big_h[:, 0:D], big_l[:, 0:D], wph[:, to], wpl[:, to], NN
        )

    def project_tile(n, carry):
        project(pl.multiple_of(n * 256, 256), 256)
        return carry

    lax.fori_loop(0, 7, project_tile, 0)
    project(1792, 128)
    for d in range(8):
        forward(xl, xfs_sem, xfr_sem, d).wait_send()
    for d in range(1, 8):
        arrival(gl, gs_sem, gr_sem, d).wait_recv()
        forward(gl, gfs_sem, gfr_sem, d).start()

    scaling = HEAD_DIM ** (-0.5)
    firsts = [min(HEAD_DIM * a // 128 * 128, 384) for a in range(LOCAL)]

    def own_lanes(a):
        lane = iota((128, 256), 1)
        low_lane = HEAD_DIM * a - firsts[a]
        return (lane >= low_lane) & (lane < low_lane + HEAD_DIM)

    def window(ref, rows, part, a):
        start = PART * part + firsts[a]
        return ref[rows, start : start + 256]

    def attend(g, carry):
        rows = pl.ds(pl.multiple_of(g * 128, 128), 128)
        same_patch = (iota((128, 128), 0) % 8) == (iota((128, 128), 1) % 8)
        for a in range(LOCAL):
            mine = own_lanes(a)
            q = stack(*split(jnp.where(mine, window(qkv, rows, 0, a), 0.0) * scaling))
            k = stack(*split(window(qkv, rows, 1, a)))
            v = stack(*split(window(qkv, rows, 2, a)))
            scores = jnp.where(same_patch, all_nt(q, k), -1e30)
            expo = jnp.exp(scores - jnp.max(scores, axis=1, keepdims=True))
            attn = expo / jnp.sum(expo, axis=1, keepdims=True)
            probs[g, a] = attn
            pltpu.store(
                mixed.at[:, firsts[a] : firsts[a] + 256], all_nn(stack(*split(attn)), v), mask=mine
            )
        high, low = split(mixed[...].T)
        mth[:, rows] = high
        mtl[:, rows] = low
        return carry

    lax.fori_loop(0, 4, attend, 0)

    for d in range(8):
        forwarded(gl, gfs_sem, gfr_sem, d).wait_recv()

    def regroup(g, carry):
        rows = pl.ds(pl.multiple_of(g * 128, 128), 128)
        value = gl[g].reshape(128, D)
        high, low = split(value)
        gqh[rows, 0:D] = high
        gql[rows, 0:D] = low
        lane = iota((128, 128), 1)
        rest = value[:, 128:256]
        for j in range(8):
            tile = 144 * j // 128
            offset = 144 * j % 128
            if offset:
                piece = value[:, 128 * tile : 128 * tile + 256]
                piece = pltpu.roll(piece, 256 - offset, 1)[:, 0:128]
            else:
                piece = value[:, 128 * tile : 128 * tile + 128]
            high, low = split(piece)
            gph[rows, 128 * j : 128 * j + 128] = high
            gpl[rows, 128 * j : 128 * j + 128] = low
            if j:
                rest = jnp.where(lane // 16 == j, value[:, 128 * (j + 1) : 128 * (j + 2)], rest)
        high, low = split(rest)
        gph[rows, 1024:1152] = high
        gpl[rows, 1024:1152] = low
        return carry

    lax.fori_loop(0, 4, regroup, 0)

    def out_tile(first, width):
        to = pl.ds(first, width)
        term = dot3(mth[...], mtl[...], gph[:, to], gpl[:, to], NN)
        outw[:, :, :, to] = term[0:576].reshape(4, 2, 72, width)

    def out_step(n, carry):
        out_tile(pl.multiple_of(n * 256, 256), 256)
        return carry

    lax.fori_loop(0, 4, out_step, 0)
    out_tile(1024, 128)

    def targets(part, dx, dy):
        first, second, third = gw[part]
        return (first.at[dx, dy], second.at[dy, :, dx], third.at[:, dx, dy])

    def out_copies(j):
        columns = pl.ds(pl.multiple_of(j * 128, 128), 128)
        copies = []
        for dx_high in range(2):
            for t, target in enumerate(targets(0, 2 * dx_high + j % 2, j // 2)):
                copies.append(
                    pltpu.make_async_copy(
                        outw.at[:, dx_high, pl.ds(24 * t, 24), columns], target, out_sem.at[j, 3 * dx_high + t]
                    )
                )
        return copies

    def out_start(j, carry):
        for copy in out_copies(j):
            copy.start()
        return carry

    def out_wait(j, carry):
        for copy in out_copies(j):
            copy.wait()
        return carry

    lax.fori_loop(0, 8, out_start, 0)

    for first, width in ((0, 256), (256, 256), (512, 128)):
        gm[:, first : first + width] = dot3(
            gqh[:, 0:D], gql[:, 0:D], woh[first : first + width, :], wol[first : first + width, :], NT
        )

    lax.fori_loop(0, 8, out_wait, 0)
    open_stage(out_shares, 0)
    for share in out_shares:
        for copy in share.loads():
            copy.start()
    for share in out_shares:
        for copy in share.loads():
            copy.wait()

    def attend_back(g, carry):
        rows = pl.ds(pl.multiple_of(g * 128, 128), 128)

        def put(part, a, value):
            start = PART * part + firsts[a]
            pltpu.store(gqkv.at[:, start : start + 256], value, mask=own_lanes(a))

        for a in range(LOCAL):
            mine = own_lanes(a)
            q = stack(*split(jnp.where(mine, window(qkv, rows, 0, a), 0.0) * scaling))
            k = stack(*split(window(qkv, rows, 1, a)))
            v = stack(*split(window(qkv, rows, 2, a)))
            m = stack(*split(jnp.where(mine, gm[rows, firsts[a] : firsts[a] + 256], 0.0)))
            attn = probs[g, a]
            grad_attn = all_nt(m, v)
            grad_scores = attn * (grad_attn - jnp.sum(grad_attn * attn, axis=1, keepdims=True))
            put(0, a, all_nn(stack(*split(grad_scores)), k) * scaling)
            put(1, a, all_nn(stack(*split(grad_scores.T)), q))
            put(2, a, all_nn(stack(*split(attn.T)), m))

        high, low = split(gqkv[...])
        gqh[rows, :] = high
        gql[rows, :] = low
        lane = iota((128, 256), 1)
        for j in range(8):
            starts = [PART * ((3 * j + k) // 8) + HEAD_DIM * ((3 * j + k) % 8) for k in range(3)]
            base = starts[0] // 128 * 128
            end = -(-(starts[2] + HEAD_DIM) // 128) * 128
            span = gqkv[:, base:end]
            value = jnp.zeros((128, 256), F32)
            done = {}
            for k in range(3):
                shift = (starts[k] - base - HEAD_DIM * k) % (end - base)
                if shift not in done:
                    moved = span if shift == 0 else pltpu.roll(span, end - base - shift, 1)
                    done[shift] = moved[:, 0:256]
                value = jnp.where((lane >= HEAD_DIM * k) & (lane < HEAD_DIM * k + HEAD_DIM), done[shift], value)
            high, low = split(value)
            big_h[rows, 256 * j : 256 * j + 256] = high
            big_l[rows, 256 * j : 256 * j + 256] = low
        return carry

    lax.fori_loop(0, 2, attend_back, 0)
    middle(out_shares, 0)
    lax.fori_loop(2, 4, attend_back, 0)
    close(out_shares, 0)
    open_stage(out_shares, 1)

    def gw_copies(which, j, slot):
        copies = []
        for dx_high in range(2):
            for t, target in enumerate(targets(1 + which, 2 * dx_high + j % 2, j // 2)):
                copies.append(
                    pltpu.make_async_copy(
                        stage_refs[which][t].at[slot, dx_high], target, gw_sem.at[which, slot, 3 * dx_high + t]
                    )
                )
        return copies

    def gw_part(which):
        high_ref, low_ref = ((xth1, xtl1), (xth2, xtl2))[which]
        size = CUTS[which][1]

        def gw_step(j, carry):
            slot = j % 2

            @pl.when(j >= 2)
            def _():
                for copy in gw_copies(which, j - 2, slot):
                    copy.wait()

            to = pl.ds(pl.multiple_of(j * 256, 256), 256)
            term = dot3(high_ref[...], low_ref[...], big_h[:, to], big_l[:, to], NN)
            inside = iota((8, 128), 1)
            inside = (inside >= 88) & (inside < 104)
            for i in range(8):
                dz, dx_high = i // 2, i % 2
                if which == 1:
                    rest = pltpu.roll(outw[dz, dx_high, :, 1024:1152], (88 + 128 - 16 * j) % 128, 1)
                top = 0
                for t in range(3):
                    for r in range(0, PARTS[1 + which][t], 8):
                        row = top + r
                        if row < size:
                            value = term[size * i + row : size * i + row + 8, 0:128]
                        else:
                            row = row - size
                            value = term[size * i + row : size * i + row + 8, 128:256]
                            if which == 1 and row < HEAD_DIM:
                                value = jnp.where(inside, rest[row : row + 8], value)
                        stage_refs[which][t][slot, dx_high, dz, r : r + 8, :] = value
                    top += PARTS[1 + which][t]
            for copy in gw_copies(which, j, slot):
                copy.start()
            return carry

        lax.fori_loop(0, 8, gw_step, 0)
        for j in (6, 7):
            for copy in gw_copies(which, j, j % 2):
                copy.wait()

    gw_part(0)
    open_stage(first_shares, 0)
    for share in first_shares:
        for copy in share.loads():
            copy.start()
    middle(out_shares, 1)
    close(out_shares, 1)
    open_stage(out_shares, 2)
    gw_part(1)
    for share in first_shares:
        for copy in share.loads():
            copy.wait()
    middle(first_shares, 0)
    open_stage(second_shares, 0)
    for share in second_shares:
        for copy in share.loads():
            copy.start()
    middle(out_shares, 2)
    close(out_shares, 2)

    def gi_cross(p):
        return pltpu.make_async_remote_copy(
            src_ref=gl.at[:, 2 * p + 1 - core],
            dst_ref=xl.at[:, 2 * p + 1 - core],
            send_sem=gx_send.at[p],
            recv_sem=gx_recv.at[p],
            device_id=sibling,
            device_id_type=MESH,
        )

    def gi_crossed(p):
        return same_place(xl.at[:, 2 * p + core], gx_send, gx_recv, p, sibling)

    def gi_back(d):
        return pltpu.make_async_remote_copy(
            src_ref=gl.at[:, 2 * ((chip + d) % 8) + core],
            dst_ref=input_out.at[chip],
            send_sem=ga_send.at[d],
            recv_sem=ga_recv.at[d],
            device_id=peer(d),
            device_id_type=MESH,
        )

    def gi_arrival(d):
        return same_place(input_out.at[(chip + 8 - d) % 8], ga_send, ga_recv, d, peer(d))

    for d in range(1, 8):
        send(gsrc, gl, gs_sem, gr_sem, d).wait_send()
    for d in range(8):
        forward(gl, gfs_sem, gfr_sem, d).wait_send()

    def input_tile(first, width):
        to = pl.ds(first, width)
        term = dot3(gqh[...], gql[...], wph[to, :], wpl[to, :], NT)
        gl[:, :, :, to] = term.reshape(4, 16, 8, width)

    def input_step(n, carry):
        input_tile(pl.multiple_of(n * 256, 256), 256)
        return carry

    lax.fori_loop(0, 4, input_step, 0)
    input_tile(1024, 128)
    for p in range(8):
        gi_cross(p).start()
    close(first_shares, 0)
    open_stage(first_shares, 1)
    for share in second_shares:
        for copy in share.loads():
            copy.wait()
    middle(second_shares, 0)
    for d in range(8):
        p = (chip + d) % 8
        gi_crossed(p).wait_recv()
        mine = 2 * p + core
        gl[:, mine] = gl[:, mine] + xl[:, mine]
        if d:
            gi_back(d).start()
    own_input = pltpu.make_async_copy(gl.at[:, own_frame], input_out.at[chip], fin_sem.at[0])
    own_input.start()
    middle(first_shares, 1)
    close(second_shares, 0)
    open_stage(second_shares, 1)
    close(first_shares, 1)
    open_stage(first_shares, 2)
    middle(second_shares, 1)
    middle(first_shares, 2)
    close(second_shares, 1)
    open_stage(second_shares, 2)
    close(first_shares, 2)

    def swap(start, size, sem):
        return pltpu.make_async_remote_copy(
            src_ref=last.at[pl.ds(start, size)], dst_ref=other.at[pl.ds(start, size)],
            send_sem=fin_sem.at[sem], recv_sem=fin_sem.at[sem + 1],
            device_id=sibling, device_id_type=MESH,
        )

    swaps = (swap(0, TOPS[2], 1), swap(TOPS[2], SHARE - TOPS[2], 3))
    swaps[0].start()
    middle(second_shares, 2)
    close(second_shares, 2)
    swaps[1].start()
    swaps[0].wait_recv()

    even = core == 0

    def qkv_rows(which):
        first, size = CUTS[which]
        top = TOPS[1 + which]

        def both(ref):
            return jnp.concatenate([ref[top : top + size], ref[top + size : top + 2 * size]], axis=1)

        def turn(value):
            return jnp.where(even, pltpu.roll(value, HEAD_DIM, 1), pltpu.roll(value, 256 - HEAD_DIM, 1))

        mine, yours = both(last), both(other)
        lane = iota((size, 256), 1)
        turned = turn(mine)
        left = jnp.where(even, mine, turned)
        right = jnp.where(even, turned, mine)
        whole = jnp.where(lane < HEAD_DIM, left, jnp.where(lane < 2 * HEAD_DIM, turn(yours), right))
        qkv_out[first : first + size, :] = whole[:, 0:216]

    qkv_rows(0)
    swaps[1].wait_recv()
    qkv_rows(1)

    def out_rows(ref):
        lane = iota((72, 128), 1)
        main = ref[0:72]
        rest = pltpu.roll(ref[TOPS[2] + 80 : TOPS[2] + 152], 128 - 32, 1)
        return jnp.where(even, main, jnp.where(lane < 56, pltpu.roll(main, 128 - HEAD_DIM, 1), rest))

    a = out_rows(last)
    b = out_rows(other)
    out_out[0:72, :] = jnp.where(even, a, b)[:, 0:HEAD_DIM]
    out_out[72:144, :] = jnp.where(even, b, a)[:, 0:HEAD_DIM]

    for d in range(1, 8):
        gi_arrival(d).wait_recv()
        gi_back(d).wait_send()
    for p in range(8):
        gi_cross(p).wait_send()
    for share in shares:
        share.finish()
    for copy in swaps:
        copy.wait_send()
    own_input.wait()


def on_device(x_saved, grad_out, keep_mask, w_qkv, w_out):
    any_space = pl.BlockSpec(memory_space=pl.ANY)
    in_vmem = pl.BlockSpec(memory_space=pltpu.VMEM)
    dma = pltpu.SemaphoreType.DMA
    shape = jax.ShapeDtypeStruct
    vmem = pltpu.VMEM
    heaps = [shape((4, 4, 4, rows, 128), F32) for part in PARTS for rows in part]
    scratch = [
        vmem((4, 16, 8, D), F32),
        vmem((4, 16, 8, D), F32),
        vmem((8, 4, 8, D), F32),
        vmem((5, 512, 128), BF16),
        vmem((D, 3 * PART), BF16),
        vmem((D, 3 * PART), BF16),
        vmem((PART, D), BF16),
        vmem((PART, D), BF16),
        vmem((512, 512), BF16),
        vmem((512, 512), BF16),
        vmem((640, 512), BF16),
        vmem((640, 512), BF16),
        vmem((512, 3 * PART), F32),
        vmem((128, 3 * PART), F32),
        vmem((512, PART), F32),
        vmem((128, PART), F32),
        vmem((4, LOCAL, 128, 128), F32),
        vmem((PART, 512), BF16),
        vmem((PART, 512), BF16),
        vmem((512, D), BF16),
        vmem((512, D), BF16),
        vmem((512, 2048), BF16),
        vmem((512, 2048), BF16),
        vmem((512, 3 * PART), BF16),
        vmem((512, 3 * PART), BF16),
        vmem((4, 2, 72, D), F32),
        vmem((SHARE, 128), F32),
        vmem((SHARE, 128), F32),
        dma((8,)), dma((8,)), dma((8,)), dma((8,)),
        dma((8,)), dma((8,)), dma((8,)), dma((8,)),
        dma((3,)), dma((10,)), dma((2, 2, 6)), dma((8, 6)),
        dma((9, 3, 6)), dma((9, 3, 6)), dma((9, 3)),
        dma((8,)), dma((8,)), dma((8,)), dma((8,)), dma((5,)),
    ]
    for part in (1, 2):
        scratch += [vmem((2, 2, 4, rows, 128), F32) for rows in PARTS[part]]
    scratch += [vmem((2, 2, 4, max(part[t] for part in PARTS), 128), F32) for t in range(3)]
    for part in PARTS:
        for rows in part:
            scratch += scratch_of(rows)
    outputs = pl.pallas_call(
        kernel,
        out_shape=[shape((8, 4, 8, D), F32), shape((144, 216), F32), shape((144, 72), F32)] + heaps,
        in_specs=[any_space, any_space, in_vmem, any_space, any_space],
        out_specs=[any_space, in_vmem, in_vmem] + [any_space] * 9,
        scratch_shapes=scratch,
        compiler_params=pltpu.CompilerParams(
            collective_id=0, has_side_effects=True, vmem_limit_bytes=64 * 2**20
        ),
        cost_estimate=pl.CostEstimate(flops=23 * 10**9, bytes_accessed=60 * 10**6, transcendentals=10**6),
    )(
        x_saved.reshape(8, 4, 8, D),
        grad_out.reshape(8, 4, 8, D),
        keep_mask.reshape(1, 256),
        w_qkv,
        w_out,
    )
    return (outputs[0].reshape(1, 1, 256, D), outputs[1], outputs[2])


def solution(mesh):
    return jax.shard_map(
        on_device,
        mesh=mesh,
        in_specs=(
            P("clip", "seq", None, None),
            P("clip", "seq", None, None),
            P("clip", "seq", None),
            P(),
            P(),
        ),
        out_specs=(P("clip", "seq", None, None), P("clip", "seq"), P("clip", "seq")),
        check_vma=False,
    )
```

```python
import jax
import jax.numpy as jnp
from jax import lax
from jax.experimental import pallas as pl
from jax.experimental.pallas import tpu as pltpu
from jax.sharding import PartitionSpec as P

HEADS = 16
HEAD_DIM = 72
KEEP_RATE = 0.9
D = 1152
LOCAL = 8
PART = 640
PARTS = ((24, 24, 24), (40, 40, 48), (48, 48, 64))
TOPS = (0, 72, 200)
SHARE = 360
CUTS = ((0, 64), (64, 80))
ORDERS = ((0, 1, 2), (1, 2, 0), (2, 0, 1))
MESH = pl.DeviceIdType.MESH
F32 = jnp.float32
BF16 = jnp.bfloat16

NN = (((1,), (0,)), ((), ()))
NT = (((1,), (1,)), ((), ()))


def split(value):
    high = value.astype(BF16)
    return high, (value - high.astype(F32)).astype(BF16)


def dot(left, right, dims):
    return lax.dot_general(left, right, dims, preferred_element_type=F32)


def dot3(left_high, left_low, right_high, right_low, dims):
    return (
        dot(left_high, right_high, dims)
        + dot(left_low, right_high, dims)
        + dot(left_high, right_low, dims)
    )


def iota(shape, dim):
    return lax.broadcasted_iota(jnp.int32, shape, dim)


def wait_copy(ref, sem):
    pltpu.make_async_copy(ref, ref, sem).wait()


class Share:
    def __init__(self, index, part, t, rows, here, at, gw, load, scratch, sems, last):
        self.index, self.t, self.rows = index, t, rows
        self.here, self.at = here, at
        self.gw, self.load = gw, load
        one1, two1, own1, one2, two2, own2, three = scratch
        self.ones, self.twos, self.three = (one1, one2), (two1, two2), three
        self.sources = (gw, own1, own2)
        self.send_sem, self.recv_sem, self.load_sem = sems
        top = TOPS[part] + sum(PARTS[part][:t])
        self.last = last.at[pl.ds(top, rows)]
        self.halves = (((0, 2), (2, 2)), ((0, 2), (2, 2)))

    def along(self, stage, step):
        axis = ORDERS[self.t][stage]
        place = list(self.here)
        place[axis] = (place[axis] + step + 4) % 4
        return self.at(*place)

    def spots(self, stage):
        me = self.here[ORDERS[self.t][stage]]
        return me, (me + 1) % 4, (me + 3) % 4, (me + 2) % 4

    def source(self, stage, spot, half):
        start, size = self.halves[stage][half]
        return self.sources[stage].at[spot, pl.ds(start, size)]

    def first_hop(self, stage, half):
        far = self.spots(stage)[3]
        size = self.halves[stage][half][1]
        return pltpu.make_async_remote_copy(
            src_ref=self.source(stage, far, half),
            dst_ref=self.ones[stage].at[half, pl.ds(0, size)],
            send_sem=self.send_sem.at[self.index, stage, half],
            recv_sem=self.recv_sem.at[self.index, stage, half],
            device_id=self.along(stage, 1 if half == 0 else -1),
            device_id_type=MESH,
        )

    def second_hop(self, stage, way, half):
        me, up, down, far = self.spots(stage)
        start, size = self.halves[stage][half]
        if half == way:
            src = self.ones[stage].at[half, pl.ds(0, size)]
        else:
            src = self.source(stage, up if way == 0 else down, half)
        slot = 2 + 2 * way + half
        return pltpu.make_async_remote_copy(
            src_ref=src,
            dst_ref=self.twos[stage].at[way, pl.ds(start, size)],
            send_sem=self.send_sem.at[self.index, stage, slot],
            recv_sem=self.recv_sem.at[self.index, stage, slot],
            device_id=self.along(stage, 1 if way == 0 else -1),
            device_id_type=MESH,
        )

    def direct(self, way):
        step = (1, -1, 2)[way]
        return pltpu.make_async_remote_copy(
            src_ref=self.sources[2].at[(self.spots(2)[0] + step + 4) % 4],
            dst_ref=self.three.at[way],
            send_sem=self.send_sem.at[self.index, 2, way],
            recv_sem=self.recv_sem.at[self.index, 2, way],
            device_id=self.along(2, step),
            device_id_type=MESH,
        )

    def loads(self):
        me, up, down, far = self.spots(0)
        copy = pltpu.make_async_copy
        return (
            copy(self.source(0, up, 0), self.load.at[0], self.load_sem.at[self.index, 0]),
            copy(self.source(0, down, 1), self.load.at[1], self.load_sem.at[self.index, 1]),
            copy(self.gw.at[me], self.sources[1], self.load_sem.at[self.index, 2]),
        )

    def middle(self, stage):
        me, up, down, far = self.spots(stage)
        for way in range(2):
            self.first_hop(stage, way).wait_recv()
            size = self.halves[stage][way][1]
            to = self.ones[stage].at[way, pl.ds(0, size)]
            if stage == 0:
                to[...] = to[...] + self.load[way]
            else:
                to[...] = to[...] + self.source(stage, up if way == 0 else down, way)[...]
            self.second_hop(stage, way, way).start()

    def close(self, stage):
        me = self.spots(stage)[0]
        if stage == 2:
            for way in range(3):
                self.direct(way).wait_recv()
            self.last[...] = self.sources[2][me] + self.three[0] + self.three[1] + self.three[2]
            return
        for way in range(2):
            for half in range(2):
                self.second_hop(stage, way, half).wait_recv()
        two = self.twos[stage]
        if stage == 0:
            own = self.sources[1]
            own[...] = own[...] + two[0] + two[1]
        else:
            own = self.sources[2]
            own[...] = self.sources[1][me] + two[0] + two[1]

    def finish(self):
        for stage in range(2):
            for half in range(2):
                self.first_hop(stage, half).wait_send()
                for way in range(2):
                    self.second_hop(stage, way, half).wait_send()
        for way in range(3):
            self.direct(way).wait_send()


def open_stage(shares, stage):
    if stage == 2:
        for way in (2, 0, 1):
            for share in shares:
                share.direct(way).start()
        return
    for half in range(2):
        for share in shares:
            share.first_hop(stage, half).start()
    for way in range(2):
        for share in shares:
            share.second_hop(stage, way, 1 - way).start()


def middle(shares, stage):
    for share in shares:
        share.middle(stage)


def close(shares, stage):
    for share in shares:
        share.close(stage)


def scratch_of(rows):
    vmem = pltpu.VMEM
    return [
        vmem((2, 2, 4, rows, 128), F32),
        vmem((2, 4, 4, rows, 128), F32),
        vmem((4, 4, rows, 128), F32),
        vmem((2, 2, rows, 128), F32),
        vmem((2, 4, rows, 128), F32),
        vmem((4, rows, 128), F32),
        vmem((3, rows, 128), F32),
    ]


def stack(high, low):
    return jnp.concatenate([high, low], axis=0)


def all_nt(left, right):
    rows = left.shape[0] // 2
    columns = right.shape[0] // 2
    full = dot(left, right, NT)
    return (full[:rows, :columns] + full[:rows, columns:]) + (full[rows:, :columns] + full[rows:, columns:])


def all_nn(left, right):
    rows = left.shape[0] // 2
    full = dot(jnp.concatenate([left, left], axis=1), right, NN)
    return full[:rows] + full[rows:]


def kernel(*refs):
    x_hbm, g_hbm, mask_ref, wqkv_hbm, wout_hbm = refs[0:5]
    input_out, qkv_out, out_out = refs[5:8]
    gw = [refs[8 + 3 * part : 11 + 3 * part] for part in range(3)]
    (
        xl, gl, gsrc, sel, wph, wpl, woh, wol, xth1, xtl1, xth2, xtl2, qkv, gqkv, gm, mixed, probs, mth, mtl,
        gph, gpl, big_h, big_l, gqh, gql, outw, last, other,
        xs_sem, xr_sem, xfs_sem, xfr_sem, gs_sem, gr_sem, gfs_sem, gfr_sem, loc_sem, w_sem, gw_sem, out_sem,
        rs_send, rs_recv, ld_sem, gx_send, gx_recv, ga_send, ga_recv, fin_sem,
    ) = refs[17:65]
    rest = refs[65:]
    stage_refs = [rest[0:3], rest[3:6]]
    load_refs = rest[6:9]
    rest = rest[9:]

    clip = lax.axis_index("clip")
    seq = lax.axis_index("seq")
    chip = seq // 2
    core = seq % 2
    sibling = (clip, 2 * chip + 1 - core)
    here = (2 * (clip % 2) + chip % 2, chip // 2, clip // 2)

    def at(x, y, z):
        return (2 * z + x // 2, 4 * y + 2 * (x % 2) + core)

    shares = []
    for part in range(3):
        for t in range(3):
            index = 3 * part + t
            rows = PARTS[part][t]
            load = load_refs[t].at[:, :, :, pl.ds(0, rows)]
            shares.append(
                Share(index, part, t, rows, here, at, gw[part][t], load,
                      rest[7 * index : 7 * index + 7], (rs_send, rs_recv, ld_sem), last)
            )
    out_shares, first_shares, second_shares = shares[0:3], shares[3:6], shares[6:9]

    def peer(d):
        return (clip, 2 * ((chip + d) % 8) + core)

    def frame_from(d, c):
        return 2 * ((chip + 8 - d) % 8) + c

    barrier = pltpu.get_barrier_semaphore()
    for d in range(1, 8):
        pl.semaphore_signal(barrier, inc=1, device_id=peer(d), device_id_type=MESH)
    pl.semaphore_signal(barrier, inc=1, device_id=sibling, device_id_type=MESH)
    for t in range(3):
        for step in (1, -1, 2):
            pl.semaphore_signal(
                barrier, inc=1, device_id=out_shares[t].along(0, step), device_id_type=MESH
            )

    own_frame = 2 * chip + core
    load_x = pltpu.make_async_copy(x_hbm.at[chip], xl.at[:, own_frame], loc_sem.at[0])
    load_x.start()
    load_g = pltpu.make_async_copy(g_hbm, gsrc, loc_sem.at[1])
    load_g.start()

    def weight_copy(step, slot):
        rows = pl.ds(pl.multiple_of((step % 6) * 192, 8), 192)
        columns = pl.ds(pl.multiple_of((step // 6) * D, 128), D)
        to = pl.ds(pl.multiple_of(slot * 192, 8), 192)
        return pltpu.make_async_copy(wqkv_hbm.at[rows, columns], qkv.at[to, pl.ds(0, D)], w_sem.at[slot])

    weight_copy(0, 0).start()
    pl.semaphore_wait(barrier, 17)

    def send(src, dst, send_sems, recv_sems, d, h):
        p = (chip + d) % 8
        return pltpu.make_async_remote_copy(
            src_ref=src.at[p, pl.ds(2 * h, 2)],
            dst_ref=dst.at[pl.ds(2 * h, 2), own_frame],
            send_sem=send_sems.at[h, d],
            recv_sem=recv_sems.at[h, d],
            device_id=peer(d),
            device_id_type=MESH,
        )

    def same_place(view, send_sems, recv_sems, d, device):
        return pltpu.make_async_remote_copy(
            src_ref=view, dst_ref=view, send_sem=send_sems.at[d], recv_sem=recv_sems.at[d],
            device_id=device, device_id_type=MESH,
        )

    def arrival(dst, send_sems, recv_sems, d, h):
        view = dst.at[pl.ds(2 * h, 2), frame_from(d, core)]
        return same_place(view, send_sems.at[h], recv_sems.at[h], d, peer(d))

    def forward(dst, send_sems, recv_sems, d, h):
        view = dst.at[pl.ds(2 * h, 2), frame_from(d, core)]
        return same_place(view, send_sems.at[h], recv_sems.at[h], d, sibling)

    def forwarded(dst, send_sems, recv_sems, d, h):
        view = dst.at[pl.ds(2 * h, 2), frame_from(d, 1 - core)]
        return same_place(view, send_sems.at[h], recv_sems.at[h], d, sibling)

    for h in range(2):
        for d in range(1, 8):
            send(x_hbm, xl, xs_sem, xr_sem, d, h).start()

    load_g.wait()
    same = iota((256, 256), 0) == iota((256, 256), 1)
    keep = mask_ref[...].astype(F32)
    column = jnp.sum(jnp.where(same, keep, 0.0), axis=1, keepdims=True) / KEEP_RATE
    column = column.reshape(8, 4, 8, 1)
    for p in range(8):
        gsrc[p] = gsrc[p] * column[p]

    bases = (0, 128, 384, 640, 640)
    for n in range(5):
        lane = iota((512, 128), 1) + 128 * n
        head = lane // HEAD_DIM
        source = lane + HEAD_DIM * (head + core) - bases[n]
        hit = (iota((512, 128), 0) == source) & (lane < LOCAL * HEAD_DIM)
        sel[n] = jnp.where(hit, 1.0, 0.0).astype(BF16)

    load_x.wait()
    for h in range(2):
        forward(xl, xfs_sem, xfr_sem, 0, h).start()

    def head_copy(a):
        return pltpu.make_async_copy(
            wout_hbm.at[pl.ds(HEAD_DIM * (2 * a + core), HEAD_DIM)],
            outw.at[a // 2, a % 2],
            w_sem.at[2 + a],
        )

    for a in range(LOCAL):
        head_copy(a).start()

    def prepare(step, carry):
        slot = step % 2

        @pl.when(step < 17)
        def _():
            weight_copy(step + 1, 1 - slot).start()

        weight_copy(step, slot).wait()
        rows = pl.ds(pl.multiple_of((step % 6) * 192, 16), 192)
        staged = pl.ds(pl.multiple_of(slot * 192, 8), 192)
        part = step // 6
        for n in range(5):
            high, low = split(qkv[staged, bases[n] : bases[n] + 512])
            to = pl.ds(pl.multiple_of(PART * part + 128 * n, 128), 128)
            wph[rows, to] = dot(high, sel[n], NN).astype(BF16)
            wpl[rows, to] = dot(low, sel[n], NN).astype(BF16)
        return carry

    lax.fori_loop(0, 18, prepare, 0)

    own_g = pltpu.make_async_copy(gsrc.at[chip], gl.at[:, own_frame], loc_sem.at[2])
    own_g.start()
    for h in range(2):
        for d in range(1, 8):
            send(gsrc, gl, gs_sem, gr_sem, d, h).start()

    def pass_on(dst, sems, h):
        for d in range(1, 8):
            arrival(dst, sems[0], sems[1], d, h).wait_recv()
            forward(dst, sems[2], sems[3], d, h).start()

    x_sems = (xs_sem, xr_sem, xfs_sem, xfr_sem)
    g_sems = (gs_sem, gr_sem, gfs_sem, gfr_sem)
    pass_on(xl, x_sems, 0)

    for a in range(LOCAL):
        head_copy(a).wait()
    for n in range(4):
        high, low = split(outw[n].reshape(144, D))
        woh[144 * n : 144 * n + 144, :] = high
        wol[144 * n : 144 * n + 144, :] = low
    woh[576:640, :] = jnp.zeros((64, D), BF16)
    wol[576:640, :] = jnp.zeros((64, D), BF16)
    for part in range(3):
        gqkv[:, PART * part + 512 : PART * part + 640] = jnp.zeros((128, 128), F32)
    mixed[:, 512:640] = jnp.zeros((128, 128), F32)

    own_g.wait()
    for h in range(2):
        forward(gl, gfs_sem, gfr_sem, 0, h).start()
    for d in range(8):
        forwarded(xl, xfs_sem, xfr_sem, d, 0).wait_recv()

    def split_x(g, carry):
        rows = pl.ds(pl.multiple_of(g * 128, 128), 128)
        value = xl[g].reshape(128, D)
        high, low = split(value)
        big_h[rows, 0:D] = high
        big_l[rows, 0:D] = low
        high, low = split(value.T)
        for i in range(8):
            xth1[64 * i : 64 * i + 64, rows] = high[144 * i : 144 * i + 64]
            xtl1[64 * i : 64 * i + 64, rows] = low[144 * i : 144 * i + 64]
            xth2[80 * i : 80 * i + 80, rows] = high[144 * i + 64 : 144 * i + 144]
            xtl2[80 * i : 80 * i + 80, rows] = low[144 * i + 64 : 144 * i + 144]
        return carry

    def project(h, first, width):
        to = pl.ds(first, width)
        rows = pl.ds(256 * h, 256)
        qkv[rows, to] = dot3(
            big_h[rows, 0:D], big_l[rows, 0:D], wph[:, to], wpl[:, to], NN
        )

    def project_half(h):
        def project_tile(n, carry):
            project(h, pl.multiple_of(n * 256, 256), 256)
            return carry

        lax.fori_loop(0, 7, project_tile, 0)
        project(h, 1792, 128)

    lax.fori_loop(0, 2, split_x, 0)
    pass_on(xl, x_sems, 1)
    project_half(0)
    for d in range(8):
        forwarded(xl, xfs_sem, xfr_sem, d, 1).wait_recv()
    lax.fori_loop(2, 4, split_x, 0)
    project_half(1)
    for h in range(2):
        for d in range(8):
            forward(xl, xfs_sem, xfr_sem, d, h).wait_send()
    pass_on(gl, g_sems, 0)
    pass_on(gl, g_sems, 1)

    scaling = HEAD_DIM ** (-0.5)
    firsts = [min(HEAD_DIM * a // 128 * 128, 384) for a in range(LOCAL)]

    def own_lanes(a):
        lane = iota((128, 256), 1)
        low_lane = HEAD_DIM * a - firsts[a]
        return (lane >= low_lane) & (lane < low_lane + HEAD_DIM)

    def window(ref, rows, part, a):
        start = PART * part + firsts[a]
        return ref[rows, start : start + 256]

    def attend(g, carry):
        rows = pl.ds(pl.multiple_of(g * 128, 128), 128)
        same_patch = (iota((128, 128), 0) % 8) == (iota((128, 128), 1) % 8)
        for a in range(LOCAL):
            mine = own_lanes(a)
            q = stack(*split(jnp.where(mine, window(qkv, rows, 0, a), 0.0) * scaling))
            k = stack(*split(window(qkv, rows, 1, a)))
            v = stack(*split(window(qkv, rows, 2, a)))
            scores = jnp.where(same_patch, all_nt(q, k), -1e30)
            expo = jnp.exp(scores - jnp.max(scores, axis=1, keepdims=True))
            attn = expo / jnp.sum(expo, axis=1, keepdims=True)
            probs[g, a] = attn
            pltpu.store(
                mixed.at[:, firsts[a] : firsts[a] + 256], all_nn(stack(*split(attn)), v), mask=mine
            )
        high, low = split(mixed[...].T)
        mth[:, rows] = high
        mtl[:, rows] = low
        return carry

    lax.fori_loop(0, 4, attend, 0)

    for h in range(2):
        for d in range(8):
            forwarded(gl, gfs_sem, gfr_sem, d, h).wait_recv()

    def regroup(g, carry):
        rows = pl.ds(pl.multiple_of(g * 128, 128), 128)
        value = gl[g].reshape(128, D)
        high, low = split(value)
        gqh[rows, 0:D] = high
        gql[rows, 0:D] = low
        lane = iota((128, 128), 1)
        rest = value[:, 128:256]
        for j in range(8):
            tile = 144 * j // 128
            offset = 144 * j % 128
            if offset:
                piece = value[:, 128 * tile : 128 * tile + 256]
                piece = pltpu.roll(piece, 256 - offset, 1)[:, 0:128]
            else:
                piece = value[:, 128 * tile : 128 * tile + 128]
            high, low = split(piece)
            gph[rows, 128 * j : 128 * j + 128] = high
            gpl[rows, 128 * j : 128 * j + 128] = low
            if j:
                rest = jnp.where(lane // 16 == j, value[:, 128 * (j + 1) : 128 * (j + 2)], rest)
        high, low = split(rest)
        gph[rows, 1024:1152] = high
        gpl[rows, 1024:1152] = low
        return carry

    lax.fori_loop(0, 4, regroup, 0)

    def out_tile(first, width):
        to = pl.ds(first, width)
        term = dot3(mth[...], mtl[...], gph[:, to], gpl[:, to], NN)
        outw[:, :, :, to] = term[0:576].reshape(4, 2, 72, width)

    def out_step(n, carry):
        out_tile(pl.multiple_of(n * 256, 256), 256)
        return carry

    lax.fori_loop(0, 4, out_step, 0)
    out_tile(1024, 128)

    def targets(part, dx, dy):
        first, second, third = gw[part]
        return (first.at[dx, dy], second.at[dy, :, dx], third.at[:, dx, dy])

    def out_copies(j):
        columns = pl.ds(pl.multiple_of(j * 128, 128), 128)
        copies = []
        for dx_high in range(2):
            for t, target in enumerate(targets(0, 2 * dx_high + j % 2, j // 2)):
                copies.append(
                    pltpu.make_async_copy(
                        outw.at[:, dx_high, pl.ds(24 * t, 24), columns], target, out_sem.at[j, 3 * dx_high + t]
                    )
                )
        return copies

    def out_start(j, carry):
        for copy in out_copies(j):
            copy.start()
        return carry

    def out_wait(j, carry):
        for copy in out_copies(j):
            copy.wait()
        return carry

    lax.fori_loop(0, 8, out_start, 0)

    for first, width in ((0, 256), (256, 256), (512, 128)):
        gm[:, first : first + width] = dot3(
            gqh[:, 0:D], gql[:, 0:D], woh[first : first + width, :], wol[first : first + width, :], NT
        )

    lax.fori_loop(0, 8, out_wait, 0)
    open_stage(out_shares, 0)
    for share in out_shares:
        for copy in share.loads():
            copy.start()
    for share in out_shares:
        for copy in share.loads():
            copy.wait()

    def attend_back(g, carry):
        rows = pl.ds(pl.multiple_of(g * 128, 128), 128)

        def put(part, a, value):
            start = PART * part + firsts[a]
            pltpu.store(gqkv.at[:, start : start + 256], value, mask=own_lanes(a))

        for a in range(LOCAL):
            mine = own_lanes(a)
            q = stack(*split(jnp.where(mine, window(qkv, rows, 0, a), 0.0) * scaling))
            k = stack(*split(window(qkv, rows, 1, a)))
            v = stack(*split(window(qkv, rows, 2, a)))
            m = stack(*split(jnp.where(mine, gm[rows, firsts[a] : firsts[a] + 256], 0.0)))
            attn = probs[g, a]
            grad_attn = all_nt(m, v)
            grad_scores = attn * (grad_attn - jnp.sum(grad_attn * attn, axis=1, keepdims=True))
            put(0, a, all_nn(stack(*split(grad_scores)), k) * scaling)
            put(1, a, all_nn(stack(*split(grad_scores.T)), q))
            put(2, a, all_nn(stack(*split(attn.T)), m))

        high, low = split(gqkv[...])
        gqh[rows, :] = high
        gql[rows, :] = low
        lane = iota((128, 256), 1)
        for j in range(8):
            starts = [PART * ((3 * j + k) // 8) + HEAD_DIM * ((3 * j + k) % 8) for k in range(3)]
            base = starts[0] // 128 * 128
            end = -(-(starts[2] + HEAD_DIM) // 128) * 128
            span = gqkv[:, base:end]
            value = jnp.zeros((128, 256), F32)
            done = {}
            for k in range(3):
                shift = (starts[k] - base - HEAD_DIM * k) % (end - base)
                if shift not in done:
                    moved = span if shift == 0 else pltpu.roll(span, end - base - shift, 1)
                    done[shift] = moved[:, 0:256]
                value = jnp.where((lane >= HEAD_DIM * k) & (lane < HEAD_DIM * k + HEAD_DIM), done[shift], value)
            high, low = split(value)
            big_h[rows, 256 * j : 256 * j + 256] = high
            big_l[rows, 256 * j : 256 * j + 256] = low
        return carry

    lax.fori_loop(0, 2, attend_back, 0)
    middle(out_shares, 0)
    lax.fori_loop(2, 4, attend_back, 0)
    close(out_shares, 0)

    def gw_copies(which, j, slot):
        copies = []
        for dx_high in range(2):
            for t, target in enumerate(targets(1 + which, 2 * dx_high + j % 2, j // 2)):
                copies.append(
                    pltpu.make_async_copy(
                        stage_refs[which][t].at[slot, dx_high], target, gw_sem.at[which, slot, 3 * dx_high + t]
                    )
                )
        return copies

    def gw_part(which):
        high_ref, low_ref = ((xth1, xtl1), (xth2, xtl2))[which]
        size = CUTS[which][1]

        def gw_step(j, carry):
            slot = j % 2

            @pl.when(j >= 2)
            def _():
                for copy in gw_copies(which, j - 2, slot):
                    copy.wait()

            to = pl.ds(pl.multiple_of(j * 256, 256), 256)
            term = dot3(high_ref[...], low_ref[...], big_h[:, to], big_l[:, to], NN)
            inside = iota((8, 128), 1)
            inside = (inside >= 88) & (inside < 104)
            for i in range(8):
                dz, dx_high = i // 2, i % 2
                if which == 1:
                    rest = pltpu.roll(outw[dz, dx_high, :, 1024:1152], (88 + 128 - 16 * j) % 128, 1)
                top = 0
                for t in range(3):
                    for r in range(0, PARTS[1 + which][t], 8):
                        row = top + r
                        if row < size:
                            value = term[size * i + row : size * i + row + 8, 0:128]
                        else:
                            row = row - size
                            value = term[size * i + row : size * i + row + 8, 128:256]
                            if which == 1 and row < HEAD_DIM:
                                value = jnp.where(inside, rest[row : row + 8], value)
                        stage_refs[which][t][slot, dx_high, dz, r : r + 8, :] = value
                    top += PARTS[1 + which][t]
            for copy in gw_copies(which, j, slot):
                copy.start()
            return carry

        lax.fori_loop(0, 8, gw_step, 0)
        for j in (6, 7):
            for copy in gw_copies(which, j, j % 2):
                copy.wait()

    gw_part(0)
    open_stage(first_shares, 0)
    for share in first_shares:
        for copy in share.loads():
            copy.start()
    gw_part(1)
    for share in first_shares:
        for copy in share.loads():
            copy.wait()
    middle(first_shares, 0)
    open_stage(second_shares, 0)
    for share in second_shares:
        for copy in share.loads():
            copy.start()

    def gi_cross(p):
        return pltpu.make_async_remote_copy(
            src_ref=gl.at[:, 2 * p + 1 - core],
            dst_ref=xl.at[:, 2 * p + 1 - core],
            send_sem=gx_send.at[p],
            recv_sem=gx_recv.at[p],
            device_id=sibling,
            device_id_type=MESH,
        )

    def gi_crossed(p):
        return same_place(xl.at[:, 2 * p + core], gx_send, gx_recv, p, sibling)

    def gi_back(d):
        return pltpu.make_async_remote_copy(
            src_ref=gl.at[:, 2 * ((chip + d) % 8) + core],
            dst_ref=input_out.at[chip],
            send_sem=ga_send.at[d],
            recv_sem=ga_recv.at[d],
            device_id=peer(d),
            device_id_type=MESH,
        )

    def gi_arrival(d):
        return same_place(input_out.at[(chip + 8 - d) % 8], ga_send, ga_recv, d, peer(d))

    for h in range(2):
        for d in range(1, 8):
            send(x_hbm, xl, xs_sem, xr_sem, d, h).wait_send()
            send(gsrc, gl, gs_sem, gr_sem, d, h).wait_send()
        for d in range(8):
            forward(gl, gfs_sem, gfr_sem, d, h).wait_send()

    def input_tile(first, width):
        to = pl.ds(first, width)
        term = dot3(gqh[...], gql[...], wph[to, :], wpl[to, :], NT)
        gl[:, :, :, to] = term.reshape(4, 16, 8, width)

    def input_step(n, carry):
        input_tile(pl.multiple_of(n * 256, 256), 256)
        return carry

    lax.fori_loop(0, 4, input_step, 0)
    input_tile(1024, 128)
    for p in range(8):
        gi_cross(p).start()
    close(first_shares, 0)
    early = out_shares + first_shares
    open_stage(early, 1)
    for share in second_shares:
        for copy in share.loads():
            copy.wait()
    middle(second_shares, 0)
    for d in range(8):
        p = (chip + d) % 8
        gi_crossed(p).wait_recv()
        mine = 2 * p + core
        gl[:, mine] = gl[:, mine] + xl[:, mine]
    own_input = pltpu.make_async_copy(gl.at[:, own_frame], input_out.at[chip], fin_sem.at[0])
    own_input.start()

    def return_input(*ds):
        for d in ds:
            gi_back(d).start()

    return_input(1, 2)
    middle(early, 1)
    return_input(3)
    close(second_shares, 0)
    open_stage(second_shares, 1)
    close(early, 1)
    open_stage(early, 2)
    return_input(4)
    middle(second_shares, 1)
    return_input(5, 6, 7)
    close(second_shares, 1)
    open_stage(second_shares, 2)
    close(early, 2)

    def swap(start, size, sem):
        return pltpu.make_async_remote_copy(
            src_ref=last.at[pl.ds(start, size)], dst_ref=other.at[pl.ds(start, size)],
            send_sem=fin_sem.at[sem], recv_sem=fin_sem.at[sem + 1],
            device_id=sibling, device_id_type=MESH,
        )

    swaps = (swap(0, TOPS[2], 1), swap(TOPS[2], SHARE - TOPS[2], 3))
    swaps[0].start()
    close(second_shares, 2)
    swaps[1].start()
    swaps[0].wait_recv()

    even = core == 0

    def qkv_rows(which):
        first, size = CUTS[which]
        top = TOPS[1 + which]

        def both(ref):
            return jnp.concatenate([ref[top : top + size], ref[top + size : top + 2 * size]], axis=1)

        def turn(value):
            return jnp.where(even, pltpu.roll(value, HEAD_DIM, 1), pltpu.roll(value, 256 - HEAD_DIM, 1))

        mine, yours = both(last), both(other)
        lane = iota((size, 256), 1)
        turned = turn(mine)
        left = jnp.where(even, mine, turned)
        right = jnp.where(even, turned, mine)
        whole = jnp.where(lane < HEAD_DIM, left, jnp.where(lane < 2 * HEAD_DIM, turn(yours), right))
        qkv_out[first : first + size, :] = whole[:, 0:216]

    qkv_rows(0)
    swaps[1].wait_recv()
    qkv_rows(1)

    def out_rows(ref):
        lane = iota((72, 128), 1)
        main = ref[0:72]
        rest = pltpu.roll(ref[TOPS[2] + 80 : TOPS[2] + 152], 128 - 32, 1)
        return jnp.where(even, main, jnp.where(lane < 56, pltpu.roll(main, 128 - HEAD_DIM, 1), rest))

    a = out_rows(last)
    b = out_rows(other)
    out_out[0:72, :] = jnp.where(even, a, b)[:, 0:HEAD_DIM]
    out_out[72:144, :] = jnp.where(even, b, a)[:, 0:HEAD_DIM]

    for d in range(1, 8):
        gi_arrival(d).wait_recv()
        gi_back(d).wait_send()
    for p in range(8):
        gi_cross(p).wait_send()
    for share in shares:
        share.finish()
    for copy in swaps:
        copy.wait_send()
    own_input.wait()


def on_device(x_saved, grad_out, keep_mask, w_qkv, w_out):
    any_space = pl.BlockSpec(memory_space=pl.ANY)
    in_vmem = pl.BlockSpec(memory_space=pltpu.VMEM)
    dma = pltpu.SemaphoreType.DMA
    shape = jax.ShapeDtypeStruct
    vmem = pltpu.VMEM
    heaps = [shape((4, 4, 4, rows, 128), F32) for part in PARTS for rows in part]
    scratch = [
        vmem((4, 16, 8, D), F32),
        vmem((4, 16, 8, D), F32),
        vmem((8, 4, 8, D), F32),
        vmem((5, 512, 128), BF16),
        vmem((D, 3 * PART), BF16),
        vmem((D, 3 * PART), BF16),
        vmem((PART, D), BF16),
        vmem((PART, D), BF16),
        vmem((512, 512), BF16),
        vmem((512, 512), BF16),
        vmem((640, 512), BF16),
        vmem((640, 512), BF16),
        vmem((512, 3 * PART), F32),
        vmem((128, 3 * PART), F32),
        vmem((512, PART), F32),
        vmem((128, PART), F32),
        vmem((4, LOCAL, 128, 128), F32),
        vmem((PART, 512), BF16),
        vmem((PART, 512), BF16),
        vmem((512, D), BF16),
        vmem((512, D), BF16),
        vmem((512, 2048), BF16),
        vmem((512, 2048), BF16),
        vmem((512, 3 * PART), BF16),
        vmem((512, 3 * PART), BF16),
        vmem((4, 2, 72, D), F32),
        vmem((SHARE, 128), F32),
        vmem((SHARE, 128), F32),
        dma((2, 8)), dma((2, 8)), dma((2, 8)), dma((2, 8)),
        dma((2, 8)), dma((2, 8)), dma((2, 8)), dma((2, 8)),
        dma((3,)), dma((10,)), dma((2, 2, 6)), dma((8, 6)),
        dma((9, 3, 6)), dma((9, 3, 6)), dma((9, 3)),
        dma((8,)), dma((8,)), dma((8,)), dma((8,)), dma((5,)),
    ]
    for part in (1, 2):
        scratch += [vmem((2, 2, 4, rows, 128), F32) for rows in PARTS[part]]
    scratch += [vmem((2, 2, 4, max(part[t] for part in PARTS), 128), F32) for t in range(3)]
    for part in PARTS:
        for rows in part:
            scratch += scratch_of(rows)
    outputs = pl.pallas_call(
        kernel,
        out_shape=[shape((8, 4, 8, D), F32), shape((144, 216), F32), shape((144, 72), F32)] + heaps,
        in_specs=[any_space, any_space, in_vmem, any_space, any_space],
        out_specs=[any_space, in_vmem, in_vmem] + [any_space] * 9,
        scratch_shapes=scratch,
        compiler_params=pltpu.CompilerParams(
            collective_id=0, has_side_effects=True, vmem_limit_bytes=64 * 2**20
        ),
        cost_estimate=pl.CostEstimate(flops=23 * 10**9, bytes_accessed=60 * 10**6, transcendentals=10**6),
    )(
        x_saved.reshape(8, 4, 8, D),
        grad_out.reshape(8, 4, 8, D),
        keep_mask.reshape(1, 256),
        w_qkv,
        w_out,
    )
    return (outputs[0].reshape(1, 1, 256, D), outputs[1], outputs[2])


def solution(mesh):
    return jax.shard_map(
        on_device,
        mesh=mesh,
        in_specs=(
            P("clip", "seq", None, None),
            P("clip", "seq", None, None),
            P("clip", "seq", None),
            P(),
            P(),
        ),
        out_specs=(P("clip", "seq", None, None), P("clip", "seq"), P("clip", "seq")),
        check_vma=False,
    )
```

```python
import jax
import jax.numpy as jnp
from jax import lax
from jax.experimental import pallas as pl
from jax.experimental.pallas import tpu as pltpu
from jax.sharding import PartitionSpec as P

HEADS = 16
HEAD_DIM = 72
KEEP_RATE = 0.9
D = 1152
LOCAL = 8
PART = 640
PARTS = ((24, 24, 24), (32, 40, 56), (48, 40, 72))
TOPS = (0, 72, 200)
SHARE = 360
CUTS = ((0, 64), (64, 80))
ORDERS = ((0, 1, 2), (1, 2, 0), (2, 0, 1))
MESH = pl.DeviceIdType.MESH
F32 = jnp.float32
BF16 = jnp.bfloat16

NN = (((1,), (0,)), ((), ()))
NT = (((1,), (1,)), ((), ()))


def split(value):
    high = value.astype(BF16)
    return high, (value - high.astype(F32)).astype(BF16)


def dot(left, right, dims):
    return lax.dot_general(left, right, dims, preferred_element_type=F32)


def dot3(left_high, left_low, right_high, right_low, dims):
    return (
        dot(left_high, right_high, dims)
        + dot(left_low, right_high, dims)
        + dot(left_high, right_low, dims)
    )


def iota(shape, dim):
    return lax.broadcasted_iota(jnp.int32, shape, dim)


def wait_copy(ref, sem):
    pltpu.make_async_copy(ref, ref, sem).wait()


class Share:
    def __init__(self, index, part, t, rows, here, at, gw, load, scratch, sems, last):
        self.index, self.t, self.rows = index, t, rows
        self.here, self.at = here, at
        self.gw, self.load = gw, load
        one1, two1, own1, one2, two2, own2, three = scratch
        self.ones, self.twos, self.three = (one1, one2), (two1, two2), three
        self.sources = (gw, own1, own2)
        self.send_sem, self.recv_sem, self.load_sem = sems
        top = TOPS[part] + sum(PARTS[part][:t])
        self.last = last.at[pl.ds(top, rows)]
        self.halves = (((0, 2), (2, 2)), ((0, 2), (2, 2)))

    def along(self, stage, step):
        axis = ORDERS[self.t][stage]
        place = list(self.here)
        place[axis] = (place[axis] + step + 4) % 4
        return self.at(*place)

    def spots(self, stage):
        me = self.here[ORDERS[self.t][stage]]
        return me, (me + 1) % 4, (me + 3) % 4, (me + 2) % 4

    def source(self, stage, spot, half):
        start, size = self.halves[stage][half]
        return self.sources[stage].at[spot, pl.ds(start, size)]

    def first_hop(self, stage, half):
        far = self.spots(stage)[3]
        size = self.halves[stage][half][1]
        return pltpu.make_async_remote_copy(
            src_ref=self.source(stage, far, half),
            dst_ref=self.ones[stage].at[half, pl.ds(0, size)],
            send_sem=self.send_sem.at[self.index, stage, half],
            recv_sem=self.recv_sem.at[self.index, stage, half],
            device_id=self.along(stage, 1 if half == 0 else -1),
            device_id_type=MESH,
        )

    def second_hop(self, stage, way, half):
        me, up, down, far = self.spots(stage)
        start, size = self.halves[stage][half]
        if half == way:
            src = self.ones[stage].at[half, pl.ds(0, size)]
        else:
            src = self.source(stage, up if way == 0 else down, half)
        slot = 2 + 2 * way + half
        return pltpu.make_async_remote_copy(
            src_ref=src,
            dst_ref=self.twos[stage].at[way, pl.ds(start, size)],
            send_sem=self.send_sem.at[self.index, stage, slot],
            recv_sem=self.recv_sem.at[self.index, stage, slot],
            device_id=self.along(stage, 1 if way == 0 else -1),
            device_id_type=MESH,
        )

    def direct(self, way):
        step = (1, -1, 2)[way]
        return pltpu.make_async_remote_copy(
            src_ref=self.sources[2].at[(self.spots(2)[0] + step + 4) % 4],
            dst_ref=self.three.at[way],
            send_sem=self.send_sem.at[self.index, 2, way],
            recv_sem=self.recv_sem.at[self.index, 2, way],
            device_id=self.along(2, step),
            device_id_type=MESH,
        )

    def loads(self):
        me, up, down, far = self.spots(0)
        copy = pltpu.make_async_copy
        return (
            copy(self.source(0, up, 0), self.load.at[0], self.load_sem.at[self.index, 0]),
            copy(self.source(0, down, 1), self.load.at[1], self.load_sem.at[self.index, 1]),
            copy(self.gw.at[me], self.sources[1], self.load_sem.at[self.index, 2]),
        )

    def middle(self, stage):
        me, up, down, far = self.spots(stage)
        for way in range(2):
            self.first_hop(stage, way).wait_recv()
            size = self.halves[stage][way][1]
            to = self.ones[stage].at[way, pl.ds(0, size)]
            if stage == 0:
                to[...] = to[...] + self.load[way]
            else:
                to[...] = to[...] + self.source(stage, up if way == 0 else down, way)[...]
            self.second_hop(stage, way, way).start()

    def close(self, stage):
        me = self.spots(stage)[0]
        if stage == 2:
            for way in range(3):
                self.direct(way).wait_recv()
            self.last[...] = self.sources[2][me] + self.three[0] + self.three[1] + self.three[2]
            return
        for way in range(2):
            for half in range(2):
                self.second_hop(stage, way, half).wait_recv()
        two = self.twos[stage]
        if stage == 0:
            own = self.sources[1]
            own[...] = own[...] + two[0] + two[1]
        else:
            own = self.sources[2]
            own[...] = self.sources[1][me] + two[0] + two[1]

    def finish(self):
        for stage in range(2):
            for half in range(2):
                self.first_hop(stage, half).wait_send()
                for way in range(2):
                    self.second_hop(stage, way, half).wait_send()
        for way in range(3):
            self.direct(way).wait_send()


def open_stage(shares, stage):
    if stage == 2:
        for way in (2, 0, 1):
            for share in shares:
                share.direct(way).start()
        return
    for half in range(2):
        for share in shares:
            share.first_hop(stage, half).start()
    for way in range(2):
        for share in shares:
            share.second_hop(stage, way, 1 - way).start()


def middle(shares, stage):
    for share in shares:
        share.middle(stage)


def close(shares, stage):
    for share in shares:
        share.close(stage)


def scratch_of(rows):
    vmem = pltpu.VMEM
    return [
        vmem((2, 2, 4, rows, 128), F32),
        vmem((2, 4, 4, rows, 128), F32),
        vmem((4, 4, rows, 128), F32),
        vmem((2, 2, rows, 128), F32),
        vmem((2, 4, rows, 128), F32),
        vmem((4, rows, 128), F32),
        vmem((3, rows, 128), F32),
    ]


def stack(high, low):
    return jnp.concatenate([high, low], axis=0)


def all_nt(left, right):
    rows = left.shape[0] // 2
    columns = right.shape[0] // 2
    full = dot(left, right, NT)
    return (full[:rows, :columns] + full[:rows, columns:]) + (full[rows:, :columns] + full[rows:, columns:])


def all_nn(left, right):
    rows = left.shape[0] // 2
    full = dot(jnp.concatenate([left, left], axis=1), right, NN)
    return full[:rows] + full[rows:]


def kernel(*refs):
    x_hbm, g_hbm, mask_ref, wqkv_hbm, wout_hbm = refs[0:5]
    input_out, qkv_out, out_out = refs[5:8]
    gw = [refs[8 + 3 * part : 11 + 3 * part] for part in range(3)]
    (
        xl, gl, gsrc, sel, wph, wpl, woh, wol, xth1, xtl1, xth2, xtl2, qkv, gqkv, gm, mixed, probs, mth, mtl,
        gph, gpl, big_h, big_l, gqh, gql, outw, last, other,
        xs_sem, xr_sem, xfs_sem, xfr_sem, gs_sem, gr_sem, gfs_sem, gfr_sem, loc_sem, w_sem, gw_sem, out_sem,
        rs_send, rs_recv, ld_sem, gx_send, gx_recv, ga_send, ga_recv, fin_sem,
    ) = refs[17:65]
    rest = refs[65:]
    stage_refs = [rest[0:3], rest[3:6]]
    load_refs = rest[6:9]
    rest = rest[9:]

    clip = lax.axis_index("clip")
    seq = lax.axis_index("seq")
    chip = seq // 2
    core = seq % 2
    sibling = (clip, 2 * chip + 1 - core)
    here = (2 * (clip % 2) + chip % 2, chip // 2, clip // 2)

    def at(x, y, z):
        return (2 * z + x // 2, 4 * y + 2 * (x % 2) + core)

    shares = []
    for part in range(3):
        for t in range(3):
            index = 3 * part + t
            rows = PARTS[part][t]
            load = load_refs[t].at[:, :, :, pl.ds(0, rows)]
            shares.append(
                Share(index, part, t, rows, here, at, gw[part][t], load,
                      rest[7 * index : 7 * index + 7], (rs_send, rs_recv, ld_sem), last)
            )
    out_shares, first_shares, second_shares = shares[0:3], shares[3:6], shares[6:9]

    def peer(d):
        return (clip, 2 * ((chip + d) % 8) + core)

    def frame_from(d, c):
        return 2 * ((chip + 8 - d) % 8) + c

    barrier = pltpu.get_barrier_semaphore()
    for d in range(1, 8):
        pl.semaphore_signal(barrier, inc=1, device_id=peer(d), device_id_type=MESH)
    pl.semaphore_signal(barrier, inc=1, device_id=sibling, device_id_type=MESH)
    for t in range(3):
        for step in (1, -1, 2):
            pl.semaphore_signal(
                barrier, inc=1, device_id=out_shares[t].along(0, step), device_id_type=MESH
            )

    own_frame = 2 * chip + core
    load_x = pltpu.make_async_copy(x_hbm.at[chip], xl.at[:, own_frame], loc_sem.at[0])
    load_x.start()
    load_g = pltpu.make_async_copy(g_hbm, gsrc, loc_sem.at[1])
    load_g.start()

    def weight_copy(step):
        rows = pl.ds(pl.multiple_of((step % 9) * 128, 8), 128)
        columns = pl.ds(pl.multiple_of((step // 9) * D, 128), D)
        slot = step % 4
        to = pl.ds(pl.multiple_of(slot * 128, 8), 128)
        return pltpu.make_async_copy(wqkv_hbm.at[rows, columns], qkv.at[to, pl.ds(0, D)], w_sem.at[slot])

    for step in range(3):
        weight_copy(step).start()
    pl.semaphore_wait(barrier, 17)

    def send(src, dst, send_sems, recv_sems, d, h):
        p = (chip + d) % 8
        return pltpu.make_async_remote_copy(
            src_ref=src.at[p, pl.ds(2 * h, 2)],
            dst_ref=dst.at[pl.ds(2 * h, 2), own_frame],
            send_sem=send_sems.at[h, d],
            recv_sem=recv_sems.at[h, d],
            device_id=peer(d),
            device_id_type=MESH,
        )

    def same_place(view, send_sems, recv_sems, d, device):
        return pltpu.make_async_remote_copy(
            src_ref=view, dst_ref=view, send_sem=send_sems.at[d], recv_sem=recv_sems.at[d],
            device_id=device, device_id_type=MESH,
        )

    def arrival(dst, send_sems, recv_sems, d, h):
        view = dst.at[pl.ds(2 * h, 2), frame_from(d, core)]
        return same_place(view, send_sems.at[h], recv_sems.at[h], d, peer(d))

    def forward(dst, send_sems, recv_sems, d, h):
        view = dst.at[pl.ds(2 * h, 2), frame_from(d, core)]
        return same_place(view, send_sems.at[h], recv_sems.at[h], d, sibling)

    def forwarded(dst, send_sems, recv_sems, d, h):
        view = dst.at[pl.ds(2 * h, 2), frame_from(d, 1 - core)]
        return same_place(view, send_sems.at[h], recv_sems.at[h], d, sibling)

    for h in range(2):
        for d in range(1, 8):
            send(x_hbm, xl, xs_sem, xr_sem, d, h).start()

    load_g.wait()
    same = iota((256, 256), 0) == iota((256, 256), 1)
    keep = mask_ref[...].astype(F32)
    column = jnp.sum(jnp.where(same, keep, 0.0), axis=1, keepdims=True) / KEEP_RATE
    column = column.reshape(8, 4, 8, 1)
    for p in range(8):
        gsrc[p] = gsrc[p] * column[p]
    own_g = pltpu.make_async_copy(gsrc.at[chip], gl.at[:, own_frame], loc_sem.at[2])
    own_g.start()
    for h in range(2):
        for d in range(1, 8):
            send(gsrc, gl, gs_sem, gr_sem, d, h).start()

    bases = (0, 128, 384, 640, 640)
    for n in range(5):
        lane = iota((512, 128), 1) + 128 * n
        head = lane // HEAD_DIM
        source = lane + HEAD_DIM * (head + core) - bases[n]
        hit = (iota((512, 128), 0) == source) & (lane < LOCAL * HEAD_DIM)
        sel[n] = jnp.where(hit, 1.0, 0.0).astype(BF16)

    load_x.wait()
    for h in range(2):
        forward(xl, xfs_sem, xfr_sem, 0, h).start()

    def head_copy(a):
        return pltpu.make_async_copy(
            wout_hbm.at[pl.ds(HEAD_DIM * (2 * a + core), HEAD_DIM)],
            outw.at[a // 2, a % 2],
            w_sem.at[4 + a],
        )

    for a in range(LOCAL):
        head_copy(a).start()

    def prepare(step, carry):
        @pl.when(step < 24)
        def _():
            weight_copy(step + 3).start()

        weight_copy(step).wait()
        rows = pl.ds(pl.multiple_of((step % 9) * 128, 16), 128)
        staged = pl.ds(pl.multiple_of((step % 4) * 128, 8), 128)
        part = step // 9
        for n in range(5):
            both = stack(*split(qkv[staged, bases[n] : bases[n] + 512]))
            both = dot(both, sel[n], NN).astype(BF16)
            to = pl.ds(pl.multiple_of(PART * part + 128 * n, 128), 128)
            wph[rows, to] = both[0:128]
            wpl[rows, to] = both[128:256]
        return carry

    lax.fori_loop(0, 27, prepare, 0)

    def pass_on(dst, sems, h):
        for d in range(1, 8):
            arrival(dst, sems[0], sems[1], d, h).wait_recv()
            forward(dst, sems[2], sems[3], d, h).start()

    x_sems = (xs_sem, xr_sem, xfs_sem, xfr_sem)
    g_sems = (gs_sem, gr_sem, gfs_sem, gfr_sem)
    pass_on(xl, x_sems, 0)

    for a in range(LOCAL):
        head_copy(a).wait()
    for n in range(4):
        high, low = split(outw[n].reshape(144, D))
        woh[144 * n : 144 * n + 144, :] = high
        wol[144 * n : 144 * n + 144, :] = low
    woh[576:640, :] = jnp.zeros((64, D), BF16)
    wol[576:640, :] = jnp.zeros((64, D), BF16)
    for part in range(3):
        gqkv[:, PART * part + 512 : PART * part + 640] = jnp.zeros((128, 128), F32)
    mixed[:, 512:640] = jnp.zeros((128, 128), F32)

    own_g.wait()
    for h in range(2):
        forward(gl, gfs_sem, gfr_sem, 0, h).start()
    for d in range(8):
        forwarded(xl, xfs_sem, xfr_sem, d, 0).wait_recv()

    def split_x(g, carry):
        rows = pl.ds(pl.multiple_of(g * 128, 128), 128)
        value = xl[g].reshape(128, D)
        high, low = split(value)
        big_h[rows, 0:D] = high
        big_l[rows, 0:D] = low
        high, low = split(value.T)
        for i in range(8):
            xth1[64 * i : 64 * i + 64, rows] = high[144 * i : 144 * i + 64]
            xtl1[64 * i : 64 * i + 64, rows] = low[144 * i : 144 * i + 64]
            xth2[80 * i : 80 * i + 80, rows] = high[144 * i + 64 : 144 * i + 144]
            xtl2[80 * i : 80 * i + 80, rows] = low[144 * i + 64 : 144 * i + 144]
        return carry

    def project(h, first, width):
        to = pl.ds(first, width)
        rows = pl.ds(256 * h, 256)
        qkv[rows, to] = dot3(
            big_h[rows, 0:D], big_l[rows, 0:D], wph[:, to], wpl[:, to], NN
        )

    def project_half(h):
        def project_tile(n, carry):
            project(h, pl.multiple_of(n * 256, 256), 256)
            return carry

        lax.fori_loop(0, 7, project_tile, 0)
        project(h, 1792, 128)

    lax.fori_loop(0, 2, split_x, 0)
    pass_on(xl, x_sems, 1)
    project_half(0)
    for d in range(8):
        forwarded(xl, xfs_sem, xfr_sem, d, 1).wait_recv()
    lax.fori_loop(2, 4, split_x, 0)
    project_half(1)
    for h in range(2):
        for d in range(8):
            forward(xl, xfs_sem, xfr_sem, d, h).wait_send()
    pass_on(gl, g_sems, 0)
    pass_on(gl, g_sems, 1)

    scaling = HEAD_DIM ** (-0.5)
    firsts = [min(HEAD_DIM * a // 128 * 128, 384) for a in range(LOCAL)]

    def own_lanes(a):
        lane = iota((128, 256), 1)
        low_lane = HEAD_DIM * a - firsts[a]
        return (lane >= low_lane) & (lane < low_lane + HEAD_DIM)

    def window(ref, rows, part, a):
        start = PART * part + firsts[a]
        return ref[rows, start : start + 256]

    def attend(g, carry):
        rows = pl.ds(pl.multiple_of(g * 128, 128), 128)
        same_patch = (iota((128, 128), 0) % 8) == (iota((128, 128), 1) % 8)
        for a in range(LOCAL):
            mine = own_lanes(a)
            q = stack(*split(jnp.where(mine, window(qkv, rows, 0, a), 0.0) * scaling))
            k = stack(*split(window(qkv, rows, 1, a)))
            v = stack(*split(window(qkv, rows, 2, a)))
            scores = jnp.where(same_patch, all_nt(q, k), -1e30)
            expo = jnp.exp(scores - jnp.max(scores, axis=1, keepdims=True))
            attn = expo / jnp.sum(expo, axis=1, keepdims=True)
            probs[g, a] = attn
            pltpu.store(
                mixed.at[:, firsts[a] : firsts[a] + 256], all_nn(stack(*split(attn)), v), mask=mine
            )
        high, low = split(mixed[...].T)
        mth[:, rows] = high
        mtl[:, rows] = low
        return carry

    lax.fori_loop(0, 4, attend, 0)

    for h in range(2):
        for d in range(8):
            forwarded(gl, gfs_sem, gfr_sem, d, h).wait_recv()

    def regroup(g, carry):
        rows = pl.ds(pl.multiple_of(g * 128, 128), 128)
        value = gl[g].reshape(128, D)
        high, low = split(value)
        gqh[rows, 0:D] = high
        gql[rows, 0:D] = low
        lane = iota((128, 128), 1)
        rest = value[:, 128:256]
        for j in range(8):
            tile = 144 * j // 128
            offset = 144 * j % 128
            if offset:
                piece = value[:, 128 * tile : 128 * tile + 256]
                piece = pltpu.roll(piece, 256 - offset, 1)[:, 0:128]
            else:
                piece = value[:, 128 * tile : 128 * tile + 128]
            high, low = split(piece)
            gph[rows, 128 * j : 128 * j + 128] = high
            gpl[rows, 128 * j : 128 * j + 128] = low
            if j:
                rest = jnp.where(lane // 16 == j, value[:, 128 * (j + 1) : 128 * (j + 2)], rest)
        high, low = split(rest)
        gph[rows, 1024:1152] = high
        gpl[rows, 1024:1152] = low
        return carry

    lax.fori_loop(0, 4, regroup, 0)

    def out_tile(first, width):
        to = pl.ds(first, width)
        term = dot3(mth[...], mtl[...], gph[:, to], gpl[:, to], NN)
        outw[:, :, :, to] = term[0:576].reshape(4, 2, 72, width)

    def out_step(n, carry):
        out_tile(pl.multiple_of(n * 256, 256), 256)
        return carry

    lax.fori_loop(0, 4, out_step, 0)
    out_tile(1024, 128)

    def targets(part, dx, dy):
        first, second, third = gw[part]
        return (first.at[dx, dy], second.at[dy, :, dx], third.at[:, dx, dy])

    def out_copies(j):
        columns = pl.ds(pl.multiple_of(j * 128, 128), 128)
        copies = []
        for dx_high in range(2):
            for t, target in enumerate(targets(0, 2 * dx_high + j % 2, j // 2)):
                copies.append(
                    pltpu.make_async_copy(
                        outw.at[:, dx_high, pl.ds(24 * t, 24), columns], target, out_sem.at[j, 3 * dx_high + t]
                    )
                )
        return copies

    def out_start(j, carry):
        for copy in out_copies(j):
            copy.start()
        return carry

    def out_wait(j, carry):
        for copy in out_copies(j):
            copy.wait()
        return carry

    lax.fori_loop(0, 8, out_start, 0)

    for first, width in ((0, 256), (256, 256), (512, 128)):
        gm[:, first : first + width] = dot3(
            gqh[:, 0:D], gql[:, 0:D], woh[first : first + width, :], wol[first : first + width, :], NT
        )

    lax.fori_loop(0, 8, out_wait, 0)
    open_stage(out_shares, 0)
    for share in out_shares:
        for copy in share.loads():
            copy.start()
    for share in out_shares:
        for copy in share.loads():
            copy.wait()

    def attend_back(g, carry):
        rows = pl.ds(pl.multiple_of(g * 128, 128), 128)

        def put(part, a, value):
            start = PART * part + firsts[a]
            pltpu.store(gqkv.at[:, start : start + 256], value, mask=own_lanes(a))

        for a in range(LOCAL):
            mine = own_lanes(a)
            q = stack(*split(jnp.where(mine, window(qkv, rows, 0, a), 0.0) * scaling))
            k = stack(*split(window(qkv, rows, 1, a)))
            v = stack(*split(window(qkv, rows, 2, a)))
            m = stack(*split(jnp.where(mine, gm[rows, firsts[a] : firsts[a] + 256], 0.0)))
            attn = probs[g, a]
            grad_attn = all_nt(m, v)
            grad_scores = attn * (grad_attn - jnp.sum(grad_attn * attn, axis=1, keepdims=True))
            put(0, a, all_nn(stack(*split(grad_scores)), k) * scaling)
            put(1, a, all_nn(stack(*split(grad_scores.T)), q))
            put(2, a, all_nn(stack(*split(attn.T)), m))

        high, low = split(gqkv[...])
        gqh[rows, :] = high
        gql[rows, :] = low
        lane = iota((128, 256), 1)
        for j in range(8):
            starts = [PART * ((3 * j + k) // 8) + HEAD_DIM * ((3 * j + k) % 8) for k in range(3)]
            base = starts[0] // 128 * 128
            end = -(-(starts[2] + HEAD_DIM) // 128) * 128
            span = gqkv[:, base:end]
            value = jnp.zeros((128, 256), F32)
            done = {}
            for k in range(3):
                shift = (starts[k] - base - HEAD_DIM * k) % (end - base)
                if shift not in done:
                    moved = span if shift == 0 else pltpu.roll(span, end - base - shift, 1)
                    done[shift] = moved[:, 0:256]
                value = jnp.where((lane >= HEAD_DIM * k) & (lane < HEAD_DIM * k + HEAD_DIM), done[shift], value)
            high, low = split(value)
            big_h[rows, 256 * j : 256 * j + 256] = high
            big_l[rows, 256 * j : 256 * j + 256] = low
        return carry

    lax.fori_loop(0, 2, attend_back, 0)
    middle(out_shares, 0)
    lax.fori_loop(2, 4, attend_back, 0)
    close(out_shares, 0)

    def gw_copies(which, j, slot):
        copies = []
        for dx_high in range(2):
            for t, target in enumerate(targets(1 + which, 2 * dx_high + j % 2, j // 2)):
                copies.append(
                    pltpu.make_async_copy(
                        stage_refs[which][t].at[slot, dx_high], target, gw_sem.at[which, slot, 3 * dx_high + t]
                    )
                )
        return copies

    def gw_part(which):
        high_ref, low_ref = ((xth1, xtl1), (xth2, xtl2))[which]
        size = CUTS[which][1]

        def gw_step(j, carry):
            slot = j % 2

            @pl.when(j >= 2)
            def _():
                for copy in gw_copies(which, j - 2, slot):
                    copy.wait()

            to = pl.ds(pl.multiple_of(j * 256, 256), 256)
            term = dot3(high_ref[...], low_ref[...], big_h[:, to], big_l[:, to], NN)
            inside = iota((8, 128), 1)
            inside = (inside >= 88) & (inside < 104)
            for i in range(8):
                dz, dx_high = i // 2, i % 2
                if which == 1:
                    rest = pltpu.roll(outw[dz, dx_high, :, 1024:1152], (88 + 128 - 16 * j) % 128, 1)
                top = 0
                for t in range(3):
                    for r in range(0, PARTS[1 + which][t], 8):
                        row = top + r
                        if row < size:
                            value = term[size * i + row : size * i + row + 8, 0:128]
                        else:
                            row = row - size
                            value = term[size * i + row : size * i + row + 8, 128:256]
                            if which == 1 and row < HEAD_DIM:
                                value = jnp.where(inside, rest[row : row + 8], value)
                        stage_refs[which][t][slot, dx_high, dz, r : r + 8, :] = value
                    top += PARTS[1 + which][t]
            for copy in gw_copies(which, j, slot):
                copy.start()
            return carry

        lax.fori_loop(0, 8, gw_step, 0)
        for j in (6, 7):
            for copy in gw_copies(which, j, j % 2):
                copy.wait()

    gw_part(0)
    open_stage(first_shares, 0)
    for share in first_shares:
        for copy in share.loads():
            copy.start()
    gw_part(1)
    for share in first_shares:
        for copy in share.loads():
            copy.wait()
    middle(first_shares, 0)
    open_stage(second_shares, 0)
    for share in second_shares:
        for copy in share.loads():
            copy.start()

    def gi_cross(p):
        return pltpu.make_async_remote_copy(
            src_ref=gl.at[:, 2 * p + 1 - core],
            dst_ref=xl.at[:, 2 * p + 1 - core],
            send_sem=gx_send.at[p],
            recv_sem=gx_recv.at[p],
            device_id=sibling,
            device_id_type=MESH,
        )

    def gi_crossed(p):
        return same_place(xl.at[:, 2 * p + core], gx_send, gx_recv, p, sibling)

    def gi_back(d):
        return pltpu.make_async_remote_copy(
            src_ref=gl.at[:, 2 * ((chip + d) % 8) + core],
            dst_ref=input_out.at[chip],
            send_sem=ga_send.at[d],
            recv_sem=ga_recv.at[d],
            device_id=peer(d),
            device_id_type=MESH,
        )

    def gi_arrival(d):
        return same_place(input_out.at[(chip + 8 - d) % 8], ga_send, ga_recv, d, peer(d))

    for h in range(2):
        for d in range(1, 8):
            send(x_hbm, xl, xs_sem, xr_sem, d, h).wait_send()
            send(gsrc, gl, gs_sem, gr_sem, d, h).wait_send()
        for d in range(8):
            forward(gl, gfs_sem, gfr_sem, d, h).wait_send()

    def input_tile(first, width):
        to = pl.ds(first, width)
        term = dot3(gqh[...], gql[...], wph[to, :], wpl[to, :], NT)
        gl[:, :, :, to] = term.reshape(4, 16, 8, width)

    def input_step(n, carry):
        input_tile(pl.multiple_of(n * 256, 256), 256)
        return carry

    lax.fori_loop(0, 4, input_step, 0)
    input_tile(1024, 128)
    for p in range(8):
        gi_cross(p).start()
    close(first_shares, 0)
    early = out_shares + first_shares
    open_stage(early, 1)
    for share in second_shares:
        for copy in share.loads():
            copy.wait()
    middle(second_shares, 0)
    for d in range(8):
        p = (chip + d) % 8
        gi_crossed(p).wait_recv()
        mine = 2 * p + core
        gl[:, mine] = gl[:, mine] + xl[:, mine]
    own_input = pltpu.make_async_copy(gl.at[:, own_frame], input_out.at[chip], fin_sem.at[0])
    own_input.start()

    def return_input(*ds):
        for d in ds:
            gi_back(d).start()

    return_input(1, 2)
    middle(early, 1)
    return_input(3)
    close(second_shares, 0)
    open_stage(second_shares, 1)
    close(early, 1)
    open_stage(early, 2)
    return_input(4)
    middle(second_shares, 1)
    return_input(5, 6, 7)
    close(second_shares, 1)
    open_stage(second_shares, 2)
    close(early, 2)

    def swap(start, size, sem):
        return pltpu.make_async_remote_copy(
            src_ref=last.at[pl.ds(start, size)], dst_ref=other.at[pl.ds(start, size)],
            send_sem=fin_sem.at[sem], recv_sem=fin_sem.at[sem + 1],
            device_id=sibling, device_id_type=MESH,
        )

    swaps = (swap(0, TOPS[2], 1), swap(TOPS[2], SHARE - TOPS[2], 3))
    swaps[0].start()
    close(second_shares, 2)
    swaps[1].start()
    swaps[0].wait_recv()

    even = core == 0

    def qkv_rows(which):
        first, size = CUTS[which]
        top = TOPS[1 + which]

        def both(ref):
            return jnp.concatenate([ref[top : top + size], ref[top + size : top + 2 * size]], axis=1)

        def turn(value):
            return jnp.where(even, pltpu.roll(value, HEAD_DIM, 1), pltpu.roll(value, 256 - HEAD_DIM, 1))

        mine, yours = both(last), both(other)
        lane = iota((size, 256), 1)
        turned = turn(mine)
        left = jnp.where(even, mine, turned)
        right = jnp.where(even, turned, mine)
        whole = jnp.where(lane < HEAD_DIM, left, jnp.where(lane < 2 * HEAD_DIM, turn(yours), right))
        qkv_out[first : first + size, :] = whole[:, 0:216]

    qkv_rows(0)
    swaps[1].wait_recv()
    qkv_rows(1)

    def out_rows(ref):
        lane = iota((72, 128), 1)
        main = ref[0:72]
        rest = pltpu.roll(ref[TOPS[2] + 80 : TOPS[2] + 152], 128 - 32, 1)
        return jnp.where(even, main, jnp.where(lane < 56, pltpu.roll(main, 128 - HEAD_DIM, 1), rest))

    a = out_rows(last)
    b = out_rows(other)
    out_out[0:72, :] = jnp.where(even, a, b)[:, 0:HEAD_DIM]
    out_out[72:144, :] = jnp.where(even, b, a)[:, 0:HEAD_DIM]

    for d in range(1, 8):
        gi_arrival(d).wait_recv()
        gi_back(d).wait_send()
    for p in range(8):
        gi_cross(p).wait_send()
    for share in shares:
        share.finish()
    for copy in swaps:
        copy.wait_send()
    own_input.wait()


def on_device(x_saved, grad_out, keep_mask, w_qkv, w_out):
    any_space = pl.BlockSpec(memory_space=pl.ANY)
    in_vmem = pl.BlockSpec(memory_space=pltpu.VMEM)
    dma = pltpu.SemaphoreType.DMA
    shape = jax.ShapeDtypeStruct
    vmem = pltpu.VMEM
    heaps = [shape((4, 4, 4, rows, 128), F32) for part in PARTS for rows in part]
    scratch = [
        vmem((4, 16, 8, D), F32),
        vmem((4, 16, 8, D), F32),
        vmem((8, 4, 8, D), F32),
        vmem((5, 512, 128), BF16),
        vmem((D, 3 * PART), BF16),
        vmem((D, 3 * PART), BF16),
        vmem((PART, D), BF16),
        vmem((PART, D), BF16),
        vmem((512, 512), BF16),
        vmem((512, 512), BF16),
        vmem((640, 512), BF16),
        vmem((640, 512), BF16),
        vmem((512, 3 * PART), F32),
        vmem((128, 3 * PART), F32),
        vmem((512, PART), F32),
        vmem((128, PART), F32),
        vmem((4, LOCAL, 128, 128), F32),
        vmem((PART, 512), BF16),
        vmem((PART, 512), BF16),
        vmem((512, D), BF16),
        vmem((512, D), BF16),
        vmem((512, 2048), BF16),
        vmem((512, 2048), BF16),
        vmem((512, 3 * PART), BF16),
        vmem((512, 3 * PART), BF16),
        vmem((4, 2, 72, D), F32),
        vmem((SHARE, 128), F32),
        vmem((SHARE, 128), F32),
        dma((2, 8)), dma((2, 8)), dma((2, 8)), dma((2, 8)),
        dma((2, 8)), dma((2, 8)), dma((2, 8)), dma((2, 8)),
        dma((3,)), dma((12,)), dma((2, 2, 6)), dma((8, 6)),
        dma((9, 3, 6)), dma((9, 3, 6)), dma((9, 3)),
        dma((8,)), dma((8,)), dma((8,)), dma((8,)), dma((5,)),
    ]
    for part in (1, 2):
        scratch += [vmem((2, 2, 4, rows, 128), F32) for rows in PARTS[part]]
    scratch += [vmem((2, 2, 4, max(part[t] for part in PARTS), 128), F32) for t in range(3)]
    for part in PARTS:
        for rows in part:
            scratch += scratch_of(rows)
    outputs = pl.pallas_call(
        kernel,
        out_shape=[shape((8, 4, 8, D), F32), shape((144, 216), F32), shape((144, 72), F32)] + heaps,
        in_specs=[any_space, any_space, in_vmem, any_space, any_space],
        out_specs=[any_space, in_vmem, in_vmem] + [any_space] * 9,
        scratch_shapes=scratch,
        compiler_params=pltpu.CompilerParams(
            collective_id=0, has_side_effects=True, vmem_limit_bytes=64 * 2**20
        ),
        cost_estimate=pl.CostEstimate(flops=23 * 10**9, bytes_accessed=60 * 10**6, transcendentals=10**6),
    )(
        x_saved.reshape(8, 4, 8, D),
        grad_out.reshape(8, 4, 8, D),
        keep_mask.reshape(1, 256),
        w_qkv,
        w_out,
    )
    return (outputs[0].reshape(1, 1, 256, D), outputs[1], outputs[2])


def solution(mesh):
    return jax.shard_map(
        on_device,
        mesh=mesh,
        in_specs=(
            P("clip", "seq", None, None),
            P("clip", "seq", None, None),
            P("clip", "seq", None),
            P(),
            P(),
        ),
        out_specs=(P("clip", "seq", None, None), P("clip", "seq"), P("clip", "seq")),
        check_vma=False,
    )
```

```python
import jax
import jax.numpy as jnp
from jax import lax
from jax.experimental import pallas as pl
from jax.experimental.pallas import tpu as pltpu
from jax.sharding import PartitionSpec as P

HEADS = 16
HEAD_DIM = 72
KEEP_RATE = 0.9
D = 1152
LOCAL = 8
PART = 640
PARTS = ((24, 24, 24), (32, 40, 56), (48, 40, 72))
TOPS = (0, 72, 200)
SHARE = 360
CUTS = ((0, 64), (64, 80))
ORDERS = ((0, 1, 2), (1, 2, 0), (2, 0, 1))
MESH = pl.DeviceIdType.MESH
F32 = jnp.float32
BF16 = jnp.bfloat16

NN = (((1,), (0,)), ((), ()))
NT = (((1,), (1,)), ((), ()))


def split(value):
    high = value.astype(BF16)
    return high, (value - high.astype(F32)).astype(BF16)


def dot(left, right, dims):
    return lax.dot_general(left, right, dims, preferred_element_type=F32)


def dot3(left_high, left_low, right_high, right_low, dims):
    return (
        dot(left_high, right_high, dims)
        + dot(left_low, right_high, dims)
        + dot(left_high, right_low, dims)
    )


def iota(shape, dim):
    return lax.broadcasted_iota(jnp.int32, shape, dim)


def wait_copy(ref, sem):
    pltpu.make_async_copy(ref, ref, sem).wait()


class Share:
    def __init__(self, index, part, t, rows, here, at, gw, load, scratch, sems, last):
        self.index, self.t, self.rows = index, t, rows
        self.here, self.at = here, at
        self.gw, self.load = gw, load
        one1, two1, own1, one2, two2, own2, three = scratch
        self.ones, self.twos, self.three = (one1, one2), (two1, two2), three
        self.sources = (gw, own1, own2)
        self.send_sem, self.recv_sem, self.load_sem = sems
        top = TOPS[part] + sum(PARTS[part][:t])
        self.last = last.at[pl.ds(top, rows)]
        self.halves = (((0, 2), (2, 2)), ((0, 2), (2, 2)))

    def along(self, stage, step):
        axis = ORDERS[self.t][stage]
        place = list(self.here)
        place[axis] = (place[axis] + step + 4) % 4
        return self.at(*place)

    def spots(self, stage):
        me = self.here[ORDERS[self.t][stage]]
        return me, (me + 1) % 4, (me + 3) % 4, (me + 2) % 4

    def source(self, stage, spot, half):
        start, size = self.halves[stage][half]
        return self.sources[stage].at[spot, pl.ds(start, size)]

    def first_hop(self, stage, half):
        far = self.spots(stage)[3]
        size = self.halves[stage][half][1]
        return pltpu.make_async_remote_copy(
            src_ref=self.source(stage, far, half),
            dst_ref=self.ones[stage].at[half, pl.ds(0, size)],
            send_sem=self.send_sem.at[self.index, stage],
            recv_sem=self.recv_sem.at[self.index, 3 * stage + half],
            device_id=self.along(stage, 1 if half == 0 else -1),
            device_id_type=MESH,
        )

    def second_hop(self, stage, way, half):
        me, up, down, far = self.spots(stage)
        start, size = self.halves[stage][half]
        if half == way:
            src = self.ones[stage].at[half, pl.ds(0, size)]
        else:
            src = self.source(stage, up if way == 0 else down, half)
        return pltpu.make_async_remote_copy(
            src_ref=src,
            dst_ref=self.twos[stage].at[way, pl.ds(start, size)],
            send_sem=self.send_sem.at[self.index, stage],
            recv_sem=self.recv_sem.at[self.index, 3 * stage + 2],
            device_id=self.along(stage, 1 if way == 0 else -1),
            device_id_type=MESH,
        )

    def direct(self, way):
        step = (1, -1, 2)[way]
        return pltpu.make_async_remote_copy(
            src_ref=self.sources[2].at[(self.spots(2)[0] + step + 4) % 4],
            dst_ref=self.three.at[way],
            send_sem=self.send_sem.at[self.index, 2],
            recv_sem=self.recv_sem.at[self.index, 6],
            device_id=self.along(2, step),
            device_id_type=MESH,
        )

    def loads(self):
        me, up, down, far = self.spots(0)
        copy = pltpu.make_async_copy
        sem = self.load_sem.at[self.index]
        return (
            copy(self.source(0, up, 0), self.load.at[0], sem),
            copy(self.source(0, down, 1), self.load.at[1], sem),
            copy(self.gw.at[me], self.sources[1], sem),
        )

    def wait_loads(self):
        wait_copy(self.gw.at[pl.ds(0, 2)], self.load_sem.at[self.index])

    def middle(self, stage):
        me, up, down, far = self.spots(stage)
        for way in range(2):
            self.first_hop(stage, way).wait_recv()
            size = self.halves[stage][way][1]
            to = self.ones[stage].at[way, pl.ds(0, size)]
            if stage == 0:
                to[...] = to[...] + self.load[way]
            else:
                to[...] = to[...] + self.source(stage, up if way == 0 else down, way)[...]
            self.second_hop(stage, way, way).start()

    def close(self, stage):
        me = self.spots(stage)[0]
        if stage == 2:
            wait_copy(self.three, self.recv_sem.at[self.index, 6])
            self.last[...] = self.sources[2][me] + self.three[0] + self.three[1] + self.three[2]
            return
        two = self.twos[stage]
        wait_copy(two, self.recv_sem.at[self.index, 3 * stage + 2])
        if stage == 0:
            own = self.sources[1]
            own[...] = own[...] + two[0] + two[1]
        else:
            own = self.sources[2]
            own[...] = self.sources[1][me] + two[0] + two[1]

    def finish(self):
        wait_copy(self.gw.at[pl.ds(0, 3)], self.send_sem.at[self.index, 0])
        wait_copy(self.gw.at[0, pl.ds(0, 3)], self.send_sem.at[self.index, 1])
        wait_copy(self.gw.at[0, 0, pl.ds(0, 3)], self.send_sem.at[self.index, 2])


def open_stage(shares, stage):
    if stage == 2:
        for way in (2, 0, 1):
            for share in shares:
                share.direct(way).start()
        return
    for half in range(2):
        for share in shares:
            share.first_hop(stage, half).start()
    for way in range(2):
        for share in shares:
            share.second_hop(stage, way, 1 - way).start()


def middle(shares, stage):
    for share in shares:
        share.middle(stage)


def close(shares, stage):
    for share in shares:
        share.close(stage)


def scratch_of(rows):
    vmem = pltpu.VMEM
    return [
        vmem((2, 2, 4, rows, 128), F32),
        vmem((2, 4, 4, rows, 128), F32),
        vmem((4, 4, rows, 128), F32),
        vmem((2, 2, rows, 128), F32),
        vmem((2, 4, rows, 128), F32),
        vmem((4, rows, 128), F32),
        vmem((3, rows, 128), F32),
    ]


def stack(high, low):
    return jnp.concatenate([high, low], axis=0)


def all_nt(left, right):
    rows = left.shape[0] // 2
    columns = right.shape[0] // 2
    full = dot(left, right, NT)
    return (full[:rows, :columns] + full[:rows, columns:]) + (full[rows:, :columns] + full[rows:, columns:])


def all_nn(left, right):
    rows = left.shape[0] // 2
    full = dot(jnp.concatenate([left, left], axis=1), right, NN)
    return full[:rows] + full[rows:]


def kernel(*refs):
    x_hbm, g_hbm, mask_ref, wqkv_hbm, wout_hbm = refs[0:5]
    input_out, qkv_out, out_out = refs[5:8]
    gw = [refs[8 + 3 * part : 11 + 3 * part] for part in range(3)]
    (
        xl, gl, gsrc, sel, wph, wpl, woh, wol, xth1, xtl1, xth2, xtl2, qkv, gqkv, gm, mixed, probs, mth, mtl,
        gph, gpl, big_h, big_l, gqh, gql, outw, last, other,
        xs_sem, xr_sem, xfs_sem, xfr_sem, gs_sem, gr_sem, gfs_sem, gfr_sem, loc_sem, w_sem, gw_sem, out_sem,
        rs_send, rs_recv, ld_sem, gx_send, gx_recv, ga_send, ga_recv, fin_sem,
    ) = refs[17:65]
    rest = refs[65:]
    stage_refs = [rest[0:3], rest[3:6]]
    load_refs = rest[6:9]
    rest = rest[9:]

    clip = lax.axis_index("clip")
    seq = lax.axis_index("seq")
    chip = seq // 2
    core = seq % 2
    sibling = (clip, 2 * chip + 1 - core)
    here = (2 * (clip % 2) + chip % 2, chip // 2, clip // 2)

    def at(x, y, z):
        return (2 * z + x // 2, 4 * y + 2 * (x % 2) + core)

    shares = []
    for part in range(3):
        for t in range(3):
            index = 3 * part + t
            rows = PARTS[part][t]
            load = load_refs[t].at[:, :, :, pl.ds(0, rows)]
            shares.append(
                Share(index, part, t, rows, here, at, gw[part][t], load,
                      rest[7 * index : 7 * index + 7], (rs_send, rs_recv, ld_sem), last)
            )
    out_shares, first_shares, second_shares = shares[0:3], shares[3:6], shares[6:9]

    def peer(d):
        return (clip, 2 * ((chip + d) % 8) + core)

    def frame_from(d, c):
        return 2 * ((chip + 8 - d) % 8) + c

    barrier = pltpu.get_barrier_semaphore()
    for d in range(1, 8):
        pl.semaphore_signal(barrier, inc=1, device_id=peer(d), device_id_type=MESH)
    pl.semaphore_signal(barrier, inc=1, device_id=sibling, device_id_type=MESH)
    for t in range(3):
        for step in (1, -1, 2):
            pl.semaphore_signal(
                barrier, inc=1, device_id=out_shares[t].along(0, step), device_id_type=MESH
            )

    own_frame = 2 * chip + core
    load_x = pltpu.make_async_copy(x_hbm.at[chip], xl.at[:, own_frame], loc_sem.at[0])
    load_x.start()
    load_g = pltpu.make_async_copy(g_hbm, gsrc, loc_sem.at[1])
    load_g.start()

    def weight_copy(step):
        rows = pl.ds(pl.multiple_of((step % 9) * 128, 8), 128)
        columns = pl.ds(pl.multiple_of((step // 9) * D, 128), D)
        slot = step % 4
        to = pl.ds(pl.multiple_of(slot * 128, 8), 128)
        return pltpu.make_async_copy(wqkv_hbm.at[rows, columns], qkv.at[to, pl.ds(0, D)], w_sem.at[slot])

    for step in range(3):
        weight_copy(step).start()
    pl.semaphore_wait(barrier, 17)

    def send(src, dst, send_sems, recv_sems, d, h):
        p = (chip + d) % 8
        return pltpu.make_async_remote_copy(
            src_ref=src.at[p, pl.ds(2 * h, 2)],
            dst_ref=dst.at[pl.ds(2 * h, 2), own_frame],
            send_sem=send_sems.at[0],
            recv_sem=recv_sems.at[h, d],
            device_id=peer(d),
            device_id_type=MESH,
        )

    def same_place(view, send_sem, recv_sem, device):
        return pltpu.make_async_remote_copy(
            src_ref=view, dst_ref=view, send_sem=send_sem, recv_sem=recv_sem,
            device_id=device, device_id_type=MESH,
        )

    def arrival(dst, send_sems, recv_sems, d, h):
        view = dst.at[pl.ds(2 * h, 2), frame_from(d, core)]
        return same_place(view, send_sems.at[0], recv_sems.at[h, d], peer(d))

    def forward(dst, send_sems, recv_sems, d, h):
        view = dst.at[pl.ds(2 * h, 2), frame_from(d, core)]
        return same_place(view, send_sems.at[0], recv_sems.at[h], sibling)

    def wait_forwarded(dst, recv_sems, h):
        wait_copy(dst.at[pl.ds(2 * h, 2), pl.ds(0, 8)], recv_sems.at[h])

    for h in range(2):
        for d in range(1, 8):
            send(x_hbm, xl, xs_sem, xr_sem, d, h).start()

    load_g.wait()
    same = iota((256, 256), 0) == iota((256, 256), 1)
    keep = mask_ref[...].astype(F32)
    column = jnp.sum(jnp.where(same, keep, 0.0), axis=1, keepdims=True) / KEEP_RATE
    column = column.reshape(8, 4, 8, 1)
    for p in range(8):
        gsrc[p] = gsrc[p] * column[p]
    own_g = pltpu.make_async_copy(gsrc.at[chip], gl.at[:, own_frame], loc_sem.at[2])
    own_g.start()
    for h in range(2):
        for d in range(1, 8):
            send(gsrc, gl, gs_sem, gr_sem, d, h).start()

    bases = (0, 128, 384, 640, 640)
    for n in range(5):
        lane = iota((512, 128), 1) + 128 * n
        head = lane // HEAD_DIM
        source = lane + HEAD_DIM * (head + core) - bases[n]
        hit = (iota((512, 128), 0) == source) & (lane < LOCAL * HEAD_DIM)
        sel[n] = jnp.where(hit, 1.0, 0.0).astype(BF16)

    load_x.wait()
    for h in range(2):
        forward(xl, xfs_sem, xfr_sem, 0, h).start()

    def head_copy(a):
        return pltpu.make_async_copy(
            wout_hbm.at[pl.ds(HEAD_DIM * (2 * a + core), HEAD_DIM)],
            outw.at[a // 2, a % 2],
            w_sem.at[4],
        )

    for a in range(LOCAL):
        head_copy(a).start()

    def prepare(step, carry):
        @pl.when(step < 24)
        def _():
            weight_copy(step + 3).start()

        weight_copy(step).wait()
        rows = pl.ds(pl.multiple_of((step % 9) * 128, 16), 128)
        staged = pl.ds(pl.multiple_of((step % 4) * 128, 8), 128)
        part = step // 9
        for n in range(5):
            both = stack(*split(qkv[staged, bases[n] : bases[n] + 512]))
            both = dot(both, sel[n], NN).astype(BF16)
            to = pl.ds(pl.multiple_of(PART * part + 128 * n, 128), 128)
            wph[rows, to] = both[0:128]
            wpl[rows, to] = both[128:256]
        return carry

    lax.fori_loop(0, 27, prepare, 0)

    def pass_on(dst, sems, h):
        for d in range(1, 8):
            arrival(dst, sems[0], sems[1], d, h).wait_recv()
            forward(dst, sems[2], sems[3], d, h).start()

    x_sems = (xs_sem, xr_sem, xfs_sem, xfr_sem)
    g_sems = (gs_sem, gr_sem, gfs_sem, gfr_sem)
    pass_on(xl, x_sems, 0)

    wait_copy(outw, w_sem.at[4])
    for n in range(4):
        high, low = split(outw[n].reshape(144, D))
        woh[144 * n : 144 * n + 144, :] = high
        wol[144 * n : 144 * n + 144, :] = low
    woh[576:640, :] = jnp.zeros((64, D), BF16)
    wol[576:640, :] = jnp.zeros((64, D), BF16)
    for part in range(3):
        gqkv[:, PART * part + 512 : PART * part + 640] = jnp.zeros((128, 128), F32)
    mixed[:, 512:640] = jnp.zeros((128, 128), F32)

    own_g.wait()
    for h in range(2):
        forward(gl, gfs_sem, gfr_sem, 0, h).start()
    wait_forwarded(xl, xfr_sem, 0)

    def split_x(g, carry):
        rows = pl.ds(pl.multiple_of(g * 128, 128), 128)
        value = xl[g].reshape(128, D)
        high, low = split(value)
        big_h[rows, 0:D] = high
        big_l[rows, 0:D] = low
        high, low = split(value.T)
        for i in range(8):
            xth1[64 * i : 64 * i + 64, rows] = high[144 * i : 144 * i + 64]
            xtl1[64 * i : 64 * i + 64, rows] = low[144 * i : 144 * i + 64]
            xth2[80 * i : 80 * i + 80, rows] = high[144 * i + 64 : 144 * i + 144]
            xtl2[80 * i : 80 * i + 80, rows] = low[144 * i + 64 : 144 * i + 144]
        return carry

    def project(h, first, width):
        to = pl.ds(first, width)
        rows = pl.ds(256 * h, 256)
        qkv[rows, to] = dot3(
            big_h[rows, 0:D], big_l[rows, 0:D], wph[:, to], wpl[:, to], NN
        )

    def project_half(h):
        def project_tile(n, carry):
            project(h, pl.multiple_of(n * 256, 256), 256)
            return carry

        lax.fori_loop(0, 7, project_tile, 0)
        project(h, 1792, 128)

    lax.fori_loop(0, 2, split_x, 0)
    pass_on(xl, x_sems, 1)
    project_half(0)
    wait_forwarded(xl, xfr_sem, 1)
    lax.fori_loop(2, 4, split_x, 0)
    project_half(1)
    wait_copy(xl.at[:, pl.ds(0, 8)], xfs_sem.at[0])
    pass_on(gl, g_sems, 0)
    pass_on(gl, g_sems, 1)

    scaling = HEAD_DIM ** (-0.5)
    firsts = [min(HEAD_DIM * a // 128 * 128, 384) for a in range(LOCAL)]

    def own_lanes(a):
        lane = iota((128, 256), 1)
        low_lane = HEAD_DIM * a - firsts[a]
        return (lane >= low_lane) & (lane < low_lane + HEAD_DIM)

    def window(ref, rows, part, a):
        start = PART * part + firsts[a]
        return ref[rows, start : start + 256]

    def attend(g, carry):
        rows = pl.ds(pl.multiple_of(g * 128, 128), 128)
        same_patch = (iota((128, 128), 0) % 8) == (iota((128, 128), 1) % 8)
        for a in range(LOCAL):
            mine = own_lanes(a)
            q = stack(*split(jnp.where(mine, window(qkv, rows, 0, a), 0.0) * scaling))
            k = stack(*split(window(qkv, rows, 1, a)))
            v = stack(*split(window(qkv, rows, 2, a)))
            scores = jnp.where(same_patch, all_nt(q, k), -1e30)
            expo = jnp.exp(scores - jnp.max(scores, axis=1, keepdims=True))
            attn = expo / jnp.sum(expo, axis=1, keepdims=True)
            probs[g, a] = attn
            pltpu.store(
                mixed.at[:, firsts[a] : firsts[a] + 256], all_nn(stack(*split(attn)), v), mask=mine
            )
        high, low = split(mixed[...].T)
        mth[:, rows] = high
        mtl[:, rows] = low
        return carry

    lax.fori_loop(0, 4, attend, 0)

    for h in range(2):
        wait_forwarded(gl, gfr_sem, h)

    def regroup(g, carry):
        rows = pl.ds(pl.multiple_of(g * 128, 128), 128)
        value = gl[g].reshape(128, D)
        high, low = split(value)
        gqh[rows, 0:D] = high
        gql[rows, 0:D] = low
        lane = iota((128, 128), 1)
        rest = value[:, 128:256]
        for j in range(8):
            tile = 144 * j // 128
            offset = 144 * j % 128
            if offset:
                piece = value[:, 128 * tile : 128 * tile + 256]
                piece = pltpu.roll(piece, 256 - offset, 1)[:, 0:128]
            else:
                piece = value[:, 128 * tile : 128 * tile + 128]
            high, low = split(piece)
            gph[rows, 128 * j : 128 * j + 128] = high
            gpl[rows, 128 * j : 128 * j + 128] = low
            if j:
                rest = jnp.where(lane // 16 == j, value[:, 128 * (j + 1) : 128 * (j + 2)], rest)
        high, low = split(rest)
        gph[rows, 1024:1152] = high
        gpl[rows, 1024:1152] = low
        return carry

    lax.fori_loop(0, 4, regroup, 0)

    def out_tile(first, width):
        to = pl.ds(first, width)
        term = dot3(mth[...], mtl[...], gph[:, to], gpl[:, to], NN)
        outw[:, :, :, to] = term[0:576].reshape(4, 2, 72, width)

    def out_step(n, carry):
        out_tile(pl.multiple_of(n * 256, 256), 256)
        return carry

    lax.fori_loop(0, 4, out_step, 0)
    out_tile(1024, 128)

    def targets(part, dx, dy):
        first, second, third = gw[part]
        return (first.at[dx, dy], second.at[dy, :, dx], third.at[:, dx, dy])

    def out_copies(j):
        columns = pl.ds(pl.multiple_of(j * 128, 128), 128)
        copies = []
        for dx_high in range(2):
            for t, target in enumerate(targets(0, 2 * dx_high + j % 2, j // 2)):
                copies.append(
                    pltpu.make_async_copy(
                        outw.at[:, dx_high, pl.ds(24 * t, 24), columns], target, out_sem.at[0]
                    )
                )
        return copies

    def out_start(j, carry):
        for copy in out_copies(j):
            copy.start()
        return carry

    lax.fori_loop(0, 8, out_start, 0)

    for first, width in ((0, 256), (256, 256), (512, 128)):
        gm[:, first : first + width] = dot3(
            gqh[:, 0:D], gql[:, 0:D], woh[first : first + width, :], wol[first : first + width, :], NT
        )

    wait_copy(outw.at[:, :, :, pl.ds(0, 1024)], out_sem.at[0])
    open_stage(out_shares, 0)
    for share in out_shares:
        for copy in share.loads():
            copy.start()
    for share in out_shares:
        share.wait_loads()

    def attend_back(g, carry):
        rows = pl.ds(pl.multiple_of(g * 128, 128), 128)

        def put(part, a, value):
            start = PART * part + firsts[a]
            pltpu.store(gqkv.at[:, start : start + 256], value, mask=own_lanes(a))

        for a in range(LOCAL):
            mine = own_lanes(a)
            q = stack(*split(jnp.where(mine, window(qkv, rows, 0, a), 0.0) * scaling))
            k = stack(*split(window(qkv, rows, 1, a)))
            v = stack(*split(window(qkv, rows, 2, a)))
            m = stack(*split(jnp.where(mine, gm[rows, firsts[a] : firsts[a] + 256], 0.0)))
            attn = probs[g, a]
            grad_attn = all_nt(m, v)
            grad_scores = attn * (grad_attn - jnp.sum(grad_attn * attn, axis=1, keepdims=True))
            put(0, a, all_nn(stack(*split(grad_scores)), k) * scaling)
            put(1, a, all_nn(stack(*split(grad_scores.T)), q))
            put(2, a, all_nn(stack(*split(attn.T)), m))

        high, low = split(gqkv[...])
        gqh[rows, :] = high
        gql[rows, :] = low
        lane = iota((128, 256), 1)
        for j in range(8):
            starts = [PART * ((3 * j + k) // 8) + HEAD_DIM * ((3 * j + k) % 8) for k in range(3)]
            base = starts[0] // 128 * 128
            end = -(-(starts[2] + HEAD_DIM) // 128) * 128
            span = gqkv[:, base:end]
            value = jnp.zeros((128, 256), F32)
            done = {}
            for k in range(3):
                shift = (starts[k] - base - HEAD_DIM * k) % (end - base)
                if shift not in done:
                    moved = span if shift == 0 else pltpu.roll(span, end - base - shift, 1)
                    done[shift] = moved[:, 0:256]
                value = jnp.where((lane >= HEAD_DIM * k) & (lane < HEAD_DIM * k + HEAD_DIM), done[shift], value)
            high, low = split(value)
            big_h[rows, 256 * j : 256 * j + 256] = high
            big_l[rows, 256 * j : 256 * j + 256] = low
        return carry

    lax.fori_loop(0, 2, attend_back, 0)
    middle(out_shares, 0)
    lax.fori_loop(2, 4, attend_back, 0)
    close(out_shares, 0)

    def gw_copies(which, j, slot):
        copies = []
        for dx_high in range(2):
            for t, target in enumerate(targets(1 + which, 2 * dx_high + j % 2, j // 2)):
                copies.append(
                    pltpu.make_async_copy(
                        stage_refs[which][t].at[slot, dx_high], target, gw_sem.at[which, slot, t]
                    )
                )
        return copies

    def wait_gw(which, slot):
        for t in range(3):
            wait_copy(stage_refs[which][t].at[slot], gw_sem.at[which, slot, t])

    def gw_part(which):
        high_ref, low_ref = ((xth1, xtl1), (xth2, xtl2))[which]
        size = CUTS[which][1]

        def gw_step(j, carry):
            slot = j % 2

            @pl.when(j >= 2)
            def _():
                wait_gw(which, slot)

            to = pl.ds(pl.multiple_of(j * 256, 256), 256)
            term = dot3(high_ref[...], low_ref[...], big_h[:, to], big_l[:, to], NN)
            inside = iota((8, 128), 1)
            inside = (inside >= 88) & (inside < 104)
            for i in range(8):
                dz, dx_high = i // 2, i % 2
                if which == 1:
                    rest = pltpu.roll(outw[dz, dx_high, :, 1024:1152], (88 + 128 - 16 * j) % 128, 1)
                top = 0
                for t in range(3):
                    for r in range(0, PARTS[1 + which][t], 8):
                        row = top + r
                        if row < size:
                            value = term[size * i + row : size * i + row + 8, 0:128]
                        else:
                            row = row - size
                            value = term[size * i + row : size * i + row + 8, 128:256]
                            if which == 1 and row < HEAD_DIM:
                                value = jnp.where(inside, rest[row : row + 8], value)
                        stage_refs[which][t][slot, dx_high, dz, r : r + 8, :] = value
                    top += PARTS[1 + which][t]
            for copy in gw_copies(which, j, slot):
                copy.start()
            return carry

        lax.fori_loop(0, 8, gw_step, 0)
        for slot in range(2):
            wait_gw(which, slot)

    gw_part(0)
    open_stage(first_shares, 0)
    for share in first_shares:
        for copy in share.loads():
            copy.start()
    gw_part(1)
    for share in first_shares:
        share.wait_loads()
    middle(first_shares, 0)
    open_stage(second_shares, 0)
    for share in second_shares:
        for copy in share.loads():
            copy.start()

    def gi_cross(p):
        return pltpu.make_async_remote_copy(
            src_ref=gl.at[:, 2 * p + 1 - core],
            dst_ref=xl.at[:, 2 * p + 1 - core],
            send_sem=gx_send.at[0],
            recv_sem=gx_recv.at[0],
            device_id=sibling,
            device_id_type=MESH,
        )

    def gi_back(d):
        return pltpu.make_async_remote_copy(
            src_ref=gl.at[:, 2 * ((chip + d) % 8) + core],
            dst_ref=input_out.at[chip],
            send_sem=ga_send.at[0],
            recv_sem=ga_recv.at[0],
            device_id=peer(d),
            device_id_type=MESH,
        )

    wait_copy(x_hbm.at[pl.ds(0, 7)], xs_sem.at[0])
    wait_copy(gsrc.at[pl.ds(0, 7)], gs_sem.at[0])
    wait_copy(gl.at[:, pl.ds(0, 8)], gfs_sem.at[0])

    def input_tile(first, width):
        to = pl.ds(first, width)
        term = dot3(gqh[...], gql[...], wph[to, :], wpl[to, :], NT)
        gl[:, :, :, to] = term.reshape(4, 16, 8, width)

    def input_step(n, carry):
        input_tile(pl.multiple_of(n * 256, 256), 256)
        return carry

    lax.fori_loop(0, 4, input_step, 0)
    input_tile(1024, 128)
    for p in range(8):
        gi_cross(p).start()
    close(first_shares, 0)
    early = out_shares + first_shares
    open_stage(early, 1)
    for share in second_shares:
        share.wait_loads()
    middle(second_shares, 0)
    wait_copy(xl.at[:, pl.ds(0, 8)], gx_recv.at[0])
    for d in range(8):
        p = (chip + d) % 8
        mine = 2 * p + core
        gl[:, mine] = gl[:, mine] + xl[:, mine]
    own_input = pltpu.make_async_copy(gl.at[:, own_frame], input_out.at[chip], fin_sem.at[0])
    own_input.start()

    def return_input(*ds):
        for d in ds:
            gi_back(d).start()

    return_input(1, 2)
    middle(early, 1)
    return_input(3)
    close(second_shares, 0)
    open_stage(second_shares, 1)
    close(early, 1)
    open_stage(early, 2)
    return_input(4)
    middle(second_shares, 1)
    return_input(5, 6, 7)
    close(second_shares, 1)
    open_stage(second_shares, 2)
    close(early, 2)

    def swap(start, size, sem):
        return pltpu.make_async_remote_copy(
            src_ref=last.at[pl.ds(start, size)], dst_ref=other.at[pl.ds(start, size)],
            send_sem=fin_sem.at[sem], recv_sem=fin_sem.at[sem + 1],
            device_id=sibling, device_id_type=MESH,
        )

    swaps = (swap(0, TOPS[2], 1), swap(TOPS[2], SHARE - TOPS[2], 3))
    swaps[0].start()
    close(second_shares, 2)
    swaps[1].start()
    swaps[0].wait_recv()

    even = core == 0

    def qkv_rows(which):
        first, size = CUTS[which]
        top = TOPS[1 + which]

        def both(ref):
            return jnp.concatenate([ref[top : top + size], ref[top + size : top + 2 * size]], axis=1)

        def turn(value):
            return jnp.where(even, pltpu.roll(value, HEAD_DIM, 1), pltpu.roll(value, 256 - HEAD_DIM, 1))

        mine, yours = both(last), both(other)
        lane = iota((size, 256), 1)
        turned = turn(mine)
        left = jnp.where(even, mine, turned)
        right = jnp.where(even, turned, mine)
        whole = jnp.where(lane < HEAD_DIM, left, jnp.where(lane < 2 * HEAD_DIM, turn(yours), right))
        qkv_out[first : first + size, :] = whole[:, 0:216]

    qkv_rows(0)
    swaps[1].wait_recv()
    qkv_rows(1)

    def out_rows(ref):
        lane = iota((72, 128), 1)
        main = ref[0:72]
        rest = pltpu.roll(ref[TOPS[2] + 80 : TOPS[2] + 152], 128 - 32, 1)
        return jnp.where(even, main, jnp.where(lane < 56, pltpu.roll(main, 128 - HEAD_DIM, 1), rest))

    a = out_rows(last)
    b = out_rows(other)
    out_out[0:72, :] = jnp.where(even, a, b)[:, 0:HEAD_DIM]
    out_out[72:144, :] = jnp.where(even, b, a)[:, 0:HEAD_DIM]

    wait_copy(input_out.at[pl.ds(0, 7)], ga_recv.at[0])
    wait_copy(gl.at[:, pl.ds(0, 7)], ga_send.at[0])
    wait_copy(gl.at[:, pl.ds(0, 8)], gx_send.at[0])
    for share in shares:
        share.finish()
    for copy in swaps:
        copy.wait_send()
    own_input.wait()


def on_device(x_saved, grad_out, keep_mask, w_qkv, w_out):
    any_space = pl.BlockSpec(memory_space=pl.ANY)
    in_vmem = pl.BlockSpec(memory_space=pltpu.VMEM)
    dma = pltpu.SemaphoreType.DMA
    shape = jax.ShapeDtypeStruct
    vmem = pltpu.VMEM
    heaps = [shape((4, 4, 4, rows, 128), F32) for part in PARTS for rows in part]
    scratch = [
        vmem((4, 16, 8, D), F32),
        vmem((4, 16, 8, D), F32),
        vmem((8, 4, 8, D), F32),
        vmem((5, 512, 128), BF16),
        vmem((D, 3 * PART), BF16),
        vmem((D, 3 * PART), BF16),
        vmem((PART, D), BF16),
        vmem((PART, D), BF16),
        vmem((512, 512), BF16),
        vmem((512, 512), BF16),
        vmem((640, 512), BF16),
        vmem((640, 512), BF16),
        vmem((512, 3 * PART), F32),
        vmem((128, 3 * PART), F32),
        vmem((512, PART), F32),
        vmem((128, PART), F32),
        vmem((4, LOCAL, 128, 128), F32),
        vmem((PART, 512), BF16),
        vmem((PART, 512), BF16),
        vmem((512, D), BF16),
        vmem((512, D), BF16),
        vmem((512, 2048), BF16),
        vmem((512, 2048), BF16),
        vmem((512, 3 * PART), BF16),
        vmem((512, 3 * PART), BF16),
        vmem((4, 2, 72, D), F32),
        vmem((SHARE, 128), F32),
        vmem((SHARE, 128), F32),
        dma((1,)), dma((2, 8)), dma((1,)), dma((2,)),
        dma((1,)), dma((2, 8)), dma((1,)), dma((2,)),
        dma((3,)), dma((5,)), dma((2, 2, 3)), dma((1,)),
        dma((9, 3)), dma((9, 7)), dma((9,)),
        dma((1,)), dma((1,)), dma((1,)), dma((1,)), dma((5,)),
    ]
    for part in (1, 2):
        scratch += [vmem((2, 2, 4, rows, 128), F32) for rows in PARTS[part]]
    scratch += [vmem((2, 2, 4, max(part[t] for part in PARTS), 128), F32) for t in range(3)]
    for part in PARTS:
        for rows in part:
            scratch += scratch_of(rows)
    outputs = pl.pallas_call(
        kernel,
        out_shape=[shape((8, 4, 8, D), F32), shape((144, 216), F32), shape((144, 72), F32)] + heaps,
        in_specs=[any_space, any_space, in_vmem, any_space, any_space],
        out_specs=[any_space, in_vmem, in_vmem] + [any_space] * 9,
        scratch_shapes=scratch,
        compiler_params=pltpu.CompilerParams(
            collective_id=0, has_side_effects=True, vmem_limit_bytes=64 * 2**20
        ),
        cost_estimate=pl.CostEstimate(flops=23 * 10**9, bytes_accessed=60 * 10**6, transcendentals=10**6),
    )(
        x_saved.reshape(8, 4, 8, D),
        grad_out.reshape(8, 4, 8, D),
        keep_mask.reshape(1, 256),
        w_qkv,
        w_out,
    )
    return (outputs[0].reshape(1, 1, 256, D), outputs[1], outputs[2])


def solution(mesh):
    return jax.shard_map(
        on_device,
        mesh=mesh,
        in_specs=(
            P("clip", "seq", None, None),
            P("clip", "seq", None, None),
            P("clip", "seq", None),
            P(),
            P(),
        ),
        out_specs=(P("clip", "seq", None, None), P("clip", "seq"), P("clip", "seq")),
        check_vma=False,
    )
```

```python
import jax
import jax.numpy as jnp
from jax import lax
from jax.experimental import pallas as pl
from jax.experimental.pallas import tpu as pltpu
from jax.sharding import PartitionSpec as P

HEADS = 16
HEAD_DIM = 72
KEEP_RATE = 0.9
D = 1152
LOCAL = 8
PART = 640
PARTS = ((24, 24, 24), (32, 40, 56), (48, 40, 72))
TOPS = (0, 72, 200)
SHARE = 360
CUTS = ((0, 64), (64, 80))
ORDERS = ((0, 1, 2), (1, 2, 0), (2, 0, 1))
MESH = pl.DeviceIdType.MESH
F32 = jnp.float32
BF16 = jnp.bfloat16

NN = (((1,), (0,)), ((), ()))
NT = (((1,), (1,)), ((), ()))


def split(value):
    high = value.astype(BF16)
    return high, (value - high.astype(F32)).astype(BF16)


def dot(left, right, dims):
    return lax.dot_general(left, right, dims, preferred_element_type=F32)


def dot3(left_high, left_low, right_high, right_low, dims):
    return (
        dot(left_high, right_high, dims)
        + dot(left_low, right_high, dims)
        + dot(left_high, right_low, dims)
    )


def iota(shape, dim):
    return lax.broadcasted_iota(jnp.int32, shape, dim)


def wait_copy(ref, sem):
    pltpu.make_async_copy(ref, ref, sem).wait()


class Share:
    def __init__(self, index, part, t, rows, here, at, gw, load, scratch, sems, last):
        self.index, self.t, self.rows = index, t, rows
        self.here, self.at = here, at
        self.gw, self.load = gw, load
        one1, two1, own1, one2, two2, own2, three = scratch
        self.ones, self.twos, self.three = (one1, one2), (two1, two2), three
        self.sources = (gw, own1, own2)
        self.send_sem, self.recv_sem, self.load_sem = sems
        top = TOPS[part] + sum(PARTS[part][:t])
        self.last = last.at[pl.ds(top, rows)]
        self.halves = (((0, 2), (2, 2)), ((0, 2), (2, 2)))

    def along(self, stage, step):
        axis = ORDERS[self.t][stage]
        place = list(self.here)
        place[axis] = (place[axis] + step + 4) % 4
        return self.at(*place)

    def spots(self, stage):
        me = self.here[ORDERS[self.t][stage]]
        return me, (me + 1) % 4, (me + 3) % 4, (me + 2) % 4

    def source(self, stage, spot, half):
        start, size = self.halves[stage][half]
        return self.sources[stage].at[spot, pl.ds(start, size)]

    def first_hop(self, stage, half):
        far = self.spots(stage)[3]
        size = self.halves[stage][half][1]
        return pltpu.make_async_remote_copy(
            src_ref=self.source(stage, far, half),
            dst_ref=self.ones[stage].at[half, pl.ds(0, size)],
            send_sem=self.send_sem.at[self.index, stage],
            recv_sem=self.recv_sem.at[self.index, 3 * stage + half],
            device_id=self.along(stage, 1 if half == 0 else -1),
            device_id_type=MESH,
        )

    def second_hop(self, stage, way, half):
        me, up, down, far = self.spots(stage)
        start, size = self.halves[stage][half]
        if half == way:
            src = self.ones[stage].at[half, pl.ds(0, size)]
        else:
            src = self.source(stage, up if way == 0 else down, half)
        return pltpu.make_async_remote_copy(
            src_ref=src,
            dst_ref=self.twos[stage].at[way, pl.ds(start, size)],
            send_sem=self.send_sem.at[self.index, stage],
            recv_sem=self.recv_sem.at[self.index, 3 * stage + 2],
            device_id=self.along(stage, 1 if way == 0 else -1),
            device_id_type=MESH,
        )

    def direct(self, way):
        step = (1, -1, 2)[way]
        return pltpu.make_async_remote_copy(
            src_ref=self.sources[2].at[(self.spots(2)[0] + step + 4) % 4],
            dst_ref=self.three.at[way],
            send_sem=self.send_sem.at[self.index, 2],
            recv_sem=self.recv_sem.at[self.index, 6],
            device_id=self.along(2, step),
            device_id_type=MESH,
        )

    def loads(self):
        me, up, down, far = self.spots(0)
        copy = pltpu.make_async_copy
        sem = self.load_sem.at[self.index]
        return (
            copy(self.source(0, up, 0), self.load.at[0], sem),
            copy(self.source(0, down, 1), self.load.at[1], sem),
            copy(self.gw.at[me], self.sources[1], sem),
        )

    def wait_loads(self):
        wait_copy(self.gw.at[pl.ds(0, 2)], self.load_sem.at[self.index])

    def middle(self, stage):
        me, up, down, far = self.spots(stage)
        for way in range(2):
            self.first_hop(stage, way).wait_recv()
            size = self.halves[stage][way][1]
            to = self.ones[stage].at[way, pl.ds(0, size)]
            if stage == 0:
                to[...] = to[...] + self.load[way]
            else:
                to[...] = to[...] + self.source(stage, up if way == 0 else down, way)[...]
            self.second_hop(stage, way, way).start()

    def close(self, stage):
        me = self.spots(stage)[0]
        if stage == 2:
            wait_copy(self.three, self.recv_sem.at[self.index, 6])
            self.last[...] = self.sources[2][me] + self.three[0] + self.three[1] + self.three[2]
            return
        two = self.twos[stage]
        wait_copy(two, self.recv_sem.at[self.index, 3 * stage + 2])
        if stage == 0:
            own = self.sources[1]
            own[...] = own[...] + two[0] + two[1]
        else:
            own = self.sources[2]
            own[...] = self.sources[1][me] + two[0] + two[1]

    def finish(self):
        wait_copy(self.gw.at[pl.ds(0, 3)], self.send_sem.at[self.index, 0])
        wait_copy(self.gw.at[0, pl.ds(0, 3)], self.send_sem.at[self.index, 1])
        wait_copy(self.gw.at[0, 0, pl.ds(0, 3)], self.send_sem.at[self.index, 2])


def open_stage(shares, stage):
    if stage == 2:
        for way in (2, 0, 1):
            for share in shares:
                share.direct(way).start()
        return
    for half in range(2):
        for share in shares:
            share.first_hop(stage, half).start()
    for way in range(2):
        for share in shares:
            share.second_hop(stage, way, 1 - way).start()


def middle(shares, stage):
    for share in shares:
        share.middle(stage)


def close(shares, stage):
    for share in shares:
        share.close(stage)


def scratch_of(rows):
    vmem = pltpu.VMEM
    return [
        vmem((2, 2, 4, rows, 128), F32),
        vmem((2, 4, 4, rows, 128), F32),
        vmem((4, 4, rows, 128), F32),
        vmem((2, 2, rows, 128), F32),
        vmem((2, 4, rows, 128), F32),
        vmem((4, rows, 128), F32),
        vmem((3, rows, 128), F32),
    ]


def stack(high, low):
    return jnp.concatenate([high, low], axis=0)


def all_nt(left, right):
    rows = left.shape[0] // 2
    columns = right.shape[0] // 2
    full = dot(left, right, NT)
    return (full[:rows, :columns] + full[:rows, columns:]) + (full[rows:, :columns] + full[rows:, columns:])


def all_nn(left, right):
    rows = left.shape[0] // 2
    full = dot(jnp.concatenate([left, left], axis=1), right, NN)
    return full[:rows] + full[rows:]


def kernel(*refs):
    x_hbm, g_hbm, mask_ref, wqkv_hbm, wout_hbm = refs[0:5]
    input_out, qkv_out, out_out = refs[5:8]
    gw = [refs[8 + 3 * part : 11 + 3 * part] for part in range(3)]
    (
        xl, gl, gsrc, sel, wph, wpl, woh, wol, xth1, xtl1, xth2, xtl2, qkv, gqkv, gm, mixed, probs, mth, mtl,
        gph, gpl, big_h, big_l, gqh, gql, outw, last, other,
        xs_sem, xr_sem, xfs_sem, xfr_sem, gs_sem, gr_sem, gfs_sem, gfr_sem, loc_sem, w_sem, gw_sem, out_sem,
        rs_send, rs_recv, ld_sem, gx_send, gx_recv, ga_send, ga_recv, fin_sem,
    ) = refs[17:65]
    rest = refs[65:]
    stage_refs = [rest[0:3], rest[3:6]]
    load_refs = rest[6:9]
    rest = rest[9:]

    clip = lax.axis_index("clip")
    seq = lax.axis_index("seq")
    chip = seq // 2
    core = seq % 2
    sibling = (clip, 2 * chip + 1 - core)
    here = (2 * (clip % 2) + chip % 2, chip // 2, clip // 2)

    def at(x, y, z):
        return (2 * z + x // 2, 4 * y + 2 * (x % 2) + core)

    shares = []
    for part in range(3):
        for t in range(3):
            index = 3 * part + t
            rows = PARTS[part][t]
            load = load_refs[t].at[:, :, :, pl.ds(0, rows)]
            shares.append(
                Share(index, part, t, rows, here, at, gw[part][t], load,
                      rest[7 * index : 7 * index + 7], (rs_send, rs_recv, ld_sem), last)
            )
    out_shares, first_shares, second_shares = shares[0:3], shares[3:6], shares[6:9]

    def peer(d):
        return (clip, 2 * ((chip + d) % 8) + core)

    def frame_from(d, c):
        return 2 * ((chip + 8 - d) % 8) + c

    barrier = pltpu.get_barrier_semaphore()
    for d in range(1, 8):
        pl.semaphore_signal(barrier, inc=1, device_id=peer(d), device_id_type=MESH)
    pl.semaphore_signal(barrier, inc=1, device_id=sibling, device_id_type=MESH)
    for t in range(3):
        for step in (1, -1, 2):
            pl.semaphore_signal(
                barrier, inc=1, device_id=out_shares[t].along(0, step), device_id_type=MESH
            )

    own_frame = 2 * chip + core
    load_x = pltpu.make_async_copy(x_hbm.at[chip], xl.at[:, own_frame], loc_sem.at[0])
    load_x.start()
    load_g = pltpu.make_async_copy(g_hbm, gsrc, loc_sem.at[1])
    load_g.start()

    def weight_copy(step):
        rows = pl.ds(pl.multiple_of((step % 9) * 128, 8), 128)
        columns = pl.ds(pl.multiple_of((step // 9) * D, 128), D)
        slot = step % 4
        to = pl.ds(pl.multiple_of(slot * 128, 8), 128)
        return pltpu.make_async_copy(wqkv_hbm.at[rows, columns], qkv.at[to, pl.ds(0, D)], w_sem.at[slot])

    for step in range(3):
        weight_copy(step).start()
    pl.semaphore_wait(barrier, 17)

    def send(src, dst, send_sems, recv_sems, d, h):
        p = (chip + d) % 8
        return pltpu.make_async_remote_copy(
            src_ref=src.at[p, pl.ds(2 * h, 2)],
            dst_ref=dst.at[pl.ds(2 * h, 2), own_frame],
            send_sem=send_sems.at[0],
            recv_sem=recv_sems.at[h, d],
            device_id=peer(d),
            device_id_type=MESH,
        )

    def same_place(view, send_sem, recv_sem, device):
        return pltpu.make_async_remote_copy(
            src_ref=view, dst_ref=view, send_sem=send_sem, recv_sem=recv_sem,
            device_id=device, device_id_type=MESH,
        )

    def arrival(dst, send_sems, recv_sems, d, h):
        view = dst.at[pl.ds(2 * h, 2), frame_from(d, core)]
        return same_place(view, send_sems.at[0], recv_sems.at[h, d], peer(d))

    def forward(dst, send_sems, recv_sems, d, h):
        view = dst.at[pl.ds(2 * h, 2), frame_from(d, core)]
        return same_place(view, send_sems.at[0], recv_sems.at[h], sibling)

    def wait_forwarded(dst, recv_sems, h):
        wait_copy(dst.at[pl.ds(2 * h, 2), pl.ds(0, 8)], recv_sems.at[h])

    for h in range(2):
        for d in range(1, 8):
            send(x_hbm, xl, xs_sem, xr_sem, d, h).start()

    load_g.wait()
    same = iota((256, 256), 0) == iota((256, 256), 1)
    keep = mask_ref[...].astype(F32)
    column = jnp.sum(jnp.where(same, keep, 0.0), axis=1, keepdims=True) / KEEP_RATE
    column = column.reshape(8, 4, 8, 1)
    for p in range(8):
        gsrc[p] = gsrc[p] * column[p]
    own_g = pltpu.make_async_copy(gsrc.at[chip], gl.at[:, own_frame], loc_sem.at[2])
    own_g.start()
    for h in range(2):
        for d in range(1, 8):
            send(gsrc, gl, gs_sem, gr_sem, d, h).start()

    tiles = ((0, 256, 0, 640), (256, 256, 384, 768), (512, 128, 640, 512))
    for first, width, base, depth in tiles:
        lane = iota((depth, width), 1) + first
        source = lane + HEAD_DIM * (lane // HEAD_DIM + core) - base
        hit = (iota((depth, width), 0) == source) & (lane < LOCAL * HEAD_DIM)
        sel[0:depth, first : first + width] = jnp.where(hit, 1.0, 0.0).astype(BF16)

    load_x.wait()
    for h in range(2):
        forward(xl, xfs_sem, xfr_sem, 0, h).start()

    def head_copy(a):
        return pltpu.make_async_copy(
            wout_hbm.at[pl.ds(HEAD_DIM * (2 * a + core), HEAD_DIM)],
            outw.at[a // 2, a % 2],
            w_sem.at[4],
        )

    for a in range(LOCAL):
        head_copy(a).start()

    def prepare(step, carry):
        @pl.when(step < 24)
        def _():
            weight_copy(step + 3).start()

        weight_copy(step).wait()
        rows = pl.ds(pl.multiple_of((step % 9) * 128, 16), 128)
        staged = pl.ds(pl.multiple_of((step % 4) * 128, 8), 128)
        part = step // 9
        for first, width, base, depth in tiles:
            both = stack(*split(qkv[staged, base : base + depth]))
            both = dot(both, sel[0:depth, first : first + width], NN).astype(BF16)
            to = pl.ds(pl.multiple_of(PART * part + first, 128), width)
            wph[rows, to] = both[0:128]
            wpl[rows, to] = both[128:256]
        return carry

    lax.fori_loop(0, 27, prepare, 0)

    def pass_on(dst, sems, h):
        for d in range(1, 8):
            arrival(dst, sems[0], sems[1], d, h).wait_recv()
            forward(dst, sems[2], sems[3], d, h).start()

    x_sems = (xs_sem, xr_sem, xfs_sem, xfr_sem)
    g_sems = (gs_sem, gr_sem, gfs_sem, gfr_sem)
    pass_on(xl, x_sems, 0)

    wait_copy(outw, w_sem.at[4])
    for n in range(4):
        high, low = split(outw[n].reshape(144, D))
        woh[144 * n : 144 * n + 144, :] = high
        wol[144 * n : 144 * n + 144, :] = low
    woh[576:640, :] = jnp.zeros((64, D), BF16)
    wol[576:640, :] = jnp.zeros((64, D), BF16)
    for part in range(3):
        gqkv[:, PART * part + 512 : PART * part + 640] = jnp.zeros((128, 128), F32)
    mixed[:, 512:640] = jnp.zeros((128, 128), F32)

    own_g.wait()
    for h in range(2):
        forward(gl, gfs_sem, gfr_sem, 0, h).start()
    wait_forwarded(xl, xfr_sem, 0)

    def split_x(g, carry):
        rows = pl.ds(pl.multiple_of(g * 128, 128), 128)
        value = xl[g].reshape(128, D)
        high, low = split(value)
        big_h[rows, 0:D] = high
        big_l[rows, 0:D] = low
        high, low = split(value.T)
        for i in range(8):
            xth1[64 * i : 64 * i + 64, rows] = high[144 * i : 144 * i + 64]
            xtl1[64 * i : 64 * i + 64, rows] = low[144 * i : 144 * i + 64]
            xth2[80 * i : 80 * i + 80, rows] = high[144 * i + 64 : 144 * i + 144]
            xtl2[80 * i : 80 * i + 80, rows] = low[144 * i + 64 : 144 * i + 144]
        return carry

    def project(h, first, width):
        to = pl.ds(first, width)
        rows = pl.ds(256 * h, 256)
        qkv[rows, to] = dot3(
            big_h[rows, 0:D], big_l[rows, 0:D], wph[:, to], wpl[:, to], NN
        )

    def project_half(h):
        def project_tile(n, carry):
            project(h, pl.multiple_of(n * 256, 256), 256)
            return carry

        lax.fori_loop(0, 7, project_tile, 0)
        project(h, 1792, 128)

    lax.fori_loop(0, 2, split_x, 0)
    pass_on(xl, x_sems, 1)
    project_half(0)
    wait_forwarded(xl, xfr_sem, 1)
    lax.fori_loop(2, 4, split_x, 0)
    project_half(1)
    wait_copy(xl.at[:, pl.ds(0, 8)], xfs_sem.at[0])
    pass_on(gl, g_sems, 0)
    pass_on(gl, g_sems, 1)

    scaling = HEAD_DIM ** (-0.5)
    firsts = [min(HEAD_DIM * a // 128 * 128, 384) for a in range(LOCAL)]

    def own_lanes(a):
        lane = iota((128, 256), 1)
        low_lane = HEAD_DIM * a - firsts[a]
        return (lane >= low_lane) & (lane < low_lane + HEAD_DIM)

    def window(ref, rows, part, a):
        start = PART * part + firsts[a]
        return ref[rows, start : start + 256]

    def attend(g, carry):
        rows = pl.ds(pl.multiple_of(g * 128, 128), 128)
        same_patch = (iota((128, 128), 0) % 8) == (iota((128, 128), 1) % 8)
        for a in range(LOCAL):
            mine = own_lanes(a)
            q = stack(*split(jnp.where(mine, window(qkv, rows, 0, a), 0.0) * scaling))
            k = stack(*split(window(qkv, rows, 1, a)))
            v = stack(*split(window(qkv, rows, 2, a)))
            scores = jnp.where(same_patch, all_nt(q, k), -1e30)
            expo = jnp.exp(scores - jnp.max(scores, axis=1, keepdims=True))
            attn = expo / jnp.sum(expo, axis=1, keepdims=True)
            probs[g, a] = attn
            pltpu.store(
                mixed.at[:, firsts[a] : firsts[a] + 256], all_nn(stack(*split(attn)), v), mask=mine
            )
        high, low = split(mixed[...].T)
        mth[:, rows] = high
        mtl[:, rows] = low
        return carry

    lax.fori_loop(0, 4, attend, 0)

    for h in range(2):
        wait_forwarded(gl, gfr_sem, h)

    def regroup(g, carry):
        rows = pl.ds(pl.multiple_of(g * 128, 128), 128)
        value = gl[g].reshape(128, D)
        high, low = split(value)
        gqh[rows, 0:D] = high
        gql[rows, 0:D] = low
        lane = iota((128, 128), 1)
        rest = value[:, 128:256]
        for j in range(8):
            tile = 144 * j // 128
            offset = 144 * j % 128
            if offset:
                piece = value[:, 128 * tile : 128 * tile + 256]
                piece = pltpu.roll(piece, 256 - offset, 1)[:, 0:128]
            else:
                piece = value[:, 128 * tile : 128 * tile + 128]
            high, low = split(piece)
            gph[rows, 128 * j : 128 * j + 128] = high
            gpl[rows, 128 * j : 128 * j + 128] = low
            if j:
                rest = jnp.where(lane // 16 == j, value[:, 128 * (j + 1) : 128 * (j + 2)], rest)
        high, low = split(rest)
        gph[rows, 1024:1152] = high
        gpl[rows, 1024:1152] = low
        return carry

    lax.fori_loop(0, 4, regroup, 0)

    def out_tile(first, width):
        to = pl.ds(first, width)
        term = dot3(mth[...], mtl[...], gph[:, to], gpl[:, to], NN)
        outw[:, :, :, to] = term[0:576].reshape(4, 2, 72, width)

    def out_step(n, carry):
        out_tile(pl.multiple_of(n * 256, 256), 256)
        return carry

    lax.fori_loop(0, 4, out_step, 0)
    out_tile(1024, 128)

    def targets(part, dx, dy):
        first, second, third = gw[part]
        return (first.at[dx, dy], second.at[dy, :, dx], third.at[:, dx, dy])

    def out_copies(j):
        columns = pl.ds(pl.multiple_of(j * 128, 128), 128)
        copies = []
        for dx_high in range(2):
            for t, target in enumerate(targets(0, 2 * dx_high + j % 2, j // 2)):
                copies.append(
                    pltpu.make_async_copy(
                        outw.at[:, dx_high, pl.ds(24 * t, 24), columns], target, out_sem.at[0]
                    )
                )
        return copies

    def out_start(j, carry):
        for copy in out_copies(j):
            copy.start()
        return carry

    lax.fori_loop(0, 8, out_start, 0)

    for first, width in ((0, 256), (256, 256), (512, 128)):
        gm[:, first : first + width] = dot3(
            gqh[:, 0:D], gql[:, 0:D], woh[first : first + width, :], wol[first : first + width, :], NT
        )

    wait_copy(outw.at[:, :, :, pl.ds(0, 1024)], out_sem.at[0])
    open_stage(out_shares, 0)
    for share in out_shares:
        for copy in share.loads():
            copy.start()
    for share in out_shares:
        share.wait_loads()

    def attend_back(g, carry):
        rows = pl.ds(pl.multiple_of(g * 128, 128), 128)

        def put(part, a, value):
            start = PART * part + firsts[a]
            pltpu.store(gqkv.at[:, start : start + 256], value, mask=own_lanes(a))

        for a in range(LOCAL):
            mine = own_lanes(a)
            q = stack(*split(jnp.where(mine, window(qkv, rows, 0, a), 0.0) * scaling))
            k = stack(*split(window(qkv, rows, 1, a)))
            v = stack(*split(window(qkv, rows, 2, a)))
            m = stack(*split(jnp.where(mine, gm[rows, firsts[a] : firsts[a] + 256], 0.0)))
            attn = probs[g, a]
            grad_attn = all_nt(m, v)
            grad_scores = attn * (grad_attn - jnp.sum(grad_attn * attn, axis=1, keepdims=True))
            put(0, a, all_nn(stack(*split(grad_scores)), k) * scaling)
            put(1, a, all_nn(stack(*split(grad_scores.T)), q))
            put(2, a, all_nn(stack(*split(attn.T)), m))

        high, low = split(gqkv[...])
        gqh[rows, :] = high
        gql[rows, :] = low
        lane = iota((128, 256), 1)
        for j in range(8):
            starts = [PART * ((3 * j + k) // 8) + HEAD_DIM * ((3 * j + k) % 8) for k in range(3)]
            base = starts[0] // 128 * 128
            end = -(-(starts[2] + HEAD_DIM) // 128) * 128
            span = gqkv[:, base:end]
            value = jnp.zeros((128, 256), F32)
            done = {}
            for k in range(3):
                shift = (starts[k] - base - HEAD_DIM * k) % (end - base)
                if shift not in done:
                    moved = span if shift == 0 else pltpu.roll(span, end - base - shift, 1)
                    done[shift] = moved[:, 0:256]
                value = jnp.where((lane >= HEAD_DIM * k) & (lane < HEAD_DIM * k + HEAD_DIM), done[shift], value)
            high, low = split(value)
            big_h[rows, 256 * j : 256 * j + 256] = high
            big_l[rows, 256 * j : 256 * j + 256] = low
        return carry

    lax.fori_loop(0, 2, attend_back, 0)
    middle(out_shares, 0)
    lax.fori_loop(2, 4, attend_back, 0)
    close(out_shares, 0)

    def gw_copies(which, j, slot):
        copies = []
        for dx_high in range(2):
            for t, target in enumerate(targets(1 + which, 2 * dx_high + j % 2, j // 2)):
                copies.append(
                    pltpu.make_async_copy(
                        stage_refs[which][t].at[slot, dx_high], target, gw_sem.at[which, slot, t]
                    )
                )
        return copies

    def wait_gw(which, slot):
        for t in range(3):
            wait_copy(stage_refs[which][t].at[slot], gw_sem.at[which, slot, t])

    def gw_part(which):
        high_ref, low_ref = ((xth1, xtl1), (xth2, xtl2))[which]
        size = CUTS[which][1]

        def gw_step(j, carry):
            slot = j % 2

            @pl.when(j >= 2)
            def _():
                wait_gw(which, slot)

            to = pl.ds(pl.multiple_of(j * 256, 256), 256)
            term = dot3(high_ref[...], low_ref[...], big_h[:, to], big_l[:, to], NN)
            inside = iota((8, 128), 1)
            inside = (inside >= 88) & (inside < 104)
            for i in range(8):
                dz, dx_high = i // 2, i % 2
                if which == 1:
                    rest = pltpu.roll(outw[dz, dx_high, :, 1024:1152], (88 + 128 - 16 * j) % 128, 1)
                top = 0
                for t in range(3):
                    for r in range(0, PARTS[1 + which][t], 8):
                        row = top + r
                        if row < size:
                            value = term[size * i + row : size * i + row + 8, 0:128]
                        else:
                            row = row - size
                            value = term[size * i + row : size * i + row + 8, 128:256]
                            if which == 1 and row < HEAD_DIM:
                                value = jnp.where(inside, rest[row : row + 8], value)
                        stage_refs[which][t][slot, dx_high, dz, r : r + 8, :] = value
                    top += PARTS[1 + which][t]
            for copy in gw_copies(which, j, slot):
                copy.start()
            return carry

        lax.fori_loop(0, 8, gw_step, 0)
        for slot in range(2):
            wait_gw(which, slot)

    gw_part(0)
    open_stage(first_shares, 0)
    for share in first_shares:
        for copy in share.loads():
            copy.start()
    gw_part(1)
    for share in first_shares:
        share.wait_loads()
    middle(first_shares, 0)
    open_stage(second_shares, 0)
    for share in second_shares:
        for copy in share.loads():
            copy.start()

    def gi_cross(p):
        return pltpu.make_async_remote_copy(
            src_ref=gl.at[:, 2 * p + 1 - core],
            dst_ref=xl.at[:, 2 * p + 1 - core],
            send_sem=gx_send.at[0],
            recv_sem=gx_recv.at[0],
            device_id=sibling,
            device_id_type=MESH,
        )

    def gi_back(d):
        return pltpu.make_async_remote_copy(
            src_ref=gl.at[:, 2 * ((chip + d) % 8) + core],
            dst_ref=input_out.at[chip],
            send_sem=ga_send.at[0],
            recv_sem=ga_recv.at[0],
            device_id=peer(d),
            device_id_type=MESH,
        )

    wait_copy(x_hbm.at[pl.ds(0, 7)], xs_sem.at[0])
    wait_copy(gsrc.at[pl.ds(0, 7)], gs_sem.at[0])
    wait_copy(gl.at[:, pl.ds(0, 8)], gfs_sem.at[0])

    def input_tile(first, width):
        to = pl.ds(first, width)
        term = dot3(gqh[...], gql[...], wph[to, :], wpl[to, :], NT)
        gl[:, :, :, to] = term.reshape(4, 16, 8, width)

    def input_step(n, carry):
        input_tile(pl.multiple_of(n * 256, 256), 256)
        return carry

    lax.fori_loop(0, 4, input_step, 0)
    input_tile(1024, 128)
    for p in range(8):
        gi_cross(p).start()
    close(first_shares, 0)
    early = out_shares + first_shares
    open_stage(early, 1)
    for share in second_shares:
        share.wait_loads()
    middle(second_shares, 0)
    wait_copy(xl.at[:, pl.ds(0, 8)], gx_recv.at[0])
    for d in range(8):
        p = (chip + d) % 8
        mine = 2 * p + core
        gl[:, mine] = gl[:, mine] + xl[:, mine]
    own_input = pltpu.make_async_copy(gl.at[:, own_frame], input_out.at[chip], fin_sem.at[0])
    own_input.start()

    def return_input(*ds):
        for d in ds:
            gi_back(d).start()

    return_input(1, 2)
    middle(early, 1)
    return_input(3)
    close(second_shares, 0)
    open_stage(second_shares, 1)
    close(early, 1)
    open_stage(early, 2)
    return_input(4)
    middle(second_shares, 1)
    return_input(5, 6, 7)
    close(second_shares, 1)
    open_stage(second_shares, 2)
    close(early, 2)

    def swap(start, size, sem):
        return pltpu.make_async_remote_copy(
            src_ref=last.at[pl.ds(start, size)], dst_ref=other.at[pl.ds(start, size)],
            send_sem=fin_sem.at[sem], recv_sem=fin_sem.at[sem + 1],
            device_id=sibling, device_id_type=MESH,
        )

    swaps = (swap(0, TOPS[2], 1), swap(TOPS[2], SHARE - TOPS[2], 3))
    swaps[0].start()
    close(second_shares, 2)
    swaps[1].start()
    swaps[0].wait_recv()

    even = core == 0

    def qkv_rows(which):
        first, size = CUTS[which]
        top = TOPS[1 + which]

        def both(ref):
            return jnp.concatenate([ref[top : top + size], ref[top + size : top + 2 * size]], axis=1)

        def turn(value):
            return jnp.where(even, pltpu.roll(value, HEAD_DIM, 1), pltpu.roll(value, 256 - HEAD_DIM, 1))

        mine, yours = both(last), both(other)
        lane = iota((size, 256), 1)
        turned = turn(mine)
        left = jnp.where(even, mine, turned)
        right = jnp.where(even, turned, mine)
        whole = jnp.where(lane < HEAD_DIM, left, jnp.where(lane < 2 * HEAD_DIM, turn(yours), right))
        qkv_out[first : first + size, :] = whole[:, 0:216]

    qkv_rows(0)
    swaps[1].wait_recv()
    qkv_rows(1)

    def out_rows(ref):
        lane = iota((72, 128), 1)
        main = ref[0:72]
        rest = pltpu.roll(ref[TOPS[2] + 80 : TOPS[2] + 152], 128 - 32, 1)
        return jnp.where(even, main, jnp.where(lane < 56, pltpu.roll(main, 128 - HEAD_DIM, 1), rest))

    a = out_rows(last)
    b = out_rows(other)
    out_out[0:72, :] = jnp.where(even, a, b)[:, 0:HEAD_DIM]
    out_out[72:144, :] = jnp.where(even, b, a)[:, 0:HEAD_DIM]

    wait_copy(input_out.at[pl.ds(0, 7)], ga_recv.at[0])
    wait_copy(gl.at[:, pl.ds(0, 7)], ga_send.at[0])
    wait_copy(gl.at[:, pl.ds(0, 8)], gx_send.at[0])
    for share in shares:
        share.finish()
    for copy in swaps:
        copy.wait_send()
    own_input.wait()


def on_device(x_saved, grad_out, keep_mask, w_qkv, w_out):
    any_space = pl.BlockSpec(memory_space=pl.ANY)
    in_vmem = pl.BlockSpec(memory_space=pltpu.VMEM)
    dma = pltpu.SemaphoreType.DMA
    shape = jax.ShapeDtypeStruct
    vmem = pltpu.VMEM
    heaps = [shape((4, 4, 4, rows, 128), F32) for part in PARTS for rows in part]
    scratch = [
        vmem((4, 16, 8, D), F32),
        vmem((4, 16, 8, D), F32),
        vmem((8, 4, 8, D), F32),
        vmem((768, PART), BF16),
        vmem((D, 3 * PART), BF16),
        vmem((D, 3 * PART), BF16),
        vmem((PART, D), BF16),
        vmem((PART, D), BF16),
        vmem((512, 512), BF16),
        vmem((512, 512), BF16),
        vmem((640, 512), BF16),
        vmem((640, 512), BF16),
        vmem((512, 3 * PART), F32),
        vmem((128, 3 * PART), F32),
        vmem((512, PART), F32),
        vmem((128, PART), F32),
        vmem((4, LOCAL, 128, 128), F32),
        vmem((PART, 512), BF16),
        vmem((PART, 512), BF16),
        vmem((512, D), BF16),
        vmem((512, D), BF16),
        vmem((512, 2048), BF16),
        vmem((512, 2048), BF16),
        vmem((512, 3 * PART), BF16),
        vmem((512, 3 * PART), BF16),
        vmem((4, 2, 72, D), F32),
        vmem((SHARE, 128), F32),
        vmem((SHARE, 128), F32),
        dma((1,)), dma((2, 8)), dma((1,)), dma((2,)),
        dma((1,)), dma((2, 8)), dma((1,)), dma((2,)),
        dma((3,)), dma((5,)), dma((2, 2, 3)), dma((1,)),
        dma((9, 3)), dma((9, 7)), dma((9,)),
        dma((1,)), dma((1,)), dma((1,)), dma((1,)), dma((5,)),
    ]
    for part in (1, 2):
        scratch += [vmem((2, 2, 4, rows, 128), F32) for rows in PARTS[part]]
    scratch += [vmem((2, 2, 4, max(part[t] for part in PARTS), 128), F32) for t in range(3)]
    for part in PARTS:
        for rows in part:
            scratch += scratch_of(rows)
    outputs = pl.pallas_call(
        kernel,
        out_shape=[shape((8, 4, 8, D), F32), shape((144, 216), F32), shape((144, 72), F32)] + heaps,
        in_specs=[any_space, any_space, in_vmem, any_space, any_space],
        out_specs=[any_space, in_vmem, in_vmem] + [any_space] * 9,
        scratch_shapes=scratch,
        compiler_params=pltpu.CompilerParams(
            collective_id=0, has_side_effects=True, vmem_limit_bytes=64 * 2**20
        ),
        cost_estimate=pl.CostEstimate(flops=23 * 10**9, bytes_accessed=60 * 10**6, transcendentals=10**6),
    )(
        x_saved.reshape(8, 4, 8, D),
        grad_out.reshape(8, 4, 8, D),
        keep_mask.reshape(1, 256),
        w_qkv,
        w_out,
    )
    return (outputs[0].reshape(1, 1, 256, D), outputs[1], outputs[2])


def solution(mesh):
    return jax.shard_map(
        on_device,
        mesh=mesh,
        in_specs=(
            P("clip", "seq", None, None),
            P("clip", "seq", None, None),
            P("clip", "seq", None),
            P(),
            P(),
        ),
        out_specs=(P("clip", "seq", None, None), P("clip", "seq"), P("clip", "seq")),
        check_vma=False,
    )
```
